32 devices in a mesh: req: 8 (over y, x, core), tp: 4 (over z).
Axes of the slice: x: 2, y: 2, z: 4, core: 2. Of those that a mesh axis runs over, the one named last changes fastest.
Arguments:
- queries: bfloat16 [1024, 8192], P('req', 'tp'), may hold values from -80 to 80
- incoming_key_value: bfloat16 [2, 1024, 1024], P(None, 'req', 'tp'), may hold values from -4 to 4
- key_value_pages: bfloat16 [4096, 32, 2, 1024], P('req', None, None, 'tp'), may hold values from -4 to 4
- page_request_home: int32 [4096], P('req'), may hold values from 0 to 4095, as said below
- lengths: int32 [256], P('req'), may hold values from 1 to 512, 65536 in all
- request_adapter_index: int32 [256], P('req'), may hold values from 0 to 15
- adapter_storage_slot: int32 [16], replicated, may hold values from 0 to 15, each once
- adapter_down_factor: bfloat16 [16, 8192, 64], P('req', 'tp'), may hold values from -0.25 to 0.25
- adapter_up_factor: bfloat16 [16, 64, 8192], P('req'), may hold values from -0.75 to 0.75
- output_projection_weight: bfloat16 [8192, 8192], P('tp', 'req'), may hold values from -0.75 to 0.75
Outputs:
- attn_out: bfloat16 [1024, 8192], P('tp', 'req')
The draws below stay inside these ranges and needn't reach their ends.
Inputs may be any that keep to these rules, and one draw needn't show every extreme that they name: `page_request_home`: each value once. Pages p with p // 512 = a hold pages of requests i with i // 32 = b, b != a, for at most 2 pages p for every pair a, b; in every draw some a holds exactly 2 pages of every b != a.
All inputs are finite; a program needn't handle non-finite values. No bound on the sum of `lengths` on one device may be relied on, other than what follows from the above.
Results may differ from the reference program's by a relative error of at most 0.0058.
Values may be sent and summed in bfloat16 or wider, within the bound.
No kernel may reach another device: no remote copies, remote signals or barrier semaphores. Data moves between devices by JAX's collectives and lax.ppermute only.
A program may use at most 128 MiB of HBM per device.

```python
import math
import jax
import jax.numpy as jnp
import numpy as np
from jax import lax

MODEL_WIDTH = 8192
QUERY_HEADS = 64
KEY_VALUE_HEADS = 8
HEAD_WIDTH = 128
ADAPTER_RANK = 64
R_DEV = 32
STEP_COUNT = 4
PAGE_LENGTH = 32
MAXP = 16
CAP = 2
REQUEST_TOTAL = 256
TOKEN_TOTAL = 1024
ADAPTER_TOTAL = 16
PAGE_TOTAL = 4096
N_REQ = 8


def home_table(key):
    per_dev = R_DEV * MAXP
    band_slots = CAP * (N_REQ - 1)
    key_masks = jax.random.fold_in(key, 11)
    key_coins = jax.random.fold_in(key, 12)
    key_center = jax.random.fold_in(key, 13)
    key_shuffle = jax.random.fold_in(key, 14)
    xor_masks = jax.random.permutation(key_masks, N_REQ - 1).astype(jnp.int32) + 1
    slot_ids = jnp.arange(per_dev, dtype=jnp.int32)
    mask_of = jnp.where(slot_ids < band_slots, xor_masks[jnp.minimum(slot_ids // CAP, N_REQ - 2)], 0)
    device_ids = jnp.arange(N_REQ, dtype=jnp.int32)[:, None]
    partner = jnp.bitwise_xor(device_ids, mask_of[None, :])
    pair_low = jnp.minimum(device_ids, partner)
    coin_flips = jax.random.randint(key_coins, (N_REQ, per_dev), 0, 2)
    paired = jnp.take_along_axis(coin_flips, pair_low, axis=0)
    center = jax.random.randint(key_center, (), 0, N_REQ)
    forced = (device_ids == center) | (partner == center)
    swapped = ((paired == 1) | forced) & (mask_of[None, :] > 0)
    owner_dev = jnp.where(swapped, partner, device_ids)
    home_ids = owner_dev * per_dev + slot_ids[None, :]
    shuffle = jax.vmap(lambda subkey: jax.random.permutation(subkey, per_dev))(jax.random.split(key_shuffle, N_REQ))
    home_ids = jnp.take_along_axis(home_ids, shuffle.astype(jnp.int32), axis=1)
    return home_ids.reshape(N_REQ * per_dev).astype(jnp.int32)


def draw_page_request_home(key, part):
    return home_table(key)


def draw_key_value_pages(key, part):
    complete_shape = (PAGE_TOTAL, PAGE_LENGTH, 2, KEY_VALUE_HEADS * HEAD_WIDTH)
    values_base = jnp.clip(jax.random.normal(jax.random.fold_in(key, 21), complete_shape, jnp.float32), -4.0, 4.0)
    return values_base.astype(jnp.bfloat16)


def draw_queries(key, part):
    complete_shape = (TOKEN_TOTAL, QUERY_HEADS * HEAD_WIDTH)
    values_base = jnp.clip(jax.random.normal(jax.random.fold_in(key, 31), complete_shape, jnp.float32), -4.0, 4.0)
    return values_base.astype(jnp.bfloat16)


def touch_ends(entries, rng, low, largest):
    dims = entries.shape
    place = [jax.random.randint(jax.random.fold_in(rng, axis), (), 0, dims[axis]) for axis in range(len(dims))]
    entries = entries.at[tuple(place)].set(low)
    longest = dims.index(max(dims))
    place[longest] = (place[longest] + 1) % dims[longest]
    return entries.at[tuple(place)].set(largest)


def levels(rng, extent, cuts, smallest, high):
    gain = 1.0
    for dim, blocks in cuts:
        heights = jax.random.uniform(jax.random.fold_in(jax.random.fold_in(rng, 6), dim), (blocks,), jnp.float32, smallest / len(cuts), high / len(cuts))
        gain = gain * jnp.repeat(jnp.exp(heights), extent[dim] // blocks).reshape((-1,) + (1,) * (len(extent) - 1 - dim))
    return gain


def rank_bounds(number_of, skew):
    loads = [(1 << 20) // math.isqrt(grade ** skew) + 1 for grade in range(1, number_of + 1)]
    deviation = 1 + sum(loads) // (1 << 30)
    return np.cumsum(np.array([max(1, weight // deviation) for weight in loads]))


def skewed_ids(rng, dims, number_of, lean):
    listing = rank_bounds(number_of, lean)
    ticket = jax.random.randint(jax.random.fold_in(rng, 1), dims, 0, int(listing[number_of - 1]))
    standing = jnp.searchsorted(jnp.asarray(listing, jnp.int32), ticket, side="right")
    return jax.random.permutation(jax.random.fold_in(rng, 2), number_of)[standing].astype(jnp.int32)


def split_up(amount, total, reach, slope):
    loads = [(1 << 20) // math.isqrt(rank ** slope) + 1 for rank in range(2, amount + 1)]
    surplus, given = total - reach - (amount - 1), [1] * (amount - 1)
    while surplus > 0:
        free = [i for i in range(amount - 1) if given[i] < reach]
        pool, left = sum([loads[i] for i in free]), surplus
        for i in free:
            extra = min(reach - given[i], max(1, left * loads[i] // pool), surplus)
            given[i] = given[i] + extra
            surplus = surplus - extra
    return np.array([reach] + given)


def uneven(stream_key, amount, total, most, slope):
    if amount == 2:
        one = jax.random.randint(stream_key, (), max(1, total - most), min(most, total - 1) + 1)
        return jnp.stack([one, total - one])
    sizes = jnp.asarray(split_up(amount, total, most, slope), jnp.int32)
    twos = (amount - 1) // 2
    donor, sink = sizes[1:1 + 2 * twos:2], sizes[2:2 + 2 * twos:2]
    margin = jnp.minimum(donor - 1, most - sink)
    passed = jax.random.randint(jax.random.fold_in(stream_key, 1), (twos,), 0, 1 << 20) % (margin + 1)
    sizes = sizes.at[1:1 + 2 * twos:2].set(donor - passed).at[2:2 + 2 * twos:2].set(sink + passed)
    return sizes[jax.random.permutation(jax.random.fold_in(stream_key, 2), amount)]


def normal_values(rng, shape, scale, bound, shards=(), kind=jnp.bfloat16):
    drawn = scale * jax.random.normal(rng, shape, jnp.float32)
    if shards:
        drawn = drawn * levels(rng, shape, shards, -0.22, 0.18)
    return jnp.clip(drawn, -bound, bound).astype(kind)


def setup_inputs(seed: int = 0) -> dict:
    splits = jax.random.split(jax.random.key(seed), 11)
    queries = draw_queries(jax.random.fold_in(splits[10], 71), 0)
    incoming_key_value = normal_values(splits[1], (2, TOKEN_TOTAL, KEY_VALUE_HEADS * HEAD_WIDTH), 1.0, 4.0, ((1, 8), (2, 4)))
    key_value_pages = draw_key_value_pages(jax.random.fold_in(splits[10], 71), 0)
    page_request_home = draw_page_request_home(jax.random.fold_in(splits[10], 71), 0)
    lengths = uneven(splits[4], REQUEST_TOTAL, REQUEST_TOTAL * MAXP * PAGE_LENGTH // 2, MAXP * PAGE_LENGTH, 2).astype(jnp.int32)
    request_adapter_index = touch_ends(skewed_ids(splits[5], (REQUEST_TOTAL,), ADAPTER_TOTAL, 2), jax.random.fold_in(splits[5], 3), 0, ADAPTER_TOTAL - 1).astype(jnp.int32)
    adapter_storage_slot = jax.random.permutation(splits[6], ADAPTER_TOTAL).astype(jnp.int32)
    adapter_down_factor = normal_values(splits[7], (ADAPTER_TOTAL, QUERY_HEADS * HEAD_WIDTH, ADAPTER_RANK), (4.0 / (QUERY_HEADS * HEAD_WIDTH) ** 0.5), 0.25, ((0, 8), (1, 4)))
    adapter_up_factor = normal_values(splits[8], (ADAPTER_TOTAL, ADAPTER_RANK, MODEL_WIDTH), ADAPTER_RANK ** -0.5, 0.75, ((0, 8),))
    output_projection_weight = normal_values(splits[9], (QUERY_HEADS * HEAD_WIDTH, MODEL_WIDTH), (12.0 / (QUERY_HEADS * HEAD_WIDTH) ** 0.5), 0.75, ((0, 4), (1, 8)))
    return dict(queries=queries, incoming_key_value=incoming_key_value, key_value_pages=key_value_pages, page_request_home=page_request_home, lengths=lengths, request_adapter_index=request_adapter_index, adapter_storage_slot=adapter_storage_slot, adapter_down_factor=adapter_down_factor, adapter_up_factor=adapter_up_factor, output_projection_weight=output_projection_weight)


def reference(queries, incoming_key_value, key_value_pages, page_request_home, lengths, request_adapter_index, adapter_storage_slot, adapter_down_factor, adapter_up_factor, output_projection_weight):
    query_group_count = QUERY_HEADS // KEY_VALUE_HEADS
    cache_extent = MAXP * PAGE_LENGTH
    score_scale = 1.0 / math.sqrt(HEAD_WIDTH)
    inverse = jnp.zeros((PAGE_TOTAL,), jnp.int32).at[page_request_home].set(jnp.arange(PAGE_TOTAL, dtype=jnp.int32))
    req_slot = adapter_storage_slot[request_adapter_index]
    position = jnp.arange(cache_extent + STEP_COUNT, dtype=jnp.int32)
    step_index = jnp.arange(STEP_COUNT, dtype=jnp.int32)

    def single_request(request_number):
        page_locations = lax.dynamic_slice_in_dim(inverse, request_number * MAXP, MAXP)
        stored_entries = key_value_pages[page_locations].reshape(cache_extent, 2, KEY_VALUE_HEADS, HEAD_WIDTH)
        fresh_key_value = lax.dynamic_slice_in_dim(incoming_key_value, request_number * STEP_COUNT, STEP_COUNT, 1).reshape(2, STEP_COUNT, KEY_VALUE_HEADS, HEAD_WIDTH)
        fresh_key_value = jnp.transpose(fresh_key_value, (1, 0, 2, 3))
        all_keys = jnp.concatenate([stored_entries, fresh_key_value], axis=0).astype(jnp.float32)
        query_vectors = lax.dynamic_slice_in_dim(queries, request_number * STEP_COUNT, STEP_COUNT, 0)
        query_vectors = query_vectors.reshape(STEP_COUNT, KEY_VALUE_HEADS, query_group_count, HEAD_WIDTH).astype(jnp.float32)
        scores = jnp.einsum('sgqd,lgd->gqsl', query_vectors, all_keys[:, 0]) * score_scale
        usable = jnp.where(position[None, :] < cache_extent, position[None, :] < lengths[request_number], position[None, :] - cache_extent <= step_index[:, None])
        scores = jnp.where(usable[None, None], scores, -jnp.inf)
        row_top = lax.optimization_barrier(jnp.max(scores, axis=-1, keepdims=True))
        weights = jnp.exp(scores - row_top)
        probs = (weights / lax.optimization_barrier(jnp.sum(weights, axis=-1, keepdims=True))).astype(jnp.bfloat16)
        attention_mixed_output = jnp.einsum('gqsl,lgd->sgqd', probs.astype(jnp.float32), all_keys[:, 1])
        attention_mixed_output = attention_mixed_output.astype(jnp.bfloat16).reshape(STEP_COUNT, QUERY_HEADS * HEAD_WIDTH)
        slot_number = req_slot[request_number]
        reduced_features = jnp.dot(attention_mixed_output, adapter_down_factor[slot_number], preferred_element_type=jnp.float32).astype(jnp.bfloat16)
        adapter_correction = jnp.dot(reduced_features, adapter_up_factor[slot_number], preferred_element_type=jnp.float32)
        return (attention_mixed_output, adapter_correction)
    attention_all_rows, adapter_total_terms = lax.map(single_request, jnp.arange(REQUEST_TOTAL, dtype=jnp.int32))
    attention_all_rows = attention_all_rows.reshape(TOKEN_TOTAL, QUERY_HEADS * HEAD_WIDTH)
    plain_output_rows = jnp.dot(attention_all_rows, output_projection_weight, preferred_element_type=jnp.float32)
    return (plain_output_rows + adapter_total_terms.reshape(TOKEN_TOTAL, MODEL_WIDTH)).astype(jnp.bfloat16)
```

```python
import functools
import math

import jax
import jax.numpy as jnp
from jax import lax
from jax.experimental import pallas as pl
from jax.experimental.pallas import tpu as pltpu
from jax.sharding import PartitionSpec as P

QUERY_HEADS = 64
KEY_VALUE_HEADS = 8
GROUP = QUERY_HEADS // KEY_VALUE_HEADS
HEAD_WIDTH = 128
STEP_COUNT = 4
PAGE_LENGTH = 32
MAXP = 16
CAP = 2
BLOCK = CAP * PAGE_LENGTH + 1
LABEL_LANE = 64
DIGIT = 16
CHUNK_PAGES = 4
CHUNKS = MAXP // CHUNK_PAGES
PAGE_ROWS = PAGE_LENGTH * 2
CHUNK_ROWS = CHUNK_PAGES * PAGE_ROWS
NEW_ROWS = STEP_COUNT * 2
NEW_GROUP = 128 // NEW_ROWS
UNROLL = 2
SLOTS = 3
VMEM_LIMIT = 56 * 1024 * 1024

HBM = pl.BlockSpec(memory_space=pltpu.HBM)
VMEM = pl.BlockSpec(memory_space=pltpu.VMEM)
SMEM = pl.BlockSpec(memory_space=pltpu.SMEM)


def params():
    return pltpu.CompilerParams(vmem_limit_bytes=VMEM_LIMIT)


def dot(a, b, contract=((1,), (0,))):
    return lax.dot_general(a, b, (contract, ((), ())), preferred_element_type=jnp.float32)


def pack_kernel(req_count, per_dev, me_ref, home_ref, ids_ref, pages, outbox, info_v, info_s, ids_v, rows_v, sem, sems):
    me = me_ref[0]
    page = lax.broadcasted_iota(jnp.int32, (req_count, per_dev), 1)
    want = lax.broadcasted_iota(jnp.int32, (req_count, per_dev), 0)
    slots = jnp.broadcast_to(home_ref[...], (req_count, per_dev)) - want * per_dev
    hit = (slots >= 0) & (slots < per_dev) & (want != me)
    lane = lax.broadcasted_iota(jnp.int32, (req_count, 128), 1)
    info = jnp.full((req_count, 128), -1, jnp.int32)
    for k in range(CAP):
        first = jnp.min(jnp.where(hit, page, per_dev), axis=1, keepdims=True)
        here = hit & (page == first)
        slot = jnp.max(jnp.where(here, slots, -1), axis=1, keepdims=True)
        info = jnp.where(lane == k, first, info)
        info = jnp.where(lane == CAP + k, slot, info)
        hit = hit & (page != first)
    info_v[...] = info
    fetch = pltpu.make_async_copy(info_v, info_s, sem)
    fetch.start()
    ids_v[...] = jnp.zeros_like(ids_v)
    ids_v[:, 0:ids_ref.shape[1]] = ids_ref[...].astype(jnp.float32)
    ids = jnp.broadcast_to(ids_v[...], (2, 128))
    fetch.wait()

    def copy(d, k):
        return pltpu.make_async_copy(
            pages.at[info_s[d, k]],
            outbox.at[d, pl.ds(k * PAGE_LENGTH, PAGE_LENGTH)],
            sems.at[d, k],
        )

    for d in range(req_count):
        for k in range(CAP):

            @pl.when(info_s[d, k] < per_dev)
            def _():
                copy(d, k).start()

    at = lax.broadcasted_iota(jnp.int32, (2, 128), 1)
    row = lax.broadcasted_iota(jnp.int32, (2, 128), 0)
    for d in range(req_count):
        value = jnp.where(row == 0, ids, 0.0)
        for k in range(CAP):
            slot = info_s[d, CAP + k]
            high = ((slot + DIGIT) >> 4) - 1
            low = slot - high * DIGIT
            digit = jnp.where(row == 0, high, low).astype(jnp.float32)
            value = jnp.where(at == LABEL_LANE + k, digit, value)
        rows_v[d, 0, :, :] = jnp.zeros(rows_v.shape[2:], jnp.bfloat16)
        rows_v[d, 0, :, 0:128] = value.astype(jnp.bfloat16)
    rows = pltpu.make_async_copy(rows_v, outbox.at[:, pl.ds(BLOCK - 1, 1)], sem)
    rows.start()
    rows.wait()
    for d in range(req_count):
        for k in range(CAP):

            @pl.when(info_s[d, k] < per_dev)
            def _():
                copy(d, k).wait()


def pack(me, page_request_home, ids, key_value_pages, req_count):
    per_dev = key_value_pages.shape[0]
    columns = key_value_pages.shape[-1]
    return pl.pallas_call(
        functools.partial(pack_kernel, req_count, per_dev),
        out_shape=jax.ShapeDtypeStruct((req_count, BLOCK, 2, columns), jnp.bfloat16),
        in_specs=[SMEM, VMEM, VMEM, HBM],
        out_specs=HBM,
        scratch_shapes=[
            pltpu.VMEM((req_count, 128), jnp.int32),
            pltpu.SMEM((req_count, 128), jnp.int32),
            pltpu.VMEM((1, 128), jnp.float32),
            pltpu.VMEM((req_count, 1, 2, columns), jnp.bfloat16),
            pltpu.SemaphoreType.DMA,
            pltpu.SemaphoreType.DMA((req_count, CAP)),
        ],
        compiler_params=params(),
        name="pack_outbox",
    )(me, page_request_home.reshape(1, per_dev), ids.reshape(1, -1), key_value_pages)


def table_kernel(per_dev, requests, me_ref, home_ref, lengths_ref, table_ref, order_ref, chunks_ref):
    base = me_ref[0] * per_dev

    @pl.loop(0, per_dev)
    def _(s):
        table_ref[s] = 0

    @pl.loop(0, per_dev)
    def _(p):
        slot = home_ref[p] - base

        @pl.when((slot >= 0) & (slot < per_dev))
        def _():
            table_ref[slot] = p

    placed = jnp.int32(0)
    for c in range(CHUNKS, 0, -1):

        def step(r, placed):
            need = lax.shift_right_logical(lengths_ref[r] + (CHUNK_ROWS // 2 - 1), 7)
            mine = need == c

            @pl.when(mine)
            def _():
                order_ref[placed] = r
                chunks_ref[placed] = need

            return placed + jnp.where(mine, 1, 0)

        placed = lax.fori_loop(0, requests, step, placed)


def build_table(me, page_request_home, lengths):
    per_dev = page_request_home.shape[0]
    requests = lengths.shape[0]
    return pl.pallas_call(
        functools.partial(table_kernel, per_dev, requests),
        out_shape=(
            jax.ShapeDtypeStruct((per_dev,), jnp.int32),
            jax.ShapeDtypeStruct((requests,), jnp.int32),
            jax.ShapeDtypeStruct((requests,), jnp.int32),
        ),
        in_specs=[SMEM, SMEM, SMEM],
        out_specs=(SMEM, SMEM, SMEM),
        compiler_params=params(),
        name="page_table",
    )(me, page_request_home, lengths)


def attend_kernel(
    req_count,
    per_dev,
    requests,
    order_ref,
    chunks_ref,
    lengths_ref,
    table_in,
    q_ref,
    new_ref,
    pages,
    inbox,
    out_ref,
    table,
    labels_v,
    labels_w,
    labels_s,
    buf,
    acc,
    sem,
    sems,
):
    columns = pages.shape[-1]
    heads_kv = columns // HEAD_WIDTH
    half = STEP_COUNT * GROUP
    rows = heads_kv * half
    heads = heads_kv * GROUP
    scale = 1.0 / math.sqrt(HEAD_WIDTH)
    page_rows = pages.reshape(per_dev, PAGE_ROWS, columns)
    inbox_rows = inbox.reshape(req_count, BLOCK * 2, columns)

    first = pltpu.make_async_copy(inbox.at[:, pl.ds(BLOCK - 1, 1)], labels_v, sem)
    first.start()
    first.wait()
    tab = pltpu.make_async_copy(table_in, table, sem)
    tab.start()
    tab.wait()
    row = lax.broadcasted_iota(jnp.int32, (2, 128), 0)
    weight = jnp.where(row == 0, float(DIGIT), 1.0)
    for d in range(req_count):
        digits = labels_v[d, 0, :, 0:128].astype(jnp.float32) * weight
        labels_w[d : d + 1, :] = jnp.sum(digits, axis=0, keepdims=True).astype(jnp.int32)
    back = pltpu.make_async_copy(labels_w, labels_s, sem)
    back.start()
    back.wait()

    @pl.loop(0, req_count)
    def _(d):
        for k in range(CAP):
            slot = labels_s[d, LABEL_LANE + k]

            @pl.when(slot >= 0)
            def _():
                table[slot] = per_dev + d * CAP + k

    steps = requests // UNROLL

    def fetch(step):
        place = lax.rem(step, SLOTS)
        count = chunks_ref[step * UNROLL] * CHUNK_PAGES
        for u in range(UNROLL):
            first_slot = order_ref[step * UNROLL + u] * MAXP

            @pl.loop(0, count)
            def _(j):
                source = table[first_slot + j]
                target = buf.at[place, u, pl.ds(pl.multiple_of(j * PAGE_ROWS, PAGE_ROWS), PAGE_ROWS)]

                @pl.when(source < per_dev)
                def _():
                    pltpu.make_async_copy(page_rows.at[source], target, sems.at[place, u]).start()

                @pl.when(source >= per_dev)
                def _():
                    e = source - per_dev
                    d = lax.shift_right_logical(e, 1)
                    k = e - d * CAP
                    pltpu.make_async_copy(
                        inbox_rows.at[d, pl.ds(pl.multiple_of(k * PAGE_ROWS, PAGE_ROWS), PAGE_ROWS)],
                        target,
                        sems.at[place, u],
                    ).start()

    for s in range(SLOTS - 1):
        fetch(jnp.int32(s))

    def compute(step, n):
        place = lax.rem(step, SLOTS)
        width = n * CHUNK_ROWS
        for u in range(UNROLL):
            whole = buf.at[place, u, pl.ds(0, width)]
            pltpu.make_async_copy(whole, whole, sems.at[place, u]).wait()
        column = lax.broadcasted_iota(jnp.int32, (rows, width), 1)
        even = (column & 1) == 0
        new_column = lax.broadcasted_iota(jnp.int32, (rows, 128), 1)
        new_row = lax.broadcasted_iota(jnp.int32, (rows, 128), 0)
        new_ok = ((new_column & 1) == 0) & (((new_column & (NEW_ROWS - 1)) >> 1) <= (new_row & (STEP_COUNT - 1)))
        for u in range(UNROLL):
            r = order_ref[step * UNROLL + u]
            length = lengths_ref[r]
            q = q_ref[pl.ds(pl.multiple_of(r * rows, rows), rows), :]
            if heads_kv == 2:
                zero = jnp.zeros((half, HEAD_WIDTH), q.dtype)
                q = jnp.concatenate(
                    [jnp.concatenate([q[:half], zero], axis=1), jnp.concatenate([zero, q[half:]], axis=1)], axis=0
                )
            kv = buf[place, u, 0:width, :]
            group = r // NEW_GROUP
            new = new_ref[pl.ds(pl.multiple_of(group * 128, 128), 128), :]
            s = dot(q, kv, ((1,), (1,))) * scale
            sn = dot(q, new, ((1,), (1,))) * scale
            s = jnp.where(even & (column < 2 * length), s, -jnp.inf)
            mine = (new_column >> 3) == (r - group * NEW_GROUP)
            sn = jnp.where(new_ok & mine, sn, -jnp.inf)
            top = jnp.maximum(jnp.max(s, axis=1, keepdims=True), jnp.max(sn, axis=1, keepdims=True))
            w = jnp.exp(s - top)
            wn = jnp.exp(sn - top)
            total = jnp.sum(w, axis=1, keepdims=True) + jnp.sum(wn, axis=1, keepdims=True)
            p = pltpu.roll(w / total, 1, 1).astype(jnp.bfloat16)
            pn = pltpu.roll(wn / total, 1, 1).astype(jnp.bfloat16)
            o = dot(p, kv) + dot(pn, new)
            if heads_kv == 2:
                o = jnp.concatenate([o[:half, :HEAD_WIDTH], o[half:, HEAD_WIDTH:]], axis=0)
            for h in range(heads):
                acc[h, pl.ds(pl.multiple_of(r * STEP_COUNT, STEP_COUNT), STEP_COUNT), :] = o[
                    h * STEP_COUNT : (h + 1) * STEP_COUNT
                ]

    @pl.loop(0, steps)
    def _(step):
        @pl.when(step + (SLOTS - 1) < steps)
        def _():
            fetch(step + (SLOTS - 1))

        count = chunks_ref[step * UNROLL]
        for n in range(1, CHUNKS + 1):

            @pl.when(count == n)
            def _():
                compute(step, n)

    out_ref[...] = acc[...].astype(jnp.bfloat16)


def attend(order, chunks, lengths, table, q, new, pages, inbox):
    per_dev, _, _, columns = pages.shape
    req_count = inbox.shape[0]
    requests = lengths.shape[0]
    heads = columns // HEAD_WIDTH * GROUP
    tokens = requests * STEP_COUNT
    return pl.pallas_call(
        functools.partial(attend_kernel, req_count, per_dev, requests),
        out_shape=jax.ShapeDtypeStruct((heads, tokens, HEAD_WIDTH), jnp.bfloat16),
        in_specs=[SMEM, SMEM, SMEM, HBM, VMEM, VMEM, HBM, HBM],
        out_specs=VMEM,
        scratch_shapes=[
            pltpu.SMEM((per_dev,), jnp.int32),
            pltpu.VMEM((req_count, 1, 2, columns), jnp.bfloat16),
            pltpu.VMEM((req_count, 128), jnp.int32),
            pltpu.SMEM((req_count, 128), jnp.int32),
            pltpu.VMEM((SLOTS, UNROLL, MAXP * PAGE_ROWS, columns), jnp.bfloat16),
            pltpu.VMEM((heads, tokens, HEAD_WIDTH), jnp.float32),
            pltpu.SemaphoreType.DMA,
            pltpu.SemaphoreType.DMA((SLOTS, UNROLL)),
        ],
        compiler_params=params(),
        name="attend",
    )(order, chunks, lengths, table, q, new, pages, inbox)


def split_kernel(x_ref, o_ref):
    o_ref[0] = x_ref[...]


def split_columns(x, parts):
    rows, columns = x.shape
    block = columns // parts
    return pl.pallas_call(
        split_kernel,
        out_shape=jax.ShapeDtypeStruct((parts, rows, block), x.dtype),
        grid=(parts,),
        in_specs=[pl.BlockSpec((rows, block), lambda i: (0, i))],
        out_specs=pl.BlockSpec((1, rows, block), lambda i: (i, 0, 0)),
        compiler_params=params(),
        name="split_columns",
    )(x)


def project_kernel(x_ref, w_ref, down_ref, o_ref, low_ref):
    blocks, heads, tokens, _ = x_ref.shape
    for b in range(blocks):
        x = jnp.concatenate([x_ref[b, h] for h in range(heads)], axis=1)
        o_ref[b * tokens : (b + 1) * tokens, :] = dot(x, w_ref[...]).astype(jnp.bfloat16)

        @pl.when(pl.program_id(0) == 0)
        def _():
            low_ref[b * tokens : (b + 1) * tokens, :] = dot(x, down_ref[...], ((1,), (1,)))


def project(x, w, down):
    blocks, heads, tokens, width = x.shape
    columns = w.shape[1]
    tile = 256
    return pl.pallas_call(
        project_kernel,
        out_shape=(
            jax.ShapeDtypeStruct((blocks * tokens, columns), jnp.bfloat16),
            jax.ShapeDtypeStruct((blocks * tokens, down.shape[0]), jnp.float32),
        ),
        grid=(columns // tile,),
        in_specs=[
            pl.BlockSpec(x.shape, lambda i: (0, 0, 0, 0)),
            pl.BlockSpec((w.shape[0], tile), lambda i: (0, i)),
            pl.BlockSpec(down.shape, lambda i: (0, 0)),
        ],
        out_specs=(
            pl.BlockSpec((blocks * tokens, tile), lambda i: (0, i)),
            pl.BlockSpec((blocks * tokens, down.shape[0]), lambda i: (0, 0)),
        ),
        compiler_params=params(),
        name="project",
    )(x, w, down)


def finish_kernel(plain_ref, low_ref, up_ref, o_ref):
    o_ref[...] = (plain_ref[...].astype(jnp.float32) + dot(low_ref[...], up_ref[...])).astype(jnp.bfloat16)


def finish(plain, low, up):
    return pl.pallas_call(
        finish_kernel,
        out_shape=jax.ShapeDtypeStruct(plain.shape, jnp.bfloat16),
        in_specs=[VMEM, VMEM, VMEM],
        out_specs=VMEM,
        compiler_params=params(),
        name="finish",
    )(plain, low, up)


def on_device(
    queries,
    incoming_key_value,
    key_value_pages,
    page_request_home,
    lengths,
    request_adapter_index,
    adapter_storage_slot,
    adapter_down_factor,
    adapter_up_factor,
    output_projection_weight,
):
    req_count = lax.axis_size("req")
    my_req = lax.axis_index("req")
    my_lane = lax.axis_index("tp")
    tp_count = lax.axis_size("tp")
    me = my_req.astype(jnp.int32).reshape(1)
    requests = lengths.shape[0]
    columns = key_value_pages.shape[-1]
    heads = columns // HEAD_WIDTH * GROUP
    own_slots, rank, model = adapter_up_factor.shape

    outbox = pack(me, page_request_home, request_adapter_index, key_value_pages, req_count)
    inbox = lax.all_to_all(outbox, "req", split_axis=0, concat_axis=0, tiled=True)

    table, order, chunks = build_table(me, page_request_home, lengths)
    q = queries.reshape(requests, STEP_COUNT, heads, HEAD_WIDTH).transpose(0, 2, 1, 3)
    q = q.reshape(requests * heads * STEP_COUNT, HEAD_WIDTH)
    new = incoming_key_value.transpose(1, 0, 2).reshape(-1, columns)
    up = split_columns(adapter_up_factor.reshape(own_slots * rank, model), req_count)
    up = lax.all_to_all(up, "req", split_axis=0, concat_axis=0, tiled=True)
    up = up.reshape(req_count * own_slots * rank, -1)

    mixed = attend(order, chunks, lengths, table, q, new, key_value_pages, inbox)
    everyone = lax.all_gather(mixed, "req", axis=0)

    ids = inbox[:, BLOCK - 1, 0, :requests].astype(jnp.int32).reshape(-1)
    slot_count = adapter_storage_slot.shape[0]
    match = ids[:, None] == jnp.arange(slot_count, dtype=jnp.int32)[None, :]
    slot = jnp.sum(jnp.where(match, adapter_storage_slot[None, :], 0), axis=1)
    token_slot = jnp.repeat(slot, STEP_COUNT)

    down = adapter_down_factor.transpose(0, 2, 1).reshape(own_slots * rank, -1)
    partial, low = project(everyone, output_projection_weight, down)
    kept = jnp.zeros((low.shape[0], rank), jnp.float32)
    for k in range(own_slots):
        here = token_slot == my_req * own_slots + k
        kept = kept + jnp.where(here[:, None], low[:, k * rank : (k + 1) * rank], 0.0)
    low_rows = lax.psum_scatter(kept, "tp", scatter_dimension=0, tiled=True)
    low_rows = lax.psum(low_rows, "req").astype(jnp.bfloat16)
    plain = lax.psum_scatter(partial, "tp", scatter_dimension=0, tiled=True)

    block_rows = low_rows.shape[0]
    block_slot = lax.dynamic_slice_in_dim(token_slot, my_lane * block_rows, block_rows)
    selector = (block_slot[:, None] == jnp.arange(slot_count, dtype=jnp.int32)[None, :]).astype(jnp.bfloat16)
    expanded = (selector[:, :, None] * low_rows[:, None, :]).reshape(block_rows, slot_count * rank)
    return finish(plain, expanded, up)


def solution(mesh):
    return jax.shard_map(
        on_device,
        mesh=mesh,
        in_specs=(
            P("req", "tp"),
            P(None, "req", "tp"),
            P("req", None, None, "tp"),
            P("req"),
            P("req"),
            P("req"),
            P(),
            P("req", "tp", None),
            P("req", None, None),
            P("tp", "req"),
        ),
        out_specs=P("tp", "req"),
        check_vma=False,
    )
```

```python
import functools
import math

import jax
import jax.numpy as jnp
from jax import lax
from jax.experimental import pallas as pl
from jax.experimental.pallas import tpu as pltpu
from jax.sharding import PartitionSpec as P

QUERY_HEADS = 64
KEY_VALUE_HEADS = 8
GROUP = QUERY_HEADS // KEY_VALUE_HEADS
HEAD_WIDTH = 128
STEP_COUNT = 4
PAGE_LENGTH = 32
MAXP = 16
CAP = 2
BLOCK = CAP * PAGE_LENGTH + 1
LABEL_LANE = 64
DIGIT = 16
CHUNK_PAGES = 4
CHUNKS = MAXP // CHUNK_PAGES
PAGE_ROWS = PAGE_LENGTH * 2
CHUNK_ROWS = CHUNK_PAGES * PAGE_ROWS
NEW_ROWS = STEP_COUNT * 2
NEW_GROUP = 128 // NEW_ROWS
UNROLL = 2
SLOTS = 6
HALVES = 2
VMEM_LIMIT = 56 * 1024 * 1024

HBM = pl.BlockSpec(memory_space=pltpu.HBM)
VMEM = pl.BlockSpec(memory_space=pltpu.VMEM)
SMEM = pl.BlockSpec(memory_space=pltpu.SMEM)


def params():
    return pltpu.CompilerParams(vmem_limit_bytes=VMEM_LIMIT)


def dot(a, b, contract=((1,), (0,))):
    return lax.dot_general(a, b, (contract, ((), ())), preferred_element_type=jnp.float32)


def pack_kernel(req_count, per_dev, me_ref, home_ref, ids_ref, pages, outbox, info_v, info_s, ids_v, rows_v, sem, sems):
    me = me_ref[0]
    page = lax.broadcasted_iota(jnp.int32, (req_count, per_dev), 1)
    want = lax.broadcasted_iota(jnp.int32, (req_count, per_dev), 0)
    slots = jnp.broadcast_to(home_ref[...], (req_count, per_dev)) - want * per_dev
    hit = (slots >= 0) & (slots < per_dev) & (want != me)
    lane = lax.broadcasted_iota(jnp.int32, (req_count, 128), 1)
    info = jnp.full((req_count, 128), -1, jnp.int32)
    for k in range(CAP):
        first = jnp.min(jnp.where(hit, page, per_dev), axis=1, keepdims=True)
        here = hit & (page == first)
        slot = jnp.max(jnp.where(here, slots, -1), axis=1, keepdims=True)
        info = jnp.where(lane == k, first, info)
        info = jnp.where(lane == CAP + k, slot, info)
        hit = hit & (page != first)
    info_v[...] = info
    fetch = pltpu.make_async_copy(info_v, info_s, sem)
    fetch.start()
    ids_v[...] = jnp.zeros_like(ids_v)
    ids_v[:, 0:ids_ref.shape[1]] = ids_ref[...].astype(jnp.float32)
    ids = jnp.broadcast_to(ids_v[...], (2, 128))
    fetch.wait()

    def copy(d, k):
        return pltpu.make_async_copy(
            pages.at[info_s[d, k]],
            outbox.at[d, pl.ds(k * PAGE_LENGTH, PAGE_LENGTH)],
            sems.at[d, k],
        )

    for d in range(req_count):
        for k in range(CAP):

            @pl.when(info_s[d, k] < per_dev)
            def _():
                copy(d, k).start()

    at = lax.broadcasted_iota(jnp.int32, (2, 128), 1)
    row = lax.broadcasted_iota(jnp.int32, (2, 128), 0)
    for d in range(req_count):
        value = jnp.where(row == 0, ids, 0.0)
        for k in range(CAP):
            slot = info_s[d, CAP + k]
            high = ((slot + DIGIT) >> 4) - 1
            low = slot - high * DIGIT
            digit = jnp.where(row == 0, high, low).astype(jnp.float32)
            value = jnp.where(at == LABEL_LANE + k, digit, value)
        rows_v[d, 0, :, :] = jnp.zeros(rows_v.shape[2:], jnp.bfloat16)
        rows_v[d, 0, :, 0:128] = value.astype(jnp.bfloat16)
    rows = pltpu.make_async_copy(rows_v, outbox.at[:, pl.ds(BLOCK - 1, 1)], sem)
    rows.start()
    rows.wait()
    for d in range(req_count):
        for k in range(CAP):

            @pl.when(info_s[d, k] < per_dev)
            def _():
                copy(d, k).wait()


def pack(me, page_request_home, ids, key_value_pages, req_count):
    per_dev = key_value_pages.shape[0]
    columns = key_value_pages.shape[-1]
    return pl.pallas_call(
        functools.partial(pack_kernel, req_count, per_dev),
        out_shape=jax.ShapeDtypeStruct((req_count, BLOCK, 2, columns), jnp.bfloat16),
        in_specs=[SMEM, VMEM, VMEM, HBM],
        out_specs=VMEM,
        scratch_shapes=[
            pltpu.VMEM((req_count, 128), jnp.int32),
            pltpu.SMEM((req_count, 128), jnp.int32),
            pltpu.VMEM((1, 128), jnp.float32),
            pltpu.VMEM((req_count, 1, 2, columns), jnp.bfloat16),
            pltpu.SemaphoreType.DMA,
            pltpu.SemaphoreType.DMA((req_count, CAP)),
        ],
        compiler_params=params(),
        name="pack_outbox",
    )(me, page_request_home.reshape(1, per_dev), ids.reshape(1, -1), key_value_pages)


def table_kernel(per_dev, requests, me_ref, home_ref, lengths_ref, table_ref, order_ref, len_v):
    base = me_ref[0] * per_dev
    lane = lax.broadcasted_iota(jnp.int32, (128, 128), 1)
    row = lax.broadcasted_iota(jnp.int32, (128, 128), 0)
    tiles = per_dev // 128
    columns = [
        jnp.transpose(jnp.broadcast_to(home_ref[i : i + 1, :] - base, (128, 128)).astype(jnp.float32))
        for i in range(tiles)
    ]
    for j in range(tiles):
        total = jnp.zeros((128, 128), jnp.float32)
        slot = (lane + j * 128).astype(jnp.float32)
        for i in range(tiles):
            total = total + jnp.where(columns[i] == slot, (row + i * 128).astype(jnp.float32), 0.0)
        table_ref[j : j + 1, :] = jnp.sum(total, axis=0, keepdims=True).astype(jnp.int32)
    half = requests // HALVES
    len_v[...] = jnp.zeros_like(len_v)
    len_v[:, 0:requests] = lengths_ref[...].astype(jnp.float32)
    along = jnp.broadcast_to(len_v[...], (128, 128))
    along = ((along.astype(jnp.int32) + (CHUNK_ROWS // 2 - 1)) >> 7).astype(jnp.float32)
    down = jnp.transpose(along)
    same = (lane // half) == (row // half)
    before = same & ((along > down) | ((along == down) & (lane < row)))
    rank = jnp.sum(jnp.where(before, 1.0, 0.0), axis=1, keepdims=True)
    place = rank + ((row // half) * half).astype(jnp.float32)
    at = place == lane.astype(jnp.float32)
    order = jnp.sum(jnp.where(at, row.astype(jnp.float32), 0.0), axis=0, keepdims=True)
    chunks = jnp.sum(jnp.where(at, down, 0.0), axis=0, keepdims=True)
    order_ref[0:1, :] = order.astype(jnp.int32)
    order_ref[1:2, :] = chunks.astype(jnp.int32)


def build_table(me, page_request_home, lengths):
    per_dev = page_request_home.shape[0]
    requests = lengths.shape[0]
    return pl.pallas_call(
        functools.partial(table_kernel, per_dev, requests),
        out_shape=(
            jax.ShapeDtypeStruct((per_dev // 128, 128), jnp.int32),
            jax.ShapeDtypeStruct((2, 128), jnp.int32),
        ),
        in_specs=[SMEM, VMEM, VMEM],
        out_specs=(VMEM, VMEM),
        scratch_shapes=[pltpu.VMEM((1, 128), jnp.float32)],
        compiler_params=params(),
        name="page_table",
    )(me, page_request_home.reshape(per_dev // 128, 128), lengths.reshape(1, requests))


def attend_kernel(
    req_count,
    per_dev,
    base,
    requests,
    order_ref,
    lengths_ref,
    table_in,
    q_ref,
    new_ref,
    pages,
    inbox,
    out_ref,
    table,
    labels_v,
    labels_w,
    labels_s,
    buf,
    acc,
    sem,
    sems,
):
    columns = pages.shape[-1]
    heads_kv = columns // HEAD_WIDTH
    half = STEP_COUNT * GROUP
    rows = heads_kv * half
    heads = heads_kv * GROUP
    scale = math.log2(math.e) / math.sqrt(HEAD_WIDTH)
    page_rows = pages.reshape(per_dev, PAGE_ROWS, columns)
    inbox_rows = inbox.reshape(req_count, BLOCK * 2, columns)

    tab = pltpu.make_async_copy(table_in, table, sem)
    tab.start()
    tab.wait()
    first = pltpu.make_async_copy(inbox.at[:, pl.ds(BLOCK - 1, 1)], labels_v, sem)
    first.start()
    first.wait()
    row = lax.broadcasted_iota(jnp.int32, (2, 128), 0)
    weight = jnp.where(row == 0, float(DIGIT), 1.0)
    for d in range(req_count):
        digits = labels_v[d, 0, :, 0:128].astype(jnp.float32) * weight
        labels_w[d : d + 1, :] = jnp.sum(digits, axis=0, keepdims=True).astype(jnp.int32)
    back = pltpu.make_async_copy(labels_w, labels_s, sem)
    back.start()
    back.wait()
    for d in range(req_count):
        for k in range(CAP):
            slot = labels_s[d, LABEL_LANE + k]

            @pl.when(slot >= 0)
            def _():
                table[lax.shift_right_logical(slot, 7), slot & 127] = per_dev + d * CAP + k

    steps = requests // UNROLL

    def fetch(step):
        place = lax.rem(step, SLOTS)
        count = order_ref[1, base + step * UNROLL]
        for u in range(UNROLL):
            slot = order_ref[0, base + step * UNROLL + u] * MAXP
            line = lax.shift_right_logical(slot, 7)
            at = slot & 127

            @pl.loop(0, count)
            def _(c):
                sources = [table[line, at + c * CHUNK_PAGES + j] for j in range(CHUNK_PAGES)]
                most = functools.reduce(jnp.maximum, sources)

                def target(j):
                    start = pl.multiple_of(c * CHUNK_ROWS + j * PAGE_ROWS, PAGE_ROWS)
                    return buf.at[place, u, pl.ds(start, PAGE_ROWS)]

                @pl.when(most < per_dev)
                def _():
                    for j in range(CHUNK_PAGES):
                        pltpu.make_async_copy(page_rows.at[sources[j]], target(j), sems.at[place, u]).start()

                @pl.when(most >= per_dev)
                def _():
                    for j in range(CHUNK_PAGES):
                        source = sources[j]

                        @pl.when(source < per_dev)
                        def _():
                            pltpu.make_async_copy(page_rows.at[source], target(j), sems.at[place, u]).start()

                        @pl.when(source >= per_dev)
                        def _():
                            e = source - per_dev
                            d = lax.shift_right_logical(e, 1)
                            k = e - d * CAP
                            start = pl.multiple_of(k * PAGE_ROWS, PAGE_ROWS)
                            pltpu.make_async_copy(
                                inbox_rows.at[d, pl.ds(start, PAGE_ROWS)], target(j), sems.at[place, u]
                            ).start()

    for s in range(min(SLOTS - 1, steps)):
        fetch(jnp.int32(s))

    def compute(step, n):
        place = lax.rem(step, SLOTS)
        width = n * CHUNK_ROWS
        for u in range(UNROLL):
            whole = buf.at[place, u, pl.ds(0, width)]
            pltpu.make_async_copy(whole, whole, sems.at[place, u]).wait()
        column = lax.broadcasted_iota(jnp.int32, (1, width), 1)
        column = jnp.where((column & 1) == 0, column, 2 * width * CHUNKS)
        new_column = lax.broadcasted_iota(jnp.int32, (rows, 128), 1)
        new_row = lax.broadcasted_iota(jnp.int32, (rows, 128), 0)
        new_ok = ((new_column & 1) == 0) & (((new_column & (NEW_ROWS - 1)) >> 1) <= (new_row & (STEP_COUNT - 1)))
        for u in range(UNROLL):
            r = order_ref[0, base + step * UNROLL + u]
            length = lengths_ref[r]
            q = q_ref[pl.ds(pl.multiple_of(r * rows, rows), rows), :]
            if heads_kv == 2:
                zero = jnp.zeros((half, HEAD_WIDTH), q.dtype)
                q = jnp.concatenate(
                    [jnp.concatenate([q[:half], zero], axis=1), jnp.concatenate([zero, q[half:]], axis=1)], axis=0
                )
            kv = buf[place, u, 0:width, :]
            group = r // NEW_GROUP
            new = new_ref[pl.ds(pl.multiple_of(group * 128, 128), 128), :]
            bias = jnp.where(column < 2 * length, 0.0, -jnp.inf)
            s = dot(q, kv, ((1,), (1,))) * scale + bias
            mine = (new_column >> 3) == (r - group * NEW_GROUP)
            sn = jnp.where(new_ok & mine, dot(q, new, ((1,), (1,))) * scale, -jnp.inf)
            top = jnp.maximum(jnp.max(s, axis=1, keepdims=True), jnp.max(sn, axis=1, keepdims=True))
            w = jnp.exp2(s - top)
            wn = jnp.exp2(sn - top)
            inverse = 1.0 / (jnp.sum(w, axis=1, keepdims=True) + jnp.sum(wn, axis=1, keepdims=True))
            p = pltpu.roll(w * inverse, 1, 1).astype(jnp.bfloat16)
            pn = pltpu.roll(wn * inverse, 1, 1).astype(jnp.bfloat16)
            o = dot(p, kv) + dot(pn, new)
            if heads_kv == 2:
                o = jnp.concatenate([o[:half, :HEAD_WIDTH], o[half:, HEAD_WIDTH:]], axis=0)
            at = pl.multiple_of((r - base) * STEP_COUNT, STEP_COUNT)
            for h in range(heads):
                acc[h, pl.ds(at, STEP_COUNT), :] = o[h * STEP_COUNT : (h + 1) * STEP_COUNT]

    @pl.loop(0, steps)
    def _(step):
        @pl.when(step + (SLOTS - 1) < steps)
        def _():
            fetch(step + (SLOTS - 1))

        count = order_ref[1, base + step * UNROLL]
        for n in range(1, CHUNKS + 1):

            @pl.when(count == n)
            def _():
                compute(step, n)

    out_ref[...] = acc[...].astype(jnp.bfloat16)


def attend(part, order, lengths, table, q, new, pages, inbox):
    per_dev, _, _, columns = pages.shape
    req_count = inbox.shape[0]
    requests = lengths.shape[0] // HALVES
    heads = columns // HEAD_WIDTH * GROUP
    tokens = requests * STEP_COUNT
    return pl.pallas_call(
        functools.partial(attend_kernel, req_count, per_dev, part * requests, requests),
        out_shape=jax.ShapeDtypeStruct((heads, tokens, HEAD_WIDTH), jnp.bfloat16),
        in_specs=[SMEM, SMEM, HBM, VMEM, VMEM, HBM, HBM],
        out_specs=VMEM,
        scratch_shapes=[
            pltpu.SMEM((per_dev // 128, 128), jnp.int32),
            pltpu.VMEM((req_count, 1, 2, columns), jnp.bfloat16),
            pltpu.VMEM((req_count, 128), jnp.int32),
            pltpu.SMEM((req_count, 128), jnp.int32),
            pltpu.VMEM((SLOTS, UNROLL, MAXP * PAGE_ROWS, columns), jnp.bfloat16),
            pltpu.VMEM((heads, tokens, HEAD_WIDTH), jnp.float32),
            pltpu.SemaphoreType.DMA,
            pltpu.SemaphoreType.DMA((SLOTS, UNROLL)),
        ],
        compiler_params=params(),
        cost_estimate=pl.CostEstimate(
            flops=16 * tokens * heads * HEAD_WIDTH * MAXP * PAGE_LENGTH,
            bytes_accessed=requests * MAXP * PAGE_ROWS * columns * 2,
            transcendentals=2 * tokens * heads * MAXP * PAGE_LENGTH,
        ),
        name="attend",
    )(order, lengths, table, q, new, pages, inbox)


def split_kernel(x_ref, o_ref):
    o_ref[0] = x_ref[...]


def split_columns(x, parts):
    rows, columns = x.shape
    block = columns // parts
    return pl.pallas_call(
        split_kernel,
        out_shape=jax.ShapeDtypeStruct((parts, rows, block), x.dtype),
        grid=(parts,),
        in_specs=[pl.BlockSpec((rows, block), lambda i: (0, i))],
        out_specs=pl.BlockSpec((1, rows, block), lambda i: (i, 0, 0)),
        compiler_params=params(),
        name="split_columns",
    )(x)


def project_kernel(count, roles, where_ref, *refs):
    xs, (w_ref, down_ref, mask_ref), rest = refs[:count], refs[count : count + 3], refs[count + 3 :]
    outs, low_ref, x_v = rest[:roles], rest[roles], rest[roles + 1]
    heads, tokens, width = xs[0].shape
    rows = count * tokens // roles

    @pl.when(pl.program_id(0) == 0)
    def _():
        for b in range(count):
            at = pl.multiple_of(where_ref[b] * tokens, tokens)
            for h in range(heads):
                x_v[pl.ds(at, tokens), h * width : (h + 1) * width] = xs[b][h]
        for j in range(roles):
            s = where_ref[count + j]
            low = dot(x_v[j * rows : (j + 1) * rows, :], down_ref[...], ((1,), (1,)))
            low_ref[s] = (low * mask_ref[s].astype(jnp.float32)).astype(jnp.bfloat16)

    y = dot(x_v[...], w_ref[...]).astype(jnp.bfloat16)
    for j in range(roles):
        outs[j][...] = y[j * rows : (j + 1) * rows, :]


def project(where, xs, w, down, mask, roles):
    count = len(xs)
    heads, tokens, width = xs[0].shape
    columns = w.shape[1]
    rows = count * tokens // roles
    tile = min(256, columns)
    return pl.pallas_call(
        functools.partial(project_kernel, count, roles),
        out_shape=[jax.ShapeDtypeStruct((rows, columns), jnp.bfloat16)] * roles
        + [jax.ShapeDtypeStruct((roles, rows, down.shape[0]), jnp.bfloat16)],
        grid=(columns // tile,),
        in_specs=[SMEM]
        + [pl.BlockSpec(xs[0].shape, lambda i: (0, 0, 0))] * count
        + [
            pl.BlockSpec((w.shape[0], tile), lambda i: (0, i)),
            pl.BlockSpec(down.shape, lambda i: (0, 0)),
            pl.BlockSpec(mask.shape, lambda i: (0, 0, 0)),
        ],
        out_specs=[pl.BlockSpec((rows, tile), lambda i: (0, i))] * roles
        + [pl.BlockSpec((roles, rows, down.shape[0]), lambda i: (0, 0, 0))],
        scratch_shapes=[pltpu.VMEM((count * tokens, heads * width), jnp.bfloat16)],
        compiler_params=params(),
        cost_estimate=pl.CostEstimate(
            flops=2 * count * tokens * heads * width * columns,
            bytes_accessed=w.size * 2 + count * tokens * (heads * width + columns) * 2,
            transcendentals=0,
        ),
        name="project",
    )(where, *xs, w, down, mask)


def add_kernel(a_ref, b_ref, o_ref):
    o_ref[...] = (a_ref[...].astype(jnp.float32) + b_ref[...].astype(jnp.float32)).astype(jnp.bfloat16)


def add(a, b):
    return pl.pallas_call(
        add_kernel,
        out_shape=jax.ShapeDtypeStruct(a.shape, a.dtype),
        in_specs=[VMEM, VMEM],
        out_specs=VMEM,
        compiler_params=params(),
        name="add",
    )(a, b)


def finish_kernel(counts, cores, low_ref, up_ref, *refs):
    terms, o_ref = refs[:-1], refs[-1]
    low = jnp.concatenate([low_ref[a] for a in range(low_ref.shape[0])], axis=1)
    extra = dot(low, up_ref[...])
    rows = terms[0].shape[0]
    tokens = rows // cores
    first = 0
    for h, count in enumerate(counts):
        total = extra[h * rows : (h + 1) * rows, :]
        for term in terms[first : first + count]:
            total = total + term[...].astype(jnp.float32)
        first = first + count
        for c in range(cores):
            at = (c * len(counts) + h) * tokens
            o_ref[at : at + tokens, :] = total[c * tokens : (c + 1) * tokens].astype(jnp.bfloat16)


def finish(terms, cores, low, up):
    flat = [t for half in terms for t in half]
    rows, columns = flat[0].shape
    tile = min(256, columns)
    return pl.pallas_call(
        functools.partial(finish_kernel, tuple(len(half) for half in terms), cores),
        out_shape=jax.ShapeDtypeStruct((len(terms) * rows, columns), jnp.bfloat16),
        grid=(columns // tile,),
        in_specs=[
            pl.BlockSpec(low.shape, lambda i: (0, 0, 0)),
            pl.BlockSpec((up.shape[0], tile), lambda i: (0, i)),
        ]
        + [pl.BlockSpec((rows, tile), lambda i: (0, i))] * len(flat),
        out_specs=pl.BlockSpec((len(terms) * rows, tile), lambda i: (0, i)),
        compiler_params=params(),
        name="finish",
    )(low, up, *flat)


def exchange(x, axis, distance):
    count = lax.axis_size(axis)
    return lax.ppermute(x, axis, [(i, i ^ distance) for i in range(count)])


def gather(x, my_req):
    count = lax.axis_size("req")
    if count != 8:
        whole = lax.all_gather(x, "req", axis=0)
        return [whole[b] for b in range(count)], [jnp.int32(b) for b in range(count)]
    far = [x] + [exchange(x, "req", d) for d in (2, 4, 6)]
    near = [exchange(block, "req", 1) for block in far]
    return far + near, [my_req ^ d for d in (0, 2, 4, 6, 1, 3, 5, 7)]


def scatter(blocks):
    if len(blocks) != 4:
        return [lax.psum_scatter(jnp.stack(blocks), "tp", scatter_dimension=0, tiled=False)]
    own, one, two, three = blocks
    onward = lax.ppermute(three, "tp", [(0, 1), (3, 2)])
    middle = lax.ppermute(three, "tp", [(1, 2), (2, 1)])
    return [own, exchange(one, "tp", 1), middle, exchange(add(two, onward), "tp", 2)]


def on_device(
    queries,
    incoming_key_value,
    key_value_pages,
    page_request_home,
    lengths,
    request_adapter_index,
    adapter_storage_slot,
    adapter_down_factor,
    adapter_up_factor,
    output_projection_weight,
):
    req_count = lax.axis_size("req")
    tp_count = lax.axis_size("tp")
    my_req = lax.axis_index("req").astype(jnp.int32)
    my_lane = lax.axis_index("tp").astype(jnp.int32)
    me = my_req.reshape(1)
    requests = lengths.shape[0]
    half = requests // HALVES
    columns = key_value_pages.shape[-1]
    heads = columns // HEAD_WIDTH * GROUP
    own_slots, rank, model = adapter_up_factor.shape
    cores = req_count // tp_count

    outbox = pack(me, page_request_home, request_adapter_index, key_value_pages, req_count)
    inbox = lax.all_to_all(outbox, "req", split_axis=0, concat_axis=0, tiled=True)

    table, order = build_table(me, page_request_home, lengths)
    q = queries.reshape(requests, STEP_COUNT, heads, HEAD_WIDTH).transpose(0, 2, 1, 3)
    q = q.reshape(requests * heads * STEP_COUNT, HEAD_WIDTH)
    new = incoming_key_value.transpose(1, 0, 2).reshape(-1, columns)
    down = adapter_down_factor.transpose(0, 2, 1).reshape(own_slots * rank, -1)
    up = split_columns(adapter_up_factor.reshape(own_slots * rank, model), req_count)
    up = lax.all_to_all(up, "req", split_axis=0, concat_axis=0, tiled=True)
    up = up.reshape(req_count * own_slots * rank, -1)

    slot_count = adapter_storage_slot.shape[0]
    ids = inbox[:, BLOCK - 1, 0, :requests].astype(jnp.int32)
    match = ids[:, :, None] == jnp.arange(slot_count, dtype=jnp.int32)
    slot = jnp.sum(jnp.where(match, adapter_storage_slot, 0), axis=2)
    mine = my_req * own_slots + jnp.arange(own_slots * rank, dtype=jnp.int32) // rank

    special = tp_count == 4
    roles = [my_lane ^ j if special else jnp.int32(j) for j in range(tp_count)]
    terms, lows = [], []
    for h in range(HALVES):
        mixed = attend(h, order, lengths, table, q, new, key_value_pages, inbox)
        blocks, origins = gather(mixed, my_req)
        where = []
        for origin in origins:
            s = origin // cores
            where.append((s ^ my_lane if special else s) * cores + origin % cores)
        where = jnp.stack(where + roles)
        token_slot = jnp.repeat(slot[:, h * half : (h + 1) * half], STEP_COUNT, axis=1)
        mask = (token_slot.reshape(tp_count, -1)[:, :, None] == mine).astype(jnp.bfloat16)
        *parts, low = project(where, blocks, output_projection_weight, down, mask, tp_count)
        lows.append(low)
        terms.append(scatter(parts))

    low = jnp.concatenate(lows, axis=1)
    low = lax.all_to_all(low, "tp", split_axis=0, concat_axis=0, tiled=True)
    low = jnp.sum(low.astype(jnp.float32), axis=0).astype(jnp.bfloat16)
    low = lax.all_gather(low, "req", axis=0)
    return finish(terms, cores, low, up)


def solution(mesh):
    return jax.shard_map(
        on_device,
        mesh=mesh,
        in_specs=(
            P("req", "tp"),
            P(None, "req", "tp"),
            P("req", None, None, "tp"),
            P("req"),
            P("req"),
            P("req"),
            P(),
            P("req", "tp", None),
            P("req", None, None),
            P("tp", "req"),
        ),
        out_specs=P("tp", "req"),
        check_vma=False,
    )
```

```python
import functools
import math

import jax
import jax.numpy as jnp
from jax import lax
from jax.experimental import pallas as pl
from jax.experimental.pallas import tpu as pltpu
from jax.sharding import PartitionSpec as P

QUERY_HEADS = 64
KEY_VALUE_HEADS = 8
GROUP = QUERY_HEADS // KEY_VALUE_HEADS
HEAD_WIDTH = 128
STEP_COUNT = 4
PAGE_LENGTH = 32
MAXP = 16
CAP = 2
BLOCK = CAP * PAGE_LENGTH + 1
LABEL_LANE = 64
DIGIT = 16
CHUNK_PAGES = 4
CHUNKS = MAXP // CHUNK_PAGES
CHUNK_POSITIONS = CHUNK_PAGES * PAGE_LENGTH
UNROLL = 2
SLOTS = 6
HALVES = 2
VMEM_LIMIT = 56 * 1024 * 1024

HBM = pl.BlockSpec(memory_space=pltpu.HBM)
VMEM = pl.BlockSpec(memory_space=pltpu.VMEM)
SMEM = pl.BlockSpec(memory_space=pltpu.SMEM)


def params():
    return pltpu.CompilerParams(vmem_limit_bytes=VMEM_LIMIT)


def dot(a, b, contract=((1,), (0,))):
    return lax.dot_general(a, b, (contract, ((), ())), preferred_element_type=jnp.float32)


def pack_kernel(req_count, per_dev, me_ref, home_ref, ids_ref, pages, outbox, info_v, info_s, ids_v, rows_v, sem, sems):
    me = me_ref[0]
    page = lax.broadcasted_iota(jnp.int32, (req_count, per_dev), 1)
    want = lax.broadcasted_iota(jnp.int32, (req_count, per_dev), 0)
    slots = jnp.broadcast_to(home_ref[...], (req_count, per_dev)) - want * per_dev
    hit = (slots >= 0) & (slots < per_dev) & (want != me)
    lane = lax.broadcasted_iota(jnp.int32, (req_count, 128), 1)
    info = jnp.full((req_count, 128), -1, jnp.int32)
    for k in range(CAP):
        first = jnp.min(jnp.where(hit, page, per_dev), axis=1, keepdims=True)
        here = hit & (page == first)
        slot = jnp.max(jnp.where(here, slots, -1), axis=1, keepdims=True)
        info = jnp.where(lane == k, first, info)
        info = jnp.where(lane == CAP + k, slot, info)
        hit = hit & (page != first)
    info_v[...] = info
    fetch = pltpu.make_async_copy(info_v, info_s, sem)
    fetch.start()
    ids_v[...] = jnp.zeros_like(ids_v)
    ids_v[:, 0:ids_ref.shape[1]] = ids_ref[...].astype(jnp.float32)
    ids = jnp.broadcast_to(ids_v[...], (2, 128))
    fetch.wait()

    def copy(d, k):
        return pltpu.make_async_copy(
            pages.at[info_s[d, k]],
            outbox.at[d, pl.ds(k * PAGE_LENGTH, PAGE_LENGTH)],
            sems.at[d, k],
        )

    for d in range(req_count):
        for k in range(CAP):

            @pl.when(info_s[d, k] < per_dev)
            def _():
                copy(d, k).start()

    at = lax.broadcasted_iota(jnp.int32, (2, 128), 1)
    row = lax.broadcasted_iota(jnp.int32, (2, 128), 0)
    for d in range(req_count):
        value = jnp.where(row == 0, ids, 0.0)
        for k in range(CAP):
            slot = info_s[d, CAP + k]
            high = ((slot + DIGIT) >> 4) - 1
            low = slot - high * DIGIT
            digit = jnp.where(row == 0, high, low).astype(jnp.float32)
            value = jnp.where(at == LABEL_LANE + k, digit, value)
        rows_v[d, 0, :, :] = jnp.zeros(rows_v.shape[2:], jnp.bfloat16)
        rows_v[d, 0, :, 0:128] = value.astype(jnp.bfloat16)
    rows = pltpu.make_async_copy(rows_v, outbox.at[:, pl.ds(BLOCK - 1, 1)], sem)
    rows.start()
    rows.wait()
    for d in range(req_count):
        for k in range(CAP):

            @pl.when(info_s[d, k] < per_dev)
            def _():
                copy(d, k).wait()


def pack(me, page_request_home, ids, key_value_pages, req_count):
    per_dev = key_value_pages.shape[0]
    columns = key_value_pages.shape[-1]
    return pl.pallas_call(
        functools.partial(pack_kernel, req_count, per_dev),
        out_shape=jax.ShapeDtypeStruct((req_count, BLOCK, 2, columns), jnp.bfloat16),
        in_specs=[SMEM, VMEM, VMEM, HBM],
        out_specs=VMEM,
        scratch_shapes=[
            pltpu.VMEM((req_count, 128), jnp.int32),
            pltpu.SMEM((req_count, 128), jnp.int32),
            pltpu.VMEM((1, 128), jnp.float32),
            pltpu.VMEM((req_count, 1, 2, columns), jnp.bfloat16),
            pltpu.SemaphoreType.DMA,
            pltpu.SemaphoreType.DMA((req_count, CAP)),
        ],
        compiler_params=params(),
        name="pack_outbox",
    )(me, page_request_home.reshape(1, per_dev), ids.reshape(1, -1), key_value_pages)


def table_kernel(per_dev, requests, me_ref, home_ref, lengths_ref, table_ref, order_ref, len_v):
    base = me_ref[0] * per_dev
    lane = lax.broadcasted_iota(jnp.int32, (128, 128), 1)
    row = lax.broadcasted_iota(jnp.int32, (128, 128), 0)
    tiles = per_dev // 128
    columns = [
        jnp.transpose(jnp.broadcast_to(home_ref[i : i + 1, :] - base, (128, 128)).astype(jnp.float32))
        for i in range(tiles)
    ]
    for j in range(tiles):
        total = jnp.zeros((128, 128), jnp.float32)
        slot = (lane + j * 128).astype(jnp.float32)
        for i in range(tiles):
            total = total + jnp.where(columns[i] == slot, (row + i * 128).astype(jnp.float32), 0.0)
        table_ref[j : j + 1, :] = jnp.sum(total, axis=0, keepdims=True).astype(jnp.int32)
    half = requests // HALVES
    len_v[...] = jnp.zeros_like(len_v)
    len_v[:, 0:requests] = lengths_ref[...].astype(jnp.float32)
    along = jnp.broadcast_to(len_v[...], (128, 128))
    along = ((along.astype(jnp.int32) + (CHUNK_POSITIONS - 1)) >> 7).astype(jnp.float32)
    down = jnp.transpose(along)
    same = (lane // half) == (row // half)
    before = same & ((along > down) | ((along == down) & (lane < row)))
    rank = jnp.sum(jnp.where(before, 1.0, 0.0), axis=1, keepdims=True)
    place = rank + ((row // half) * half).astype(jnp.float32)
    at = place == lane.astype(jnp.float32)
    order = jnp.sum(jnp.where(at, row.astype(jnp.float32), 0.0), axis=0, keepdims=True)
    chunks = jnp.sum(jnp.where(at, down, 0.0), axis=0, keepdims=True)
    order_ref[0:1, :] = order.astype(jnp.int32)
    order_ref[1:2, :] = chunks.astype(jnp.int32)


def build_table(me, page_request_home, lengths):
    per_dev = page_request_home.shape[0]
    requests = lengths.shape[0]
    return pl.pallas_call(
        functools.partial(table_kernel, per_dev, requests),
        out_shape=(
            jax.ShapeDtypeStruct((per_dev // 128, 128), jnp.int32),
            jax.ShapeDtypeStruct((2, 128), jnp.int32),
        ),
        in_specs=[SMEM, VMEM, VMEM],
        out_specs=(VMEM, VMEM),
        scratch_shapes=[pltpu.VMEM((1, 128), jnp.float32)],
        compiler_params=params(),
        name="page_table",
    )(me, page_request_home.reshape(per_dev // 128, 128), lengths.reshape(1, requests))


def attend_kernel(
    req_count,
    per_dev,
    base,
    requests,
    order_ref,
    lengths_ref,
    table_in,
    q_ref,
    new_ref,
    pages,
    inbox,
    out_ref,
    table,
    labels_v,
    labels_w,
    labels_s,
    buf,
    acc,
    sem,
    sems,
):
    heads_kv = pages.shape[2]
    page_size = PAGE_LENGTH * heads_kv * 2
    chunk_size = CHUNK_PAGES * page_size
    new_rows = STEP_COUNT * heads_kv * 2
    new_group = 128 // new_rows
    half = STEP_COUNT * GROUP
    rows = heads_kv * half
    heads = heads_kv * GROUP
    scale = math.log2(math.e) / math.sqrt(HEAD_WIDTH)
    page_rows = pages.reshape(per_dev, page_size, HEAD_WIDTH)
    inbox_rows = inbox.reshape(req_count, BLOCK * heads_kv * 2, HEAD_WIDTH)

    tab = pltpu.make_async_copy(table_in, table, sem)
    tab.start()
    tab.wait()
    first = pltpu.make_async_copy(inbox.at[:, pl.ds(BLOCK - 1, 1)], labels_v, sem)
    first.start()
    first.wait()
    row = lax.broadcasted_iota(jnp.int32, (2, 128), 0)
    weight = jnp.where(row == 0, float(DIGIT), 1.0)
    for d in range(req_count):
        digits = labels_v[d, 0, 0, :, :].astype(jnp.float32) * weight
        labels_w[d : d + 1, :] = jnp.sum(digits, axis=0, keepdims=True).astype(jnp.int32)
    back = pltpu.make_async_copy(labels_w, labels_s, sem)
    back.start()
    back.wait()
    for d in range(req_count):
        for k in range(CAP):
            slot = labels_s[d, LABEL_LANE + k]

            @pl.when(slot >= 0)
            def _():
                table[lax.shift_right_logical(slot, 7), slot & 127] = per_dev + d * CAP + k

    steps = requests // UNROLL

    def fetch(step):
        place = lax.rem(step, SLOTS)
        count = order_ref[1, base + step * UNROLL]
        for u in range(UNROLL):
            slot = order_ref[0, base + step * UNROLL + u] * MAXP
            line = lax.shift_right_logical(slot, 7)
            at = slot & 127

            @pl.loop(0, count)
            def _(c):
                sources = [table[line, at + c * CHUNK_PAGES + j] for j in range(CHUNK_PAGES)]
                most = functools.reduce(jnp.maximum, sources)

                def target(j):
                    start = pl.multiple_of(c * chunk_size + j * page_size, page_size)
                    return buf.at[place, u, pl.ds(start, page_size)]

                @pl.when(most < per_dev)
                def _():
                    for j in range(CHUNK_PAGES):
                        pltpu.make_async_copy(page_rows.at[sources[j]], target(j), sems.at[place, u]).start()

                @pl.when(most >= per_dev)
                def _():
                    for j in range(CHUNK_PAGES):
                        source = sources[j]

                        @pl.when(source < per_dev)
                        def _():
                            pltpu.make_async_copy(page_rows.at[source], target(j), sems.at[place, u]).start()

                        @pl.when(source >= per_dev)
                        def _():
                            e = source - per_dev
                            d = lax.shift_right_logical(e, 1)
                            k = e - d * CAP
                            start = pl.multiple_of(k * page_size, page_size)
                            pltpu.make_async_copy(
                                inbox_rows.at[d, pl.ds(start, page_size)], target(j), sems.at[place, u]
                            ).start()

    for s in range(min(SLOTS - 1, steps)):
        fetch(jnp.int32(s))

    def compute(step, n):
        place = lax.rem(step, SLOTS)
        width = n * chunk_size
        for u in range(UNROLL):
            whole = buf.at[place, u, pl.ds(0, width)]
            pltpu.make_async_copy(whole, whole, sems.at[place, u]).wait()
        column = lax.broadcasted_iota(jnp.int32, (1, width), 1)
        new_column = lax.broadcasted_iota(jnp.int32, (half, 128), 1)
        new_row = lax.broadcasted_iota(jnp.int32, (half, 128), 0)
        new_step = (new_column & (new_rows - 1)) // (2 * heads_kv)
        new_key = new_column & (2 * heads_kv - 1)
        visible = new_step <= (new_row & (STEP_COUNT - 1))
        for u in range(UNROLL):
            r = order_ref[0, base + step * UNROLL + u]
            length = lengths_ref[r]
            q = q_ref[pl.ds(pl.multiple_of(r * rows, rows), rows), :]
            kv = buf[place, u, 0:width, :]
            group = r // new_group
            new = new_ref[pl.ds(pl.multiple_of(group * 128, 128), 128), :]
            seen = visible & (new_column // new_rows == r - group * new_group)
            cached = column < 2 * heads_kv * length
            whole_s = dot(q, kv, ((1,), (1,)))
            whole_sn = dot(q, new, ((1,), (1,)))
            ps, pns = [], []
            for g in range(heads_kv):
                key = (column & (2 * heads_kv - 1)) == 2 * g
                bias = jnp.where(cached & key, 0.0, -jnp.inf)
                s = whole_s[g * half : (g + 1) * half] * scale + bias
                sn = whole_sn[g * half : (g + 1) * half] * scale
                sn = jnp.where(seen & (new_key == 2 * g), sn, -jnp.inf)
                top = jnp.maximum(jnp.max(s, axis=1, keepdims=True), jnp.max(sn, axis=1, keepdims=True))
                w = jnp.exp2(s - top)
                wn = jnp.exp2(sn - top)
                inverse = 1.0 / (jnp.sum(w, axis=1, keepdims=True) + jnp.sum(wn, axis=1, keepdims=True))
                ps.append(pltpu.roll(w * inverse, 1, 1).astype(jnp.bfloat16))
                pns.append(pltpu.roll(wn * inverse, 1, 1).astype(jnp.bfloat16))
            o = dot(jnp.concatenate(ps, axis=0), kv) + dot(jnp.concatenate(pns, axis=0), new)
            at = pl.multiple_of((r - base) * STEP_COUNT, STEP_COUNT)
            for h in range(heads):
                acc[h, pl.ds(at, STEP_COUNT), :] = o[h * STEP_COUNT : (h + 1) * STEP_COUNT]

    @pl.loop(0, steps)
    def _(step):
        @pl.when(step + (SLOTS - 1) < steps)
        def _():
            fetch(step + (SLOTS - 1))

        count = order_ref[1, base + step * UNROLL]
        for n in range(1, CHUNKS + 1):

            @pl.when(count == n)
            def _():
                compute(step, n)

    out_ref[...] = acc[...].astype(jnp.bfloat16)


def attend(part, order, lengths, table, q, new, pages, inbox):
    per_dev, _, heads_kv, _, _ = pages.shape
    req_count = inbox.shape[0]
    requests = lengths.shape[0] // HALVES
    heads = heads_kv * GROUP
    extent = MAXP * PAGE_LENGTH * heads_kv * 2
    tokens = requests * STEP_COUNT
    return pl.pallas_call(
        functools.partial(attend_kernel, req_count, per_dev, part * requests, requests),
        out_shape=jax.ShapeDtypeStruct((heads, tokens, HEAD_WIDTH), jnp.bfloat16),
        in_specs=[SMEM, SMEM, HBM, VMEM, VMEM, HBM, HBM],
        out_specs=VMEM,
        scratch_shapes=[
            pltpu.SMEM((per_dev // 128, 128), jnp.int32),
            pltpu.VMEM((req_count, 1, heads_kv, 2, HEAD_WIDTH), jnp.bfloat16),
            pltpu.VMEM((req_count, 128), jnp.int32),
            pltpu.SMEM((req_count, 128), jnp.int32),
            pltpu.VMEM((SLOTS, UNROLL, extent, HEAD_WIDTH), jnp.bfloat16),
            pltpu.VMEM((heads, tokens, HEAD_WIDTH), jnp.float32),
            pltpu.SemaphoreType.DMA,
            pltpu.SemaphoreType.DMA((SLOTS, UNROLL)),
        ],
        compiler_params=params(),
        cost_estimate=pl.CostEstimate(
            flops=16 * tokens * heads * HEAD_WIDTH * MAXP * PAGE_LENGTH,
            bytes_accessed=requests * extent * HEAD_WIDTH * 2,
            transcendentals=2 * tokens * heads * MAXP * PAGE_LENGTH,
        ),
        name="attend",
    )(order, lengths, table, q, new, pages, inbox)


def split_kernel(x_ref, o_ref, sems):
    parts, _, block = o_ref.shape
    copies = [
        pltpu.make_async_copy(x_ref.at[:, pl.ds(i * block, block)], o_ref.at[i], sems.at[i]) for i in range(parts)
    ]
    for copy in copies:
        copy.start()
    for copy in copies:
        copy.wait()


def split_columns(x, parts):
    rows, columns = x.shape
    return pl.pallas_call(
        split_kernel,
        out_shape=jax.ShapeDtypeStruct((parts, rows, columns // parts), x.dtype),
        in_specs=[HBM],
        out_specs=VMEM,
        scratch_shapes=[pltpu.SemaphoreType.DMA((parts,))],
        compiler_params=params(),
        name="split_columns",
    )(x)


def project_kernel(count, roles, where_ref, *refs):
    xs, (w_ref, down_ref, mask_ref), rest = refs[:count], refs[count : count + 3], refs[count + 3 :]
    outs, low_ref, x_v = rest[:roles], rest[roles], rest[roles + 1]
    heads, tokens, width = xs[0].shape
    rows = count * tokens // roles

    @pl.when(pl.program_id(0) == 0)
    def _():
        for b in range(count):
            at = pl.multiple_of(where_ref[b] * tokens, tokens)
            for h in range(heads):
                x_v[pl.ds(at, tokens), h * width : (h + 1) * width] = xs[b][h]
        for j in range(roles):
            s = where_ref[count + j]
            low = dot(x_v[j * rows : (j + 1) * rows, :], down_ref[...], ((1,), (1,)))
            low_ref[s] = (low * mask_ref[s].astype(jnp.float32)).astype(jnp.bfloat16)

    y = dot(x_v[...], w_ref[...]).astype(jnp.bfloat16)
    for j in range(roles):
        outs[j][...] = y[j * rows : (j + 1) * rows, :]


def project(where, xs, w, down, mask, roles):
    count = len(xs)
    heads, tokens, width = xs[0].shape
    columns = w.shape[1]
    rows = count * tokens // roles
    tile = min(256, columns)
    return pl.pallas_call(
        functools.partial(project_kernel, count, roles),
        out_shape=[jax.ShapeDtypeStruct((rows, columns), jnp.bfloat16)] * roles
        + [jax.ShapeDtypeStruct((roles, rows, down.shape[0]), jnp.bfloat16)],
        grid=(columns // tile,),
        in_specs=[SMEM]
        + [pl.BlockSpec(xs[0].shape, lambda i: (0, 0, 0))] * count
        + [
            pl.BlockSpec((w.shape[0], tile), lambda i: (0, i)),
            pl.BlockSpec(down.shape, lambda i: (0, 0)),
            pl.BlockSpec(mask.shape, lambda i: (0, 0, 0)),
        ],
        out_specs=[pl.BlockSpec((rows, tile), lambda i: (0, i))] * roles
        + [pl.BlockSpec((roles, rows, down.shape[0]), lambda i: (0, 0, 0))],
        scratch_shapes=[pltpu.VMEM((count * tokens, heads * width), jnp.bfloat16)],
        compiler_params=params(),
        cost_estimate=pl.CostEstimate(
            flops=2 * count * tokens * heads * width * columns,
            bytes_accessed=w.size * 2 + count * tokens * (heads * width + columns) * 2,
            transcendentals=0,
        ),
        name="project",
    )(where, *xs, w, down, mask)


def add_kernel(a_ref, b_ref, o_ref):
    o_ref[...] = (a_ref[...].astype(jnp.float32) + b_ref[...].astype(jnp.float32)).astype(jnp.bfloat16)


def add(a, b):
    return pl.pallas_call(
        add_kernel,
        out_shape=jax.ShapeDtypeStruct(a.shape, a.dtype),
        in_specs=[VMEM, VMEM],
        out_specs=VMEM,
        compiler_params=params(),
        name="add",
    )(a, b)


def finish_kernel(counts, cores, low_ref, up_ref, *refs):
    terms, o_ref = refs[:-1], refs[-1]
    low = jnp.concatenate([low_ref[a] for a in range(low_ref.shape[0])], axis=1)
    extra = dot(low, up_ref[...])
    rows = terms[0].shape[0]
    tokens = rows // cores
    first = 0
    for h, count in enumerate(counts):
        total = extra[h * rows : (h + 1) * rows, :]
        for term in terms[first : first + count]:
            total = total + term[...].astype(jnp.float32)
        first = first + count
        for c in range(cores):
            at = (c * len(counts) + h) * tokens
            o_ref[at : at + tokens, :] = total[c * tokens : (c + 1) * tokens].astype(jnp.bfloat16)


def finish(terms, cores, low, up):
    flat = [t for half in terms for t in half]
    rows, columns = flat[0].shape
    tile = min(256, columns)
    return pl.pallas_call(
        functools.partial(finish_kernel, tuple(len(half) for half in terms), cores),
        out_shape=jax.ShapeDtypeStruct((len(terms) * rows, columns), jnp.bfloat16),
        grid=(columns // tile,),
        in_specs=[
            pl.BlockSpec(low.shape, lambda i: (0, 0, 0)),
            pl.BlockSpec((up.shape[0], tile), lambda i: (0, i)),
        ]
        + [pl.BlockSpec((rows, tile), lambda i: (0, i))] * len(flat),
        out_specs=pl.BlockSpec((len(terms) * rows, tile), lambda i: (0, i)),
        compiler_params=params(),
        name="finish",
    )(low, up, *flat)


def exchange(x, axis, distance):
    count = lax.axis_size(axis)
    return lax.ppermute(x, axis, [(i, i ^ distance) for i in range(count)])


def after(x, *others):
    return lax.optimization_barrier((x, *others))[0]


def gather(x, gates):
    my_req = lax.axis_index("req").astype(jnp.int32)
    count = lax.axis_size("req")
    if count != 8:
        whole = lax.all_gather(x, "req", axis=0)
        return [whole[b] for b in range(count)], [jnp.int32(b) for b in range(count)], []
    far = [exchange(x, "req", d) for d in (2, 4, 6)]
    held = [x] + [after(block, *gates) for block in far] if gates else [x] + far
    near = [exchange(block, "req", 1) for block in held]
    return held + near, [my_req ^ d for d in (0, 2, 4, 6, 1, 3, 5, 7)], far


def scatter(blocks):
    if len(blocks) != 4:
        return [lax.psum_scatter(jnp.stack(blocks), "tp", scatter_dimension=0, tiled=False)], blocks[0]
    own, one, two, three = blocks
    onward = lax.ppermute(three, "tp", [(0, 1), (3, 2)])
    middle = lax.ppermute(three, "tp", [(1, 2), (2, 1)])
    passed = add(two, onward)
    return [own, exchange(one, "tp", 1), middle, exchange(passed, "tp", 2)], passed


def split_heads(x):
    return x.reshape(*x.shape[:3], -1, HEAD_WIDTH).transpose(0, 1, 3, 2, 4)


def on_device(
    queries,
    incoming_key_value,
    key_value_pages,
    page_request_home,
    lengths,
    request_adapter_index,
    adapter_storage_slot,
    adapter_down_factor,
    adapter_up_factor,
    output_projection_weight,
):
    req_count = lax.axis_size("req")
    tp_count = lax.axis_size("tp")
    my_req = lax.axis_index("req").astype(jnp.int32)
    my_lane = lax.axis_index("tp").astype(jnp.int32)
    me = my_req.reshape(1)
    requests = lengths.shape[0]
    half = requests // HALVES
    columns = key_value_pages.shape[-1]
    heads = columns // HEAD_WIDTH * GROUP
    own_slots, rank, model = adapter_up_factor.shape
    cores = req_count // tp_count

    outbox = pack(me, page_request_home, request_adapter_index, key_value_pages, req_count)
    inbox = lax.all_to_all(outbox, "req", split_axis=0, concat_axis=0, tiled=True)

    table, order = build_table(me, page_request_home, lengths)
    q = queries.reshape(requests, STEP_COUNT, heads, HEAD_WIDTH).transpose(0, 2, 1, 3)
    q = q.reshape(requests * heads * STEP_COUNT, HEAD_WIDTH)
    up_blocks = split_columns(adapter_up_factor.reshape(own_slots * rank, model), req_count)
    new = incoming_key_value.reshape(2, requests * STEP_COUNT, -1, HEAD_WIDTH).transpose(1, 2, 0, 3)
    new = new.reshape(-1, HEAD_WIDTH)
    q = after(q, up_blocks)
    pages = split_heads(key_value_pages)
    inbox_pages = split_heads(inbox)
    down = adapter_down_factor.transpose(0, 2, 1).reshape(own_slots * rank, -1)
    up = lax.all_to_all(up_blocks, "req", split_axis=0, concat_axis=0, tiled=True)
    up = up.reshape(req_count * own_slots * rank, -1)

    slot_count = adapter_storage_slot.shape[0]
    ids = inbox[:, BLOCK - 1, 0, :requests].astype(jnp.int32)
    match = ids[:, :, None] == jnp.arange(slot_count, dtype=jnp.int32)
    slot = jnp.sum(jnp.where(match, adapter_storage_slot, 0), axis=2)
    mine = my_req * own_slots + jnp.arange(own_slots * rank, dtype=jnp.int32) // rank

    special = tp_count == 4
    roles = [my_lane ^ j if special else jnp.int32(j) for j in range(tp_count)]
    terms, lows, early, gates = [], [], [], []
    mixed = [attend(h, order, lengths, table, q, new, pages, inbox_pages) for h in range(HALVES)]
    for h in range(HALVES):
        blocks, origins, far = gather(after(mixed[h], *early), gates)
        early = far
        where = []
        for origin in origins:
            s = origin // cores
            where.append((s ^ my_lane if special else s) * cores + origin % cores)
        where = jnp.stack(where + roles)
        token_slot = jnp.repeat(slot[:, h * half : (h + 1) * half], STEP_COUNT, axis=1)
        mask = (token_slot.reshape(tp_count, -1)[:, :, None] == mine).astype(jnp.bfloat16)
        mask = after(mask, passed if h else up)
        *parts, low = project(where, blocks, output_projection_weight, down, mask, tp_count)
        gates = [low]
        lows.append(low)
        sums, passed = scatter(parts)
        terms.append(sums)

    low = after(jnp.concatenate(lows, axis=1), passed)
    low = lax.all_to_all(low, "tp", split_axis=0, concat_axis=0, tiled=True)
    low = jnp.sum(low.astype(jnp.float32), axis=0).astype(jnp.bfloat16)
    low = lax.all_gather(low, "req", axis=0)
    return finish(terms, cores, low, up)


def solution(mesh):
    return jax.shard_map(
        on_device,
        mesh=mesh,
        in_specs=(
            P("req", "tp"),
            P(None, "req", "tp"),
            P("req", None, None, "tp"),
            P("req"),
            P("req"),
            P("req"),
            P(),
            P("req", "tp", None),
            P("req", None, None),
            P("tp", "req"),
        ),
        out_specs=P("tp", "req"),
        check_vma=False,
    )
```

```python
import functools
import math

import jax
import jax.numpy as jnp
from jax import lax
from jax.experimental import pallas as pl
from jax.experimental.pallas import tpu as pltpu
from jax.sharding import PartitionSpec as P

QUERY_HEADS = 64
KEY_VALUE_HEADS = 8
GROUP = QUERY_HEADS // KEY_VALUE_HEADS
HEAD_WIDTH = 128
STEP_COUNT = 4
PAGE_LENGTH = 32
MAXP = 16
CAP = 2
BLOCK = CAP * PAGE_LENGTH + 1
LABEL_LANE = 64
DIGIT = 16
CHUNK_PAGES = 4
CHUNKS = MAXP // CHUNK_PAGES
CHUNK_POSITIONS = CHUNK_PAGES * PAGE_LENGTH
UNROLL = 2
SLOTS = 6
HALVES = 2
VMEM_LIMIT = 56 * 1024 * 1024

SMALL = pl.CostEstimate(flops=1, bytes_accessed=1, transcendentals=0)

ANY = pl.BlockSpec(memory_space=pl.ANY)
HBM = pl.BlockSpec(memory_space=pltpu.HBM)
VMEM = pl.BlockSpec(memory_space=pltpu.VMEM)
SMEM = pl.BlockSpec(memory_space=pltpu.SMEM)


def params():
    return pltpu.CompilerParams(vmem_limit_bytes=VMEM_LIMIT)


def dot(a, b, contract=((1,), (0,))):
    return lax.dot_general(a, b, (contract, ((), ())), preferred_element_type=jnp.float32)


def pack_kernel(req_count, per_dev, me_ref, home_ref, ids_ref, pages, outbox, info_v, info_s, ids_v, rows_v, sem, sems):
    me = me_ref[0]
    page = lax.broadcasted_iota(jnp.int32, (req_count, per_dev), 1)
    want = lax.broadcasted_iota(jnp.int32, (req_count, per_dev), 0)
    slots = jnp.broadcast_to(home_ref[...], (req_count, per_dev)) - want * per_dev
    hit = (slots >= 0) & (slots < per_dev) & (want != me)
    lane = lax.broadcasted_iota(jnp.int32, (req_count, 128), 1)
    info = jnp.full((req_count, 128), -1, jnp.int32)
    for k in range(CAP):
        first = jnp.min(jnp.where(hit, page, per_dev), axis=1, keepdims=True)
        here = hit & (page == first)
        slot = jnp.max(jnp.where(here, slots, -1), axis=1, keepdims=True)
        info = jnp.where(lane == k, first, info)
        info = jnp.where(lane == CAP + k, slot, info)
        hit = hit & (page != first)
    info_v[...] = info
    fetch = pltpu.make_async_copy(info_v, info_s, sem)
    fetch.start()
    ids_v[...] = jnp.zeros_like(ids_v)
    ids_v[:, 0:ids_ref.shape[1]] = ids_ref[...].astype(jnp.float32)
    ids = jnp.broadcast_to(ids_v[...], (2, 128))
    fetch.wait()

    def copy(d, k):
        return pltpu.make_async_copy(
            pages.at[info_s[d, k]],
            outbox.at[d, pl.ds(k * PAGE_LENGTH, PAGE_LENGTH)],
            sems.at[d, k],
        )

    for d in range(req_count):
        for k in range(CAP):

            @pl.when(info_s[d, k] < per_dev)
            def _():
                copy(d, k).start()

    at = lax.broadcasted_iota(jnp.int32, (2, 128), 1)
    row = lax.broadcasted_iota(jnp.int32, (2, 128), 0)
    for d in range(req_count):
        value = jnp.where(row == 0, ids, 0.0)
        for k in range(CAP):
            slot = info_s[d, CAP + k]
            high = ((slot + DIGIT) >> 4) - 1
            low = slot - high * DIGIT
            digit = jnp.where(row == 0, high, low).astype(jnp.float32)
            value = jnp.where(at == LABEL_LANE + k, digit, value)
        rows_v[d, 0, :, :] = jnp.zeros(rows_v.shape[2:], jnp.bfloat16)
        rows_v[d, 0, :, 0:128] = value.astype(jnp.bfloat16)
    rows = pltpu.make_async_copy(rows_v, outbox.at[:, pl.ds(BLOCK - 1, 1)], sem)
    rows.start()
    rows.wait()
    for d in range(req_count):
        for k in range(CAP):

            @pl.when(info_s[d, k] < per_dev)
            def _():
                copy(d, k).wait()


def pack(me, page_request_home, ids, key_value_pages, req_count):
    per_dev = key_value_pages.shape[0]
    columns = key_value_pages.shape[-1]
    return pl.pallas_call(
        functools.partial(pack_kernel, req_count, per_dev),
        out_shape=jax.ShapeDtypeStruct((req_count, BLOCK, 2, columns), jnp.bfloat16),
        in_specs=[SMEM, VMEM, VMEM, HBM],
        out_specs=VMEM,
        scratch_shapes=[
            pltpu.VMEM((req_count, 128), jnp.int32),
            pltpu.SMEM((req_count, 128), jnp.int32),
            pltpu.VMEM((1, 128), jnp.float32),
            pltpu.VMEM((req_count, 1, 2, columns), jnp.bfloat16),
            pltpu.SemaphoreType.DMA,
            pltpu.SemaphoreType.DMA((req_count, CAP)),
        ],
        compiler_params=params(),
        cost_estimate=SMALL,
        name="pack_outbox",
    )(me, page_request_home.reshape(1, per_dev), ids.reshape(1, -1), key_value_pages)


def table_kernel(per_dev, requests, me_ref, home_ref, lengths_ref, table_ref, order_ref, len_v):
    base = me_ref[0] * per_dev
    lane = lax.broadcasted_iota(jnp.int32, (128, 128), 1)
    row = lax.broadcasted_iota(jnp.int32, (128, 128), 0)
    tiles = per_dev // 128
    columns = [
        jnp.transpose(jnp.broadcast_to(home_ref[i : i + 1, :] - base, (128, 128)).astype(jnp.float32))
        for i in range(tiles)
    ]
    for j in range(tiles):
        total = jnp.zeros((128, 128), jnp.float32)
        slot = (lane + j * 128).astype(jnp.float32)
        for i in range(tiles):
            total = total + jnp.where(columns[i] == slot, (row + i * 128).astype(jnp.float32), 0.0)
        table_ref[j : j + 1, :] = jnp.sum(total, axis=0, keepdims=True).astype(jnp.int32)
    half = requests // HALVES
    len_v[...] = jnp.zeros_like(len_v)
    len_v[:, 0:requests] = lengths_ref[...].astype(jnp.float32)
    along = jnp.broadcast_to(len_v[...], (128, 128))
    along = ((along.astype(jnp.int32) + (CHUNK_POSITIONS - 1)) >> 7).astype(jnp.float32)
    down = jnp.transpose(along)
    same = (lane // half) == (row // half)
    before = same & ((along > down) | ((along == down) & (lane < row)))
    rank = jnp.sum(jnp.where(before, 1.0, 0.0), axis=1, keepdims=True)
    place = rank + ((row // half) * half).astype(jnp.float32)
    at = place == lane.astype(jnp.float32)
    order = jnp.sum(jnp.where(at, row.astype(jnp.float32), 0.0), axis=0, keepdims=True)
    chunks = jnp.sum(jnp.where(at, down, 0.0), axis=0, keepdims=True)
    order_ref[0:1, :] = order.astype(jnp.int32)
    order_ref[1:2, :] = chunks.astype(jnp.int32)


def build_table(me, page_request_home, lengths):
    per_dev = page_request_home.shape[0]
    requests = lengths.shape[0]
    return pl.pallas_call(
        functools.partial(table_kernel, per_dev, requests),
        out_shape=(
            jax.ShapeDtypeStruct((per_dev // 128, 128), jnp.int32),
            jax.ShapeDtypeStruct((2, 128), jnp.int32),
        ),
        in_specs=[SMEM, VMEM, VMEM],
        out_specs=(VMEM, VMEM),
        scratch_shapes=[pltpu.VMEM((1, 128), jnp.float32)],
        compiler_params=params(),
        cost_estimate=SMALL,
        name="page_table",
    )(me, page_request_home.reshape(per_dev // 128, 128), lengths.reshape(1, requests))


def attend_kernel(
    req_count,
    per_dev,
    base,
    requests,
    order_ref,
    lengths_ref,
    table_in,
    q_ref,
    new_ref,
    pages,
    inbox,
    out_ref,
    table,
    labels_v,
    labels_w,
    labels_s,
    buf,
    acc,
    sem,
    sems,
):
    heads_kv = pages.shape[2]
    page_size = PAGE_LENGTH * heads_kv * 2
    chunk_size = CHUNK_PAGES * page_size
    new_rows = STEP_COUNT * heads_kv * 2
    new_group = 128 // new_rows
    half = STEP_COUNT * GROUP
    rows = heads_kv * half
    heads = heads_kv * GROUP
    scale = math.log2(math.e) / math.sqrt(HEAD_WIDTH)
    pairs = PAGE_LENGTH * heads_kv
    page_rows = pages.reshape(per_dev, pairs, 2, HEAD_WIDTH)
    inbox_rows = inbox.reshape(req_count, BLOCK * heads_kv, 2, HEAD_WIDTH)

    tab = pltpu.make_async_copy(table_in, table, sem)
    tab.start()
    tab.wait()
    first = pltpu.make_async_copy(inbox.at[:, pl.ds(BLOCK - 1, 1)], labels_v, sem)
    first.start()
    first.wait()
    row = lax.broadcasted_iota(jnp.int32, (2, 128), 0)
    weight = jnp.where(row == 0, float(DIGIT), 1.0)
    for d in range(req_count):
        digits = labels_v[d, 0, 0, :, :].astype(jnp.float32) * weight
        labels_w[d : d + 1, :] = jnp.sum(digits, axis=0, keepdims=True).astype(jnp.int32)
    back = pltpu.make_async_copy(labels_w, labels_s, sem)
    back.start()
    back.wait()
    for d in range(req_count):
        for k in range(CAP):
            slot = labels_s[d, LABEL_LANE + k]

            @pl.when(slot >= 0)
            def _():
                table[lax.shift_right_logical(slot, 7), slot & 127] = per_dev + d * CAP + k

    steps = requests // UNROLL
    flat = buf.reshape(SLOTS, UNROLL, MAXP * page_size, HEAD_WIDTH)

    def fetch(step):
        place = lax.rem(step, SLOTS)
        count = order_ref[1, base + step * UNROLL]
        for u in range(UNROLL):
            slot = order_ref[0, base + step * UNROLL + u] * MAXP
            line = lax.shift_right_logical(slot, 7)
            at = slot & 127

            @pl.loop(0, count)
            def _(c):
                sources = [table[line, at + c * CHUNK_PAGES + j] for j in range(CHUNK_PAGES)]
                most = functools.reduce(jnp.maximum, sources)

                def target(j):
                    return buf.at[place, u, pl.ds((c * CHUNK_PAGES + j) * pairs, pairs)]

                @pl.when(most < per_dev)
                def _():
                    for j in range(CHUNK_PAGES):
                        pltpu.make_async_copy(page_rows.at[sources[j]], target(j), sems.at[place, u]).start()

                @pl.when(most >= per_dev)
                def _():
                    for j in range(CHUNK_PAGES):
                        source = sources[j]

                        @pl.when(source < per_dev)
                        def _():
                            pltpu.make_async_copy(page_rows.at[source], target(j), sems.at[place, u]).start()

                        @pl.when(source >= per_dev)
                        def _():
                            e = source - per_dev
                            d = lax.shift_right_logical(e, 1)
                            k = e - d * CAP
                            pltpu.make_async_copy(
                                inbox_rows.at[d, pl.ds(k * pairs, pairs)], target(j), sems.at[place, u]
                            ).start()

    for s in range(min(SLOTS - 1, steps)):
        fetch(jnp.int32(s))

    def compute(step, n):
        place = lax.rem(step, SLOTS)
        width = n * chunk_size
        for u in range(UNROLL):
            whole = buf.at[place, u, pl.ds(0, width // 2)]
            pltpu.make_async_copy(whole, whole, sems.at[place, u]).wait()
        column = lax.broadcasted_iota(jnp.int32, (1, width), 1)
        new_column = lax.broadcasted_iota(jnp.int32, (half, 128), 1)
        new_row = lax.broadcasted_iota(jnp.int32, (half, 128), 0)
        new_step = (new_column & (new_rows - 1)) // (2 * heads_kv)
        new_key = new_column & (2 * heads_kv - 1)
        visible = new_step <= (new_row & (STEP_COUNT - 1))
        for u in range(UNROLL):
            r = order_ref[0, base + step * UNROLL + u]
            length = lengths_ref[r]
            q = q_ref[pl.ds(pl.multiple_of(r * rows, rows), rows), :]
            kv = flat[place, u, 0:width, :]
            group = r // new_group
            new = new_ref[pl.ds(pl.multiple_of(group * 128, 128), 128), :]
            seen = visible & (new_column // new_rows == r - group * new_group)
            cached = column < 2 * heads_kv * length
            whole_s = dot(q, kv, ((1,), (1,)))
            whole_sn = dot(q, new, ((1,), (1,)))
            ps, pns = [], []
            for g in range(heads_kv):
                key = (column & (2 * heads_kv - 1)) == 2 * g
                bias = jnp.where(cached & key, 0.0, -jnp.inf)
                s = whole_s[g * half : (g + 1) * half] * scale + bias
                sn = whole_sn[g * half : (g + 1) * half] * scale
                sn = jnp.where(seen & (new_key == 2 * g), sn, -jnp.inf)
                top = jnp.maximum(jnp.max(s, axis=1, keepdims=True), jnp.max(sn, axis=1, keepdims=True))
                w = jnp.exp2(s - top)
                wn = jnp.exp2(sn - top)
                inverse = 1.0 / (jnp.sum(w, axis=1, keepdims=True) + jnp.sum(wn, axis=1, keepdims=True))
                ps.append(pltpu.roll(w * inverse, 1, 1).astype(jnp.bfloat16))
                pns.append(pltpu.roll(wn * inverse, 1, 1).astype(jnp.bfloat16))
            o = dot(jnp.concatenate(ps, axis=0), kv) + dot(jnp.concatenate(pns, axis=0), new)
            at = pl.multiple_of((r - base) * STEP_COUNT, STEP_COUNT)
            for h in range(heads):
                acc[h, pl.ds(at, STEP_COUNT), :] = o[h * STEP_COUNT : (h + 1) * STEP_COUNT]

    @pl.loop(0, steps)
    def _(step):
        @pl.when(step + (SLOTS - 1) < steps)
        def _():
            fetch(step + (SLOTS - 1))

        count = order_ref[1, base + step * UNROLL]
        for n in range(1, CHUNKS + 1):

            @pl.when(count == n)
            def _():
                compute(step, n)

    for h in range(heads):
        out_ref[:, h * HEAD_WIDTH : (h + 1) * HEAD_WIDTH] = acc[h].astype(jnp.bfloat16)


def attend(part, order, lengths, table, q, new, pages, inbox):
    per_dev, _, heads_kv, _, _ = pages.shape
    req_count = inbox.shape[0]
    requests = lengths.shape[0] // HALVES
    heads = heads_kv * GROUP
    extent = MAXP * PAGE_LENGTH * heads_kv * 2
    tokens = requests * STEP_COUNT
    return pl.pallas_call(
        functools.partial(attend_kernel, req_count, per_dev, part * requests, requests),
        out_shape=jax.ShapeDtypeStruct((tokens, heads * HEAD_WIDTH), jnp.bfloat16),
        in_specs=[SMEM, SMEM, HBM, VMEM, VMEM, HBM, HBM],
        out_specs=VMEM,
        scratch_shapes=[
            pltpu.SMEM((per_dev // 128, 128), jnp.int32),
            pltpu.VMEM((req_count, 1, heads_kv, 2, HEAD_WIDTH), jnp.bfloat16),
            pltpu.VMEM((req_count, 128), jnp.int32),
            pltpu.SMEM((req_count, 128), jnp.int32),
            pltpu.VMEM((SLOTS, UNROLL, extent // 2, 2, HEAD_WIDTH), jnp.bfloat16),
            pltpu.VMEM((heads, tokens, HEAD_WIDTH), jnp.float32),
            pltpu.SemaphoreType.DMA,
            pltpu.SemaphoreType.DMA((SLOTS, UNROLL)),
        ],
        compiler_params=params(),
        cost_estimate=SMALL,
        name="attend",
    )(order, lengths, table, q, new, pages, inbox)


def split_kernel(x_ref, o_ref, sems):
    parts, _, block = o_ref.shape
    copies = [
        pltpu.make_async_copy(x_ref.at[:, pl.ds(i * block, block)], o_ref.at[i], sems.at[i]) for i in range(parts)
    ]
    for copy in copies:
        copy.start()
    for copy in copies:
        copy.wait()


def split_columns(x, parts):
    rows, columns = x.shape
    return pl.pallas_call(
        split_kernel,
        out_shape=jax.ShapeDtypeStruct((parts, rows, columns // parts), x.dtype),
        in_specs=[HBM],
        out_specs=VMEM,
        scratch_shapes=[pltpu.SemaphoreType.DMA((parts,))],
        compiler_params=params(),
        cost_estimate=SMALL,
        name="split_columns",
    )(x)


def project_kernel(count, roles, where_ref, *refs):
    xs, (w_ref, down_ref, mask_ref), rest = refs[:count], refs[count : count + 3], refs[count + 3 :]
    outs, low_ref, x_v, sems = rest[:roles], rest[roles], rest[roles + 1], rest[roles + 2]
    tokens = xs[0].shape[0]
    rows = count * tokens // roles

    @pl.when(pl.program_id(0) == 0)
    def _():
        copies = []
        for b in range(count):
            at = pl.multiple_of(where_ref[b] * tokens, tokens)
            copies.append(pltpu.make_async_copy(xs[b], x_v.at[pl.ds(at, tokens)], sems.at[b]))
        for copy in copies:
            copy.start()
        for copy in copies:
            copy.wait()
        low = dot(x_v[...], down_ref[...], ((1,), (1,)))
        for j in range(roles):
            s = where_ref[count + j]
            low_ref[s] = (low[j * rows : (j + 1) * rows] * mask_ref[s].astype(jnp.float32)).astype(jnp.bfloat16)

    y = dot(x_v[...], w_ref[...]).astype(jnp.bfloat16)
    for j in range(roles):
        outs[j][...] = y[j * rows : (j + 1) * rows, :]


def project(where, xs, w, down, mask, roles):
    count = len(xs)
    tokens, width = xs[0].shape
    columns = w.shape[1]
    rows = count * tokens // roles
    tile = min(256, columns)
    return pl.pallas_call(
        functools.partial(project_kernel, count, roles),
        out_shape=[jax.ShapeDtypeStruct((rows, columns), jnp.bfloat16)] * roles
        + [jax.ShapeDtypeStruct((roles, rows, down.shape[0]), jnp.bfloat16)],
        grid=(columns // tile,),
        in_specs=[SMEM]
        + [ANY] * count
        + [
            pl.BlockSpec((width, tile), lambda i: (0, i)),
            pl.BlockSpec(down.shape, lambda i: (0, 0)),
            pl.BlockSpec(mask.shape, lambda i: (0, 0, 0)),
        ],
        out_specs=[pl.BlockSpec((rows, tile), lambda i: (0, i))] * roles
        + [pl.BlockSpec((roles, rows, down.shape[0]), lambda i: (0, 0, 0))],
        scratch_shapes=[pltpu.VMEM((count * tokens, width), jnp.bfloat16), pltpu.SemaphoreType.DMA((count,))],
        compiler_params=params(),
        cost_estimate=SMALL,
        name="project",
    )(where, *xs, w, down, mask)


def add_kernel(a_ref, b_ref, o_ref):
    o_ref[...] = (a_ref[...].astype(jnp.float32) + b_ref[...].astype(jnp.float32)).astype(jnp.bfloat16)


def add(a, b):
    return pl.pallas_call(
        add_kernel,
        out_shape=jax.ShapeDtypeStruct(a.shape, a.dtype),
        in_specs=[VMEM, VMEM],
        out_specs=VMEM,
        compiler_params=params(),
        cost_estimate=SMALL,
        name="add",
    )(a, b)


def adapt_kernel(low_ref, up_ref, o_ref):
    low = jnp.concatenate([low_ref[a] for a in range(low_ref.shape[0])], axis=1)
    o_ref[...] = dot(low, up_ref[...])


def adapt(low, up):
    columns = up.shape[1]
    tile = min(256, columns)
    return pl.pallas_call(
        adapt_kernel,
        out_shape=jax.ShapeDtypeStruct((low.shape[1], columns), jnp.float32),
        grid=(columns // tile,),
        in_specs=[
            pl.BlockSpec(low.shape, lambda i: (0, 0, 0)),
            pl.BlockSpec((up.shape[0], tile), lambda i: (0, i)),
        ],
        out_specs=pl.BlockSpec((low.shape[1], tile), lambda i: (0, i)),
        compiler_params=params(),
        cost_estimate=SMALL,
        name="adapt",
    )(low, up)


def finish_kernel(counts, cores, extra_ref, *refs):
    terms, o_ref = refs[:-1], refs[-1]
    rows = terms[0].shape[0]
    tokens = rows // cores
    first = 0
    for h, count in enumerate(counts):
        total = extra_ref[h * rows : (h + 1) * rows, :]
        for term in terms[first : first + count]:
            total = total + term[...].astype(jnp.float32)
        first = first + count
        for c in range(cores):
            at = (c * len(counts) + h) * tokens
            o_ref[at : at + tokens, :] = total[c * tokens : (c + 1) * tokens].astype(jnp.bfloat16)


def finish(terms, cores, extra):
    flat = [t for half in terms for t in half]
    return pl.pallas_call(
        functools.partial(finish_kernel, tuple(len(half) for half in terms), cores),
        out_shape=jax.ShapeDtypeStruct(extra.shape, jnp.bfloat16),
        in_specs=[VMEM] * (1 + len(flat)),
        out_specs=VMEM,
        compiler_params=params(),
        cost_estimate=SMALL,
        name="finish",
    )(extra, *flat)


def exchange(x, axis, distance):
    count = lax.axis_size(axis)
    return lax.ppermute(x, axis, [(i, i ^ distance) for i in range(count)])


def after(x, *others):
    return lax.optimization_barrier((x, *others))[0]


def gather(x, gates):
    my_req = lax.axis_index("req").astype(jnp.int32)
    count = lax.axis_size("req")
    if count != 8:
        whole = lax.all_gather(x, "req", axis=0)
        return [whole[b] for b in range(count)], [jnp.int32(b) for b in range(count)], []
    far = [exchange(x, "req", d) for d in (2, 4, 6)]
    held = [x] + [after(block, *gates) for block in far] if gates else [x] + far
    near = [exchange(block, "req", 1) for block in held]
    return held + near, [my_req ^ d for d in (0, 2, 4, 6, 1, 3, 5, 7)], far


def scatter(blocks):
    if len(blocks) != 4:
        return [lax.psum_scatter(jnp.stack(blocks), "tp", scatter_dimension=0, tiled=False)], blocks[0]
    own, one, two, three = blocks
    onward = lax.ppermute(three, "tp", [(0, 1), (3, 2)])
    middle = lax.ppermute(three, "tp", [(1, 2), (2, 1)])
    passed = add(two, onward)
    return [own, exchange(one, "tp", 1), middle, exchange(passed, "tp", 2)], passed


def split_heads(x):
    return x.reshape(*x.shape[:3], -1, HEAD_WIDTH).transpose(0, 1, 3, 2, 4)


def on_device(
    queries,
    incoming_key_value,
    key_value_pages,
    page_request_home,
    lengths,
    request_adapter_index,
    adapter_storage_slot,
    adapter_down_factor,
    adapter_up_factor,
    output_projection_weight,
):
    req_count = lax.axis_size("req")
    tp_count = lax.axis_size("tp")
    my_req = lax.axis_index("req").astype(jnp.int32)
    my_lane = lax.axis_index("tp").astype(jnp.int32)
    me = my_req.reshape(1)
    requests = lengths.shape[0]
    half = requests // HALVES
    columns = key_value_pages.shape[-1]
    heads = columns // HEAD_WIDTH * GROUP
    own_slots, rank, model = adapter_up_factor.shape
    cores = req_count // tp_count

    outbox = pack(me, page_request_home, request_adapter_index, key_value_pages, req_count)
    inbox = lax.all_to_all(outbox, "req", split_axis=0, concat_axis=0, tiled=True)

    table, order = build_table(me, page_request_home, lengths)
    q = queries.reshape(requests, STEP_COUNT, heads, HEAD_WIDTH).transpose(0, 2, 1, 3)
    q = q.reshape(requests * heads * STEP_COUNT, HEAD_WIDTH)
    up_blocks = split_columns(adapter_up_factor.reshape(own_slots * rank, model), req_count)
    new = incoming_key_value.reshape(2, requests * STEP_COUNT, -1, HEAD_WIDTH).transpose(1, 2, 0, 3)
    new = new.reshape(-1, HEAD_WIDTH)
    q = after(q, up_blocks)
    pages = split_heads(key_value_pages)
    inbox_pages = split_heads(inbox)
    down = adapter_down_factor.transpose(0, 2, 1).reshape(own_slots * rank, -1)
    up = lax.all_to_all(up_blocks, "req", split_axis=0, concat_axis=0, tiled=True)
    up = up.reshape(req_count * own_slots * rank, -1)

    slot_count = adapter_storage_slot.shape[0]
    ids = inbox[:, BLOCK - 1, 0, :requests].astype(jnp.int32)
    match = ids[:, :, None] == jnp.arange(slot_count, dtype=jnp.int32)
    slot = jnp.sum(jnp.where(match, adapter_storage_slot, 0), axis=2)
    mine = my_req * own_slots + jnp.arange(own_slots * rank, dtype=jnp.int32) // rank

    special = tp_count == 4
    roles = [my_lane ^ j if special else jnp.int32(j) for j in range(tp_count)]
    terms, lows, early, gates = [], [], [], []
    mixed = [attend(h, order, lengths, table, q, new, pages, inbox_pages) for h in range(HALVES)]
    gates = [mixed[-1]]
    for h in range(HALVES):
        blocks, origins, far = gather(after(mixed[h], *early), gates)
        early = far
        where = []
        for origin in origins:
            s = origin // cores
            where.append((s ^ my_lane if special else s) * cores + origin % cores)
        where = jnp.stack(where + roles)
        token_slot = jnp.repeat(slot[:, h * half : (h + 1) * half], STEP_COUNT, axis=1)
        mask = (token_slot.reshape(tp_count, -1)[:, :, None] == mine).astype(jnp.bfloat16)
        mask = after(mask, passed if h else up)
        *parts, low = project(where, blocks, output_projection_weight, down, mask, tp_count)
        gates = [low]
        lows.append(low)
        sums, passed = scatter(parts)
        terms.append(sums)

    low = after(jnp.concatenate(lows, axis=1), passed)
    low = lax.all_to_all(low, "tp", split_axis=0, concat_axis=0, tiled=True)
    low = jnp.sum(low.astype(jnp.float32), axis=0).astype(jnp.bfloat16)
    low = lax.all_gather(low, "req", axis=0)
    return finish(terms, cores, adapt(low, up))


def solution(mesh):
    return jax.shard_map(
        on_device,
        mesh=mesh,
        in_specs=(
            P("req", "tp"),
            P(None, "req", "tp"),
            P("req", None, None, "tp"),
            P("req"),
            P("req"),
            P("req"),
            P(),
            P("req", "tp", None),
            P("req", None, None),
            P("tp", "req"),
        ),
        out_specs=P("tp", "req"),
        check_vma=False,
    )
```

```python
import functools
import math

import jax
import jax.numpy as jnp
from jax import lax
from jax.experimental import pallas as pl
from jax.experimental.pallas import tpu as pltpu
from jax.sharding import PartitionSpec as P

QUERY_HEADS = 64
KEY_VALUE_HEADS = 8
GROUP = QUERY_HEADS // KEY_VALUE_HEADS
HEAD_WIDTH = 128
STEP_COUNT = 4
PAGE_LENGTH = 32
MAXP = 16
CAP = 2
BLOCK = CAP * PAGE_LENGTH + 1
LABEL_LANE = 64
DIGIT = 16
CHUNK_PAGES = 4
CHUNKS = MAXP // CHUNK_PAGES
CHUNK_POSITIONS = CHUNK_PAGES * PAGE_LENGTH
BUFFERS = 12
UNROLLS = (2, 4)
PRIORITIES = (2, 1)
HALVES = 2
VMEM_LIMIT = 24 * 1024 * 1024
WHOLE_VMEM = 60 * 1024 * 1024

SMALL = pl.CostEstimate(flops=1, bytes_accessed=1, transcendentals=0)

ANY = pl.BlockSpec(memory_space=pl.ANY)
HBM = pl.BlockSpec(memory_space=pltpu.HBM)
VMEM = pl.BlockSpec(memory_space=pltpu.VMEM)
SMEM = pl.BlockSpec(memory_space=pltpu.SMEM)


def params(limit=VMEM_LIMIT):
    return pltpu.CompilerParams(vmem_limit_bytes=limit)


def dot(a, b, contract=((1,), (0,))):
    return lax.dot_general(a, b, (contract, ((), ())), preferred_element_type=jnp.float32)


def pack_kernel(req_count, per_dev, me_ref, home_ref, ids_ref, pages, outbox, info_v, info_s, ids_v, rows_v, sem, sems):
    me = me_ref[0]
    page = lax.broadcasted_iota(jnp.int32, (req_count, per_dev), 1)
    want = lax.broadcasted_iota(jnp.int32, (req_count, per_dev), 0)
    slots = jnp.broadcast_to(home_ref[...], (req_count, per_dev)) - want * per_dev
    hit = (slots >= 0) & (slots < per_dev) & (want != me)
    lane = lax.broadcasted_iota(jnp.int32, (req_count, 128), 1)
    info = jnp.full((req_count, 128), -1, jnp.int32)
    for k in range(CAP):
        first = jnp.min(jnp.where(hit, page, per_dev), axis=1, keepdims=True)
        here = hit & (page == first)
        slot = jnp.max(jnp.where(here, slots, -1), axis=1, keepdims=True)
        info = jnp.where(lane == k, first, info)
        info = jnp.where(lane == CAP + k, slot, info)
        hit = hit & (page != first)
    info_v[...] = info
    fetch = pltpu.make_async_copy(info_v, info_s, sem)
    fetch.start()
    ids_v[...] = jnp.zeros_like(ids_v)
    ids_v[:, 0:ids_ref.shape[1]] = ids_ref[...].astype(jnp.float32)
    ids = jnp.broadcast_to(ids_v[...], (2, 128))
    fetch.wait()

    def copy(d, k):
        return pltpu.make_async_copy(
            pages.at[info_s[d, k]],
            outbox.at[d, pl.ds(k * PAGE_LENGTH, PAGE_LENGTH)],
            sems.at[d, k],
        )

    for d in range(req_count):
        for k in range(CAP):

            @pl.when(info_s[d, k] < per_dev)
            def _():
                copy(d, k).start()

    at = lax.broadcasted_iota(jnp.int32, (2, 128), 1)
    row = lax.broadcasted_iota(jnp.int32, (2, 128), 0)
    for d in range(req_count):
        value = jnp.where(row == 0, ids, 0.0)
        for k in range(CAP):
            slot = info_s[d, CAP + k]
            high = ((slot + DIGIT) >> 4) - 1
            low = slot - high * DIGIT
            digit = jnp.where(row == 0, high, low).astype(jnp.float32)
            value = jnp.where(at == LABEL_LANE + k, digit, value)
        rows_v[d, 0, :, :] = jnp.zeros(rows_v.shape[2:], jnp.bfloat16)
        rows_v[d, 0, :, 0:128] = value.astype(jnp.bfloat16)
    rows = pltpu.make_async_copy(rows_v, outbox.at[:, pl.ds(BLOCK - 1, 1)], sem)
    rows.start()
    rows.wait()
    for d in range(req_count):
        for k in range(CAP):

            @pl.when(info_s[d, k] < per_dev)
            def _():
                copy(d, k).wait()


def pack(me, page_request_home, ids, key_value_pages, req_count):
    per_dev = key_value_pages.shape[0]
    columns = key_value_pages.shape[-1]
    return pl.pallas_call(
        functools.partial(pack_kernel, req_count, per_dev),
        out_shape=jax.ShapeDtypeStruct((req_count, BLOCK, 2, columns), jnp.bfloat16),
        in_specs=[SMEM, VMEM, VMEM, HBM],
        out_specs=VMEM,
        scratch_shapes=[
            pltpu.VMEM((req_count, 128), jnp.int32),
            pltpu.SMEM((req_count, 128), jnp.int32),
            pltpu.VMEM((1, 128), jnp.float32),
            pltpu.VMEM((req_count, 1, 2, columns), jnp.bfloat16),
            pltpu.SemaphoreType.DMA,
            pltpu.SemaphoreType.DMA((req_count, CAP)),
        ],
        compiler_params=params(WHOLE_VMEM),
        cost_estimate=SMALL,
        name="pack_outbox",
    )(me, page_request_home.reshape(1, per_dev), ids.reshape(1, -1), key_value_pages)


def table_kernel(per_dev, requests, me_ref, home_ref, lengths_ref, table_ref, order_ref, len_v):
    base = me_ref[0] * per_dev
    lane = lax.broadcasted_iota(jnp.int32, (128, 128), 1)
    row = lax.broadcasted_iota(jnp.int32, (128, 128), 0)
    tiles = per_dev // 128
    columns = [
        jnp.transpose(jnp.broadcast_to(home_ref[i : i + 1, :] - base, (128, 128)).astype(jnp.float32))
        for i in range(tiles)
    ]
    for j in range(tiles):
        total = jnp.zeros((128, 128), jnp.float32)
        slot = (lane + j * 128).astype(jnp.float32)
        for i in range(tiles):
            total = total + jnp.where(columns[i] == slot, (row + i * 128).astype(jnp.float32), 0.0)
        table_ref[j : j + 1, :] = jnp.sum(total, axis=0, keepdims=True).astype(jnp.int32)
    half = requests // HALVES
    len_v[...] = jnp.zeros_like(len_v)
    len_v[:, 0:requests] = lengths_ref[...].astype(jnp.float32)
    along = jnp.broadcast_to(len_v[...], (128, 128))
    along = ((along.astype(jnp.int32) + (CHUNK_POSITIONS - 1)) >> 7).astype(jnp.float32)
    down = jnp.transpose(along)
    same = (lane // half) == (row // half)
    before = same & ((along > down) | ((along == down) & (lane < row)))
    rank = jnp.sum(jnp.where(before, 1.0, 0.0), axis=1, keepdims=True)
    place = rank + ((row // half) * half).astype(jnp.float32)
    at = place == lane.astype(jnp.float32)
    order = jnp.sum(jnp.where(at, row.astype(jnp.float32), 0.0), axis=0, keepdims=True)
    chunks = jnp.sum(jnp.where(at, down, 0.0), axis=0, keepdims=True)
    order_ref[0:1, :] = order.astype(jnp.int32)
    order_ref[1:2, :] = chunks.astype(jnp.int32)


def build_table(me, page_request_home, lengths):
    per_dev = page_request_home.shape[0]
    requests = lengths.shape[0]
    return pl.pallas_call(
        functools.partial(table_kernel, per_dev, requests),
        out_shape=(
            jax.ShapeDtypeStruct((per_dev // 128, 128), jnp.int32),
            jax.ShapeDtypeStruct((2, 128), jnp.int32),
        ),
        in_specs=[SMEM, VMEM, VMEM],
        out_specs=(VMEM, VMEM),
        scratch_shapes=[pltpu.VMEM((1, 128), jnp.float32)],
        compiler_params=params(),
        cost_estimate=SMALL,
        name="page_table",
    )(me, page_request_home.reshape(per_dev // 128, 128), lengths.reshape(1, requests))


def attend_kernel(
    req_count,
    per_dev,
    base,
    requests,
    unroll,
    priorities,
    order_ref,
    lengths_ref,
    table_in,
    q_ref,
    new_ref,
    pages,
    inbox,
    out_ref,
    table,
    labels_v,
    labels_w,
    labels_s,
    buf,
    acc,
    sem,
    sems,
):
    heads_kv = pages.shape[2]
    page_size = PAGE_LENGTH * heads_kv * 2
    chunk_size = CHUNK_PAGES * page_size
    new_rows = STEP_COUNT * heads_kv * 2
    new_group = 128 // new_rows
    half = STEP_COUNT * GROUP
    rows = heads_kv * half
    heads = heads_kv * GROUP
    scale = math.log2(math.e) / math.sqrt(HEAD_WIDTH)
    pairs = PAGE_LENGTH * heads_kv
    page_rows = pages.reshape(per_dev, pairs, 2, HEAD_WIDTH)
    inbox_rows = inbox.reshape(req_count, BLOCK * heads_kv, 2, HEAD_WIDTH)

    tab = pltpu.make_async_copy(table_in, table, sem)
    tab.start()
    tab.wait()
    first = pltpu.make_async_copy(inbox.at[:, pl.ds(BLOCK - 1, 1)], labels_v, sem)
    first.start()
    first.wait()
    row = lax.broadcasted_iota(jnp.int32, (2, 128), 0)
    weight = jnp.where(row == 0, float(DIGIT), 1.0)
    for d in range(req_count):
        digits = labels_v[d, 0, 0, :, :].astype(jnp.float32) * weight
        labels_w[d : d + 1, :] = jnp.sum(digits, axis=0, keepdims=True).astype(jnp.int32)
    back = pltpu.make_async_copy(labels_w, labels_s, sem)
    back.start()
    back.wait()
    for d in range(req_count):
        for k in range(CAP):
            slot = labels_s[d, LABEL_LANE + k]

            @pl.when(slot >= 0)
            def _():
                table[lax.shift_right_logical(slot, 7), slot & 127] = per_dev + d * CAP + k

    slots = BUFFERS // unroll
    steps = requests // unroll
    flat = buf.reshape(slots, unroll, MAXP * page_size, HEAD_WIDTH)

    def fetch(step):
        place = lax.rem(step, slots)
        count = order_ref[1, base + step * unroll]
        for u in range(unroll):
            slot = order_ref[0, base + step * unroll + u] * MAXP
            line = lax.shift_right_logical(slot, 7)
            at = slot & 127

            @pl.loop(0, count)
            def _(c):
                sources = [table[line, at + c * CHUNK_PAGES + j] for j in range(CHUNK_PAGES)]
                most = functools.reduce(jnp.maximum, sources)

                def target(j):
                    return buf.at[place, u, pl.ds((c * CHUNK_PAGES + j) * pairs, pairs)]

                @pl.when(most < per_dev)
                def _():
                    for j in range(CHUNK_PAGES):
                        pltpu.make_async_copy(page_rows.at[sources[j]], target(j), sems.at[place, u]).start(
                            priority=j % priorities
                        )

                @pl.when(most >= per_dev)
                def _():
                    for j in range(CHUNK_PAGES):
                        source = sources[j]

                        @pl.when(source < per_dev)
                        def _():
                            pltpu.make_async_copy(page_rows.at[source], target(j), sems.at[place, u]).start()

                        @pl.when(source >= per_dev)
                        def _():
                            e = source - per_dev
                            d = lax.shift_right_logical(e, 1)
                            k = e - d * CAP
                            pltpu.make_async_copy(
                                inbox_rows.at[d, pl.ds(k * pairs, pairs)], target(j), sems.at[place, u]
                            ).start()

    for s in range(min(slots - 1, steps)):
        fetch(jnp.int32(s))

    def compute(step, n):
        place = lax.rem(step, slots)
        width = n * chunk_size
        for u in range(unroll):
            whole = buf.at[place, u, pl.ds(0, width // 2)]
            pltpu.make_async_copy(whole, whole, sems.at[place, u]).wait()
        column = lax.broadcasted_iota(jnp.int32, (1, width), 1)
        new_column = lax.broadcasted_iota(jnp.int32, (half, 128), 1)
        new_row = lax.broadcasted_iota(jnp.int32, (half, 128), 0)
        new_step = (new_column & (new_rows - 1)) // (2 * heads_kv)
        new_key = new_column & (2 * heads_kv - 1)
        visible = new_step <= (new_row & (STEP_COUNT - 1))
        for u in range(unroll):
            r = order_ref[0, base + step * unroll + u]
            length = lengths_ref[r]
            q = q_ref[pl.ds(pl.multiple_of(r * rows, rows), rows), :]
            kv = flat[place, u, 0:width, :]
            group = r // new_group
            new = new_ref[pl.ds(pl.multiple_of(group * 128, 128), 128), :]
            seen = visible & (new_column // new_rows == r - group * new_group)
            cached = column < 2 * heads_kv * length
            whole_s = dot(q, kv, ((1,), (1,)))
            whole_sn = dot(q, new, ((1,), (1,)))
            ps, pns = [], []
            for g in range(heads_kv):
                key = (column & (2 * heads_kv - 1)) == 2 * g
                bias = jnp.where(cached & key, 0.0, -jnp.inf)
                s = whole_s[g * half : (g + 1) * half] * scale + bias
                sn = whole_sn[g * half : (g + 1) * half] * scale
                sn = jnp.where(seen & (new_key == 2 * g), sn, -jnp.inf)
                top = jnp.maximum(jnp.max(s, axis=1, keepdims=True), jnp.max(sn, axis=1, keepdims=True))
                w = jnp.exp2(s - top)
                wn = jnp.exp2(sn - top)
                inverse = 1.0 / (jnp.sum(w, axis=1, keepdims=True) + jnp.sum(wn, axis=1, keepdims=True))
                ps.append(pltpu.roll(w * inverse, 1, 1).astype(jnp.bfloat16))
                pns.append(pltpu.roll(wn * inverse, 1, 1).astype(jnp.bfloat16))
            o = dot(jnp.concatenate(ps, axis=0), kv) + dot(jnp.concatenate(pns, axis=0), new)
            at = pl.multiple_of((r - base) * STEP_COUNT, STEP_COUNT)
            for h in range(heads):
                acc[h, pl.ds(at, STEP_COUNT), :] = o[h * STEP_COUNT : (h + 1) * STEP_COUNT]

    @pl.loop(0, steps)
    def _(step):
        @pl.when(step + (slots - 1) < steps)
        def _():
            fetch(step + (slots - 1))

        count = order_ref[1, base + step * unroll]
        for n in range(1, CHUNKS + 1):

            @pl.when(count == n)
            def _():
                compute(step, n)

    for h in range(heads):
        out_ref[:, h * HEAD_WIDTH : (h + 1) * HEAD_WIDTH] = acc[h].astype(jnp.bfloat16)


def attend(part, order, lengths, table, q, new, pages, inbox):
    per_dev, _, heads_kv, _, _ = pages.shape
    req_count = inbox.shape[0]
    requests = lengths.shape[0] // HALVES
    heads = heads_kv * GROUP
    extent = MAXP * PAGE_LENGTH * heads_kv * 2
    unroll = UNROLLS[part]
    tokens = requests * STEP_COUNT
    return pl.pallas_call(
        functools.partial(attend_kernel, req_count, per_dev, part * requests, requests, unroll, PRIORITIES[part]),
        out_shape=jax.ShapeDtypeStruct((tokens, heads * HEAD_WIDTH), jnp.bfloat16),
        in_specs=[SMEM, SMEM, HBM, VMEM, VMEM, HBM, HBM],
        out_specs=VMEM,
        scratch_shapes=[
            pltpu.SMEM((per_dev // 128, 128), jnp.int32),
            pltpu.VMEM((req_count, 1, heads_kv, 2, HEAD_WIDTH), jnp.bfloat16),
            pltpu.VMEM((req_count, 128), jnp.int32),
            pltpu.SMEM((req_count, 128), jnp.int32),
            pltpu.VMEM((BUFFERS // unroll, unroll, extent // 2, 2, HEAD_WIDTH), jnp.bfloat16),
            pltpu.VMEM((heads, tokens, HEAD_WIDTH), jnp.float32),
            pltpu.SemaphoreType.DMA,
            pltpu.SemaphoreType.DMA((BUFFERS // unroll, unroll)),
        ],
        compiler_params=params(),
        cost_estimate=pl.CostEstimate(
            flops=16 * tokens * heads * HEAD_WIDTH * MAXP * PAGE_LENGTH,
            bytes_accessed=requests * extent * HEAD_WIDTH * 2,
            transcendentals=2 * tokens * heads * MAXP * PAGE_LENGTH,
        ),
        name="attend",
    )(order, lengths, table, q, new, pages, inbox)


def split_kernel(x_ref, o_ref, sems):
    parts, _, block = o_ref.shape
    copies = [
        pltpu.make_async_copy(x_ref.at[:, pl.ds(i * block, block)], o_ref.at[i], sems.at[i]) for i in range(parts)
    ]
    for copy in copies:
        copy.start()
    for copy in copies:
        copy.wait()


def split_columns(x, parts):
    rows, columns = x.shape
    return pl.pallas_call(
        split_kernel,
        out_shape=jax.ShapeDtypeStruct((parts, rows, columns // parts), x.dtype),
        in_specs=[HBM],
        out_specs=VMEM,
        scratch_shapes=[pltpu.SemaphoreType.DMA((parts,))],
        compiler_params=params(),
        cost_estimate=SMALL,
        name="split_columns",
    )(x)


def project_kernel(count, roles, tile, where_ref, *refs):
    xs, (w_ref, down_ref, mask_ref), rest = refs[:count], refs[count : count + 3], refs[count + 3 :]
    outs, low_ref, x_v = rest[:roles], rest[roles], rest[roles + 1]
    tokens = xs[0].shape[0]
    rows = count * tokens // roles
    for b in range(count):
        x_v[pl.ds(pl.multiple_of(where_ref[b] * tokens, tokens), tokens), :] = xs[b][...]
    low = dot(x_v[...], down_ref[...], ((1,), (1,)))
    for j in range(roles):
        s = where_ref[count + j]
        low_ref[s] = (low[j * rows : (j + 1) * rows] * mask_ref[s].astype(jnp.float32)).astype(jnp.bfloat16)

    @pl.loop(0, w_ref.shape[1] // tile)
    def _(i):
        at = pl.ds(pl.multiple_of(i * tile, tile), tile)
        y = dot(x_v[...], w_ref[:, at]).astype(jnp.bfloat16)
        for j in range(roles):
            outs[j][:, at] = y[j * rows : (j + 1) * rows, :]


def project(where, xs, w, down, mask, roles):
    count = len(xs)
    tokens, width = xs[0].shape
    columns = w.shape[1]
    rows = count * tokens // roles
    return pl.pallas_call(
        functools.partial(project_kernel, count, roles, min(256, columns)),
        out_shape=[jax.ShapeDtypeStruct((rows, columns), jnp.bfloat16)] * roles
        + [jax.ShapeDtypeStruct((roles, rows, down.shape[0]), jnp.bfloat16)],
        in_specs=[SMEM] + [VMEM] * (count + 3),
        out_specs=[VMEM] * (roles + 1),
        scratch_shapes=[pltpu.VMEM((count * tokens, width), jnp.bfloat16)],
        compiler_params=params(),
        cost_estimate=SMALL,
        name="project",
    )(where, *xs, w, down, mask)


def add_kernel(a_ref, b_ref, o_ref):
    o_ref[...] = (a_ref[...].astype(jnp.float32) + b_ref[...].astype(jnp.float32)).astype(jnp.bfloat16)


def add(a, b):
    return pl.pallas_call(
        add_kernel,
        out_shape=jax.ShapeDtypeStruct(a.shape, a.dtype),
        in_specs=[VMEM, VMEM],
        out_specs=VMEM,
        compiler_params=params(),
        cost_estimate=SMALL,
        name="add",
    )(a, b)


def adapt_kernel(low_ref, up_ref, o_ref):
    low = jnp.concatenate([low_ref[a] for a in range(low_ref.shape[0])], axis=1)
    o_ref[...] = dot(low, up_ref[...])


def adapt(low, up):
    return pl.pallas_call(
        adapt_kernel,
        out_shape=jax.ShapeDtypeStruct((low.shape[1], up.shape[1]), jnp.float32),
        in_specs=[VMEM, VMEM],
        out_specs=VMEM,
        compiler_params=params(),
        cost_estimate=SMALL,
        name="adapt",
    )(low, up)


def finish_kernel(counts, cores, extra_ref, *refs):
    terms, o_ref = refs[:-1], refs[-1]
    rows = terms[0].shape[0]
    tokens = rows // cores
    first = 0
    for h, count in enumerate(counts):
        total = extra_ref[h * rows : (h + 1) * rows, :]
        for term in terms[first : first + count]:
            total = total + term[...].astype(jnp.float32)
        first = first + count
        for c in range(cores):
            at = (c * len(counts) + h) * tokens
            o_ref[at : at + tokens, :] = total[c * tokens : (c + 1) * tokens].astype(jnp.bfloat16)


def finish(terms, cores, extra):
    flat = [t for half in terms for t in half]
    return pl.pallas_call(
        functools.partial(finish_kernel, tuple(len(half) for half in terms), cores),
        out_shape=jax.ShapeDtypeStruct(extra.shape, jnp.bfloat16),
        in_specs=[VMEM] * (1 + len(flat)),
        out_specs=VMEM,
        compiler_params=params(),
        cost_estimate=SMALL,
        name="finish",
    )(extra, *flat)


def exchange(x, axis, distance):
    count = lax.axis_size(axis)
    return lax.ppermute(x, axis, [(i, i ^ distance) for i in range(count)])


def after(x, *others):
    return lax.optimization_barrier((x, *others))[0]


def gather(x, gates):
    my_req = lax.axis_index("req").astype(jnp.int32)
    count = lax.axis_size("req")
    if count != 8:
        whole = lax.all_gather(x, "req", axis=0)
        return [whole[b] for b in range(count)], [jnp.int32(b) for b in range(count)], []
    far = [exchange(x, "req", d) for d in (2, 4, 6)]
    held = [x] + [after(block, *gates) for block in far] if gates else [x] + far
    near = [exchange(block, "req", 1) for block in held]
    return held + near, [my_req ^ d for d in (0, 2, 4, 6, 1, 3, 5, 7)], far


def scatter(blocks):
    if len(blocks) != 4:
        return [lax.psum_scatter(jnp.stack(blocks), "tp", scatter_dimension=0, tiled=False)], blocks[0]
    own, one, two, three = blocks
    onward = lax.ppermute(three, "tp", [(0, 1), (3, 2)])
    middle = lax.ppermute(three, "tp", [(1, 2), (2, 1)])
    passed = add(two, onward)
    return [own, exchange(one, "tp", 1), middle, exchange(passed, "tp", 2)], passed


def split_heads(x):
    return x.reshape(*x.shape[:3], -1, HEAD_WIDTH).transpose(0, 1, 3, 2, 4)


def on_device(
    queries,
    incoming_key_value,
    key_value_pages,
    page_request_home,
    lengths,
    request_adapter_index,
    adapter_storage_slot,
    adapter_down_factor,
    adapter_up_factor,
    output_projection_weight,
):
    req_count = lax.axis_size("req")
    tp_count = lax.axis_size("tp")
    my_req = lax.axis_index("req").astype(jnp.int32)
    my_lane = lax.axis_index("tp").astype(jnp.int32)
    me = my_req.reshape(1)
    requests = lengths.shape[0]
    half = requests // HALVES
    columns = key_value_pages.shape[-1]
    heads = columns // HEAD_WIDTH * GROUP
    own_slots, rank, model = adapter_up_factor.shape
    cores = req_count // tp_count

    outbox = pack(me, page_request_home, request_adapter_index, key_value_pages, req_count)
    inbox = lax.all_to_all(outbox, "req", split_axis=0, concat_axis=0, tiled=True)

    table, order = build_table(me, page_request_home, lengths)
    q = queries.reshape(requests, STEP_COUNT, heads, HEAD_WIDTH).transpose(0, 2, 1, 3)
    q = q.reshape(requests * heads * STEP_COUNT, HEAD_WIDTH)
    up_blocks = split_columns(adapter_up_factor.reshape(own_slots * rank, model), req_count)
    new = incoming_key_value.reshape(2, requests * STEP_COUNT, -1, HEAD_WIDTH).transpose(1, 2, 0, 3)
    new = new.reshape(-1, HEAD_WIDTH)
    pages = split_heads(key_value_pages)
    inbox_pages = split_heads(inbox)
    down = adapter_down_factor.transpose(0, 2, 1).reshape(own_slots * rank, -1)

    slot_count = adapter_storage_slot.shape[0]
    ids = inbox[:, BLOCK - 1, 0, :requests].astype(jnp.int32)
    match = ids[:, :, None] == jnp.arange(slot_count, dtype=jnp.int32)
    slot = jnp.sum(jnp.where(match, adapter_storage_slot, 0), axis=2)
    mine = my_req * own_slots + jnp.arange(own_slots * rank, dtype=jnp.int32) // rank

    special = tp_count == 4
    roles = [my_lane ^ j if special else jnp.int32(j) for j in range(tp_count)]
    terms, lows, early, gates = [], [], [], []
    mixed = [attend(h, order, lengths, table, q, new, pages, inbox_pages) for h in range(HALVES)]
    gates = [mixed[-1]]
    for h in range(HALVES):
        blocks, origins, far = gather(after(mixed[h], *early), gates)
        early = far
        where = []
        for origin in origins:
            s = origin // cores
            where.append((s ^ my_lane if special else s) * cores + origin % cores)
        where = jnp.stack(where + roles)
        token_slot = jnp.repeat(slot[:, h * half : (h + 1) * half], STEP_COUNT, axis=1)
        mask = (token_slot.reshape(tp_count, -1)[:, :, None] == mine).astype(jnp.bfloat16)
        if h:
            mask = after(mask, passed)
        *parts, low = project(where, blocks, output_projection_weight, down, mask, tp_count)
        gates = [low]
        lows.append(low)
        sums, passed = scatter(parts)
        terms.append(sums)

    up = lax.all_to_all(after(up_blocks, lows[0]), "req", split_axis=0, concat_axis=0, tiled=True)
    up = up.reshape(req_count * own_slots * rank, -1)
    low = after(jnp.concatenate(lows, axis=1), *terms[0])
    low = lax.all_to_all(low, "tp", split_axis=0, concat_axis=0, tiled=True)
    low = jnp.sum(low.astype(jnp.float32), axis=0).astype(jnp.bfloat16)
    low = after(low, *terms[1][:3])
    low = lax.all_gather(low, "req", axis=0)
    return finish(terms, cores, adapt(low, up))


def solution(mesh):
    return jax.shard_map(
        on_device,
        mesh=mesh,
        in_specs=(
            P("req", "tp"),
            P(None, "req", "tp"),
            P("req", None, None, "tp"),
            P("req"),
            P("req"),
            P("req"),
            P(),
            P("req", "tp", None),
            P("req", None, None),
            P("tp", "req"),
        ),
        out_specs=P("tp", "req"),
        check_vma=False,
    )
```

```python
import functools
import math

import jax
import jax.numpy as jnp
from jax import lax
from jax.experimental import pallas as pl
from jax.experimental.pallas import tpu as pltpu
from jax.sharding import PartitionSpec as P

QUERY_HEADS = 64
KEY_VALUE_HEADS = 8
GROUP = QUERY_HEADS // KEY_VALUE_HEADS
HEAD_WIDTH = 128
STEP_COUNT = 4
PAGE_LENGTH = 32
MAXP = 16
CAP = 2
BLOCK = CAP * PAGE_LENGTH + 1
LABEL_LANE = 64
DIGIT = 16
CHUNK_PAGES = 4
CHUNKS = MAXP // CHUNK_PAGES
CHUNK_POSITIONS = CHUNK_PAGES * PAGE_LENGTH
UNROLL = 4
STAGE_PARTS = 8
HALVES = 2
VMEM_LIMIT = 24 * 1024 * 1024
WHOLE_VMEM = 60 * 1024 * 1024

SMALL = pl.CostEstimate(flops=1, bytes_accessed=1, transcendentals=0)

ANY = pl.BlockSpec(memory_space=pl.ANY)
HBM = pl.BlockSpec(memory_space=pltpu.HBM)
VMEM = pl.BlockSpec(memory_space=pltpu.VMEM)
SMEM = pl.BlockSpec(memory_space=pltpu.SMEM)


def params(limit=VMEM_LIMIT):
    return pltpu.CompilerParams(vmem_limit_bytes=limit)


def dot(a, b, contract=((1,), (0,))):
    return lax.dot_general(a, b, (contract, ((), ())), preferred_element_type=jnp.float32)


def pack_kernel(req_count, per_dev, me_ref, home_ref, ids_ref, pages, outbox, info_v, info_s, ids_v, rows_v, sem, sems):
    me = me_ref[0]
    page = lax.broadcasted_iota(jnp.int32, (req_count, per_dev), 1)
    want = lax.broadcasted_iota(jnp.int32, (req_count, per_dev), 0)
    slots = jnp.broadcast_to(home_ref[...], (req_count, per_dev)) - want * per_dev
    hit = (slots >= 0) & (slots < per_dev) & (want != me)
    lane = lax.broadcasted_iota(jnp.int32, (req_count, 128), 1)
    info = jnp.full((req_count, 128), -1, jnp.int32)
    for k in range(CAP):
        first = jnp.min(jnp.where(hit, page, per_dev), axis=1, keepdims=True)
        here = hit & (page == first)
        slot = jnp.max(jnp.where(here, slots, -1), axis=1, keepdims=True)
        info = jnp.where(lane == k, first, info)
        info = jnp.where(lane == CAP + k, slot, info)
        hit = hit & (page != first)
    info_v[...] = info
    fetch = pltpu.make_async_copy(info_v, info_s, sem)
    fetch.start()
    ids_v[...] = jnp.zeros_like(ids_v)
    ids_v[:, 0:ids_ref.shape[1]] = ids_ref[...].astype(jnp.float32)
    ids = jnp.broadcast_to(ids_v[...], (2, 128))
    fetch.wait()

    def copy(d, k):
        return pltpu.make_async_copy(
            pages.at[info_s[d, k]],
            outbox.at[d, pl.ds(k * PAGE_LENGTH, PAGE_LENGTH)],
            sems.at[d, k],
        )

    for d in range(req_count):
        for k in range(CAP):

            @pl.when(info_s[d, k] < per_dev)
            def _():
                copy(d, k).start()

    at = lax.broadcasted_iota(jnp.int32, (2, 128), 1)
    row = lax.broadcasted_iota(jnp.int32, (2, 128), 0)
    for d in range(req_count):
        value = jnp.where(row == 0, ids, 0.0)
        for k in range(CAP):
            slot = info_s[d, CAP + k]
            high = ((slot + DIGIT) >> 4) - 1
            low = slot - high * DIGIT
            digit = jnp.where(row == 0, high, low).astype(jnp.float32)
            value = jnp.where(at == LABEL_LANE + k, digit, value)
        rows_v[d, 0, :, :] = jnp.zeros(rows_v.shape[2:], jnp.bfloat16)
        rows_v[d, 0, :, 0:128] = value.astype(jnp.bfloat16)
    rows = pltpu.make_async_copy(rows_v, outbox.at[:, pl.ds(BLOCK - 1, 1)], sem)
    rows.start()
    rows.wait()
    for d in range(req_count):
        for k in range(CAP):

            @pl.when(info_s[d, k] < per_dev)
            def _():
                copy(d, k).wait()


def pack(me, page_request_home, ids, key_value_pages, req_count):
    per_dev = key_value_pages.shape[0]
    columns = key_value_pages.shape[-1]
    return pl.pallas_call(
        functools.partial(pack_kernel, req_count, per_dev),
        out_shape=jax.ShapeDtypeStruct((req_count, BLOCK, 2, columns), jnp.bfloat16),
        in_specs=[SMEM, VMEM, VMEM, HBM],
        out_specs=VMEM,
        scratch_shapes=[
            pltpu.VMEM((req_count, 128), jnp.int32),
            pltpu.SMEM((req_count, 128), jnp.int32),
            pltpu.VMEM((1, 128), jnp.float32),
            pltpu.VMEM((req_count, 1, 2, columns), jnp.bfloat16),
            pltpu.SemaphoreType.DMA,
            pltpu.SemaphoreType.DMA((req_count, CAP)),
        ],
        compiler_params=params(WHOLE_VMEM),
        cost_estimate=SMALL,
        name="pack_outbox",
    )(me, page_request_home.reshape(1, per_dev), ids.reshape(1, -1), key_value_pages)


def table_kernel(per_dev, requests, me_ref, home_ref, lengths_ref, table_ref, order_ref, len_v):
    base = me_ref[0] * per_dev
    lane = lax.broadcasted_iota(jnp.int32, (128, 128), 1)
    row = lax.broadcasted_iota(jnp.int32, (128, 128), 0)
    tiles = per_dev // 128
    columns = [
        jnp.transpose(jnp.broadcast_to(home_ref[i : i + 1, :] - base, (128, 128)).astype(jnp.float32))
        for i in range(tiles)
    ]
    for j in range(tiles):
        total = jnp.zeros((128, 128), jnp.float32)
        slot = (lane + j * 128).astype(jnp.float32)
        for i in range(tiles):
            total = total + jnp.where(columns[i] == slot, (row + i * 128).astype(jnp.float32), 0.0)
        table_ref[j : j + 1, :] = jnp.sum(total, axis=0, keepdims=True).astype(jnp.int32)
    half = requests // HALVES
    len_v[...] = jnp.zeros_like(len_v)
    len_v[:, 0:requests] = lengths_ref[...].astype(jnp.float32)
    along = jnp.broadcast_to(len_v[...], (128, 128))
    along = ((along.astype(jnp.int32) + (CHUNK_POSITIONS - 1)) >> 7).astype(jnp.float32)
    down = jnp.transpose(along)
    same = (lane // half) == (row // half)
    before = same & ((along > down) | ((along == down) & (lane < row)))
    rank = jnp.sum(jnp.where(before, 1.0, 0.0), axis=1, keepdims=True)
    place = rank + ((row // half) * half).astype(jnp.float32)
    at = place == lane.astype(jnp.float32)
    order = jnp.sum(jnp.where(at, row.astype(jnp.float32), 0.0), axis=0, keepdims=True)
    chunks = jnp.sum(jnp.where(at, down, 0.0), axis=0, keepdims=True)
    order_ref[0:1, :] = order.astype(jnp.int32)
    order_ref[1:2, :] = chunks.astype(jnp.int32)


def build_table(me, page_request_home, lengths):
    per_dev = page_request_home.shape[0]
    requests = lengths.shape[0]
    return pl.pallas_call(
        functools.partial(table_kernel, per_dev, requests),
        out_shape=(
            jax.ShapeDtypeStruct((per_dev // 128, 128), jnp.int32),
            jax.ShapeDtypeStruct((2, 128), jnp.int32),
        ),
        in_specs=[SMEM, VMEM, VMEM],
        out_specs=(VMEM, VMEM),
        scratch_shapes=[pltpu.VMEM((1, 128), jnp.float32)],
        compiler_params=params(),
        cost_estimate=SMALL,
        name="page_table",
    )(me, page_request_home.reshape(per_dev // 128, 128), lengths.reshape(1, requests))


def stage_kernel(x_ref, o_ref, sems):
    step = x_ref.shape[0] // STAGE_PARTS
    copies = []
    for i in range(STAGE_PARTS):
        at = pl.ds(i * step, step)
        copies.append(pltpu.make_async_copy(x_ref.at[at], o_ref.at[at], sems.at[i]))
    for copy in copies:
        copy.start()
    for copy in copies:
        copy.wait()


def stage(pages):
    return pl.pallas_call(
        stage_kernel,
        out_shape=jax.ShapeDtypeStruct(pages.shape, pages.dtype),
        in_specs=[HBM],
        out_specs=VMEM,
        scratch_shapes=[pltpu.SemaphoreType.DMA((STAGE_PARTS,))],
        compiler_params=params(),
        cost_estimate=pl.CostEstimate(flops=0, bytes_accessed=2 * pages.size * 2, transcendentals=0),
        name="stage",
    )(pages)


def attend_kernel(
    req_count,
    per_dev,
    base,
    requests,
    order_ref,
    lengths_ref,
    table_in,
    q_ref,
    new_ref,
    pages,
    inbox,
    out_ref,
    table,
    labels_w,
    labels_s,
    buf,
    acc,
    sem,
):
    heads_kv = pages.shape[2]
    page_size = PAGE_LENGTH * heads_kv * 2
    chunk_size = CHUNK_PAGES * page_size
    new_rows = STEP_COUNT * heads_kv * 2
    new_group = 128 // new_rows
    half = STEP_COUNT * GROUP
    rows = heads_kv * half
    heads = heads_kv * GROUP
    scale = math.log2(math.e) / math.sqrt(HEAD_WIDTH)
    page_rows = pages.reshape(per_dev, page_size, HEAD_WIDTH)
    inbox_rows = inbox.reshape(req_count, BLOCK * heads_kv * 2, HEAD_WIDTH)

    tab = pltpu.make_async_copy(table_in, table, sem)
    tab.start()
    tab.wait()
    row = lax.broadcasted_iota(jnp.int32, (2, 128), 0)
    weight = jnp.where(row == 0, float(DIGIT), 1.0)
    for d in range(req_count):
        digits = inbox[d, BLOCK - 1, 0, :, :].astype(jnp.float32) * weight
        labels_w[d : d + 1, :] = jnp.sum(digits, axis=0, keepdims=True).astype(jnp.int32)
    back = pltpu.make_async_copy(labels_w, labels_s, sem)
    back.start()
    back.wait()
    for d in range(req_count):
        for k in range(CAP):
            slot = labels_s[d, LABEL_LANE + k]

            @pl.when(slot >= 0)
            def _():
                table[lax.shift_right_logical(slot, 7), slot & 127] = per_dev + d * CAP + k

    steps = requests // UNROLL

    def fetch(step):
        count = order_ref[1, base + step * UNROLL]
        for u in range(UNROLL):
            slot = order_ref[0, base + step * UNROLL + u] * MAXP
            line = lax.shift_right_logical(slot, 7)
            at = slot & 127

            @pl.loop(0, count)
            def _(c):
                sources = [table[line, at + c * CHUNK_PAGES + j] for j in range(CHUNK_PAGES)]
                most = functools.reduce(jnp.maximum, sources)

                def put(j, page):
                    start = pl.multiple_of(c * chunk_size + j * page_size, page_size)
                    buf[u, pl.ds(start, page_size), :] = page

                @pl.when(most < per_dev)
                def _():
                    for j in range(CHUNK_PAGES):
                        put(j, page_rows[sources[j]])

                @pl.when(most >= per_dev)
                def _():
                    for j in range(CHUNK_PAGES):
                        source = sources[j]

                        @pl.when(source < per_dev)
                        def _():
                            put(j, page_rows[source])

                        @pl.when(source >= per_dev)
                        def _():
                            e = source - per_dev
                            d = lax.shift_right_logical(e, 1)
                            k = e - d * CAP

                            @pl.when(k == 0)
                            def _():
                                put(j, inbox_rows[d, 0:page_size])

                            @pl.when(k == 1)
                            def _():
                                put(j, inbox_rows[d, page_size : 2 * page_size])

    def compute(step, n):
        width = n * chunk_size
        column = lax.broadcasted_iota(jnp.int32, (1, width), 1)
        new_column = lax.broadcasted_iota(jnp.int32, (half, 128), 1)
        new_row = lax.broadcasted_iota(jnp.int32, (half, 128), 0)
        new_step = (new_column & (new_rows - 1)) // (2 * heads_kv)
        new_key = new_column & (2 * heads_kv - 1)
        visible = new_step <= (new_row & (STEP_COUNT - 1))
        for u in range(UNROLL):
            r = order_ref[0, base + step * UNROLL + u]
            length = lengths_ref[r]
            q = q_ref[pl.ds(pl.multiple_of(r * rows, rows), rows), :]
            kv = buf[u, 0:width, :]
            group = r // new_group
            new = new_ref[pl.ds(pl.multiple_of(group * 128, 128), 128), :]
            seen = visible & (new_column // new_rows == r - group * new_group)
            cached = column < 2 * heads_kv * length
            whole_s = dot(q, kv, ((1,), (1,)))
            whole_sn = dot(q, new, ((1,), (1,)))
            ps, pns = [], []
            for g in range(heads_kv):
                key = (column & (2 * heads_kv - 1)) == 2 * g
                bias = jnp.where(cached & key, 0.0, -jnp.inf)
                s = whole_s[g * half : (g + 1) * half] * scale + bias
                sn = whole_sn[g * half : (g + 1) * half] * scale
                sn = jnp.where(seen & (new_key == 2 * g), sn, -jnp.inf)
                top = jnp.maximum(jnp.max(s, axis=1, keepdims=True), jnp.max(sn, axis=1, keepdims=True))
                w = jnp.exp2(s - top)
                wn = jnp.exp2(sn - top)
                inverse = 1.0 / (jnp.sum(w, axis=1, keepdims=True) + jnp.sum(wn, axis=1, keepdims=True))
                ps.append(pltpu.roll(w * inverse, 1, 1).astype(jnp.bfloat16))
                pns.append(pltpu.roll(wn * inverse, 1, 1).astype(jnp.bfloat16))
            o = dot(jnp.concatenate(ps, axis=0), kv) + dot(jnp.concatenate(pns, axis=0), new)
            at = pl.multiple_of((r - base) * STEP_COUNT, STEP_COUNT)
            for h in range(heads):
                acc[h, pl.ds(at, STEP_COUNT), :] = o[h * STEP_COUNT : (h + 1) * STEP_COUNT]

    @pl.loop(0, steps)
    def _(step):
        fetch(step)
        count = order_ref[1, base + step * UNROLL]
        for n in range(1, CHUNKS + 1):

            @pl.when(count == n)
            def _():
                compute(step, n)

    for h in range(heads):
        out_ref[:, h * HEAD_WIDTH : (h + 1) * HEAD_WIDTH] = acc[h].astype(jnp.bfloat16)


def attend(part, order, lengths, table, q, new, pages, inbox):
    per_dev, _, heads_kv, _, _ = pages.shape
    req_count = inbox.shape[0]
    requests = lengths.shape[0] // HALVES
    heads = heads_kv * GROUP
    extent = MAXP * PAGE_LENGTH * heads_kv * 2
    tokens = requests * STEP_COUNT
    return pl.pallas_call(
        functools.partial(attend_kernel, req_count, per_dev, part * requests, requests),
        out_shape=jax.ShapeDtypeStruct((tokens, heads * HEAD_WIDTH), jnp.bfloat16),
        in_specs=[SMEM, SMEM, ANY, VMEM, VMEM, VMEM, VMEM],
        out_specs=VMEM,
        scratch_shapes=[
            pltpu.SMEM((per_dev // 128, 128), jnp.int32),
            pltpu.VMEM((req_count, 128), jnp.int32),
            pltpu.SMEM((req_count, 128), jnp.int32),
            pltpu.VMEM((UNROLL, extent, HEAD_WIDTH), jnp.bfloat16),
            pltpu.VMEM((heads, tokens, HEAD_WIDTH), jnp.float32),
            pltpu.SemaphoreType.DMA,
        ],
        compiler_params=params(),
        cost_estimate=pl.CostEstimate(
            flops=16 * tokens * heads * HEAD_WIDTH * MAXP * PAGE_LENGTH,
            bytes_accessed=requests * extent * HEAD_WIDTH * 2,
            transcendentals=2 * tokens * heads * MAXP * PAGE_LENGTH,
        ),
        name="attend",
    )(order, lengths, table, q, new, pages, inbox)


def split_kernel(x_ref, o_ref, sems):
    parts, _, block = o_ref.shape
    copies = [
        pltpu.make_async_copy(x_ref.at[:, pl.ds(i * block, block)], o_ref.at[i], sems.at[i]) for i in range(parts)
    ]
    for copy in copies:
        copy.start()
    for copy in copies:
        copy.wait()


def split_columns(x, parts):
    rows, columns = x.shape
    return pl.pallas_call(
        split_kernel,
        out_shape=jax.ShapeDtypeStruct((parts, rows, columns // parts), x.dtype),
        in_specs=[HBM],
        out_specs=VMEM,
        scratch_shapes=[pltpu.SemaphoreType.DMA((parts,))],
        compiler_params=params(),
        cost_estimate=SMALL,
        name="split_columns",
    )(x)


def project_kernel(count, roles, tile, where_ref, *refs):
    xs, (w_ref, down_ref, mask_ref), rest = refs[:count], refs[count : count + 3], refs[count + 3 :]
    outs, low_ref, x_v = rest[:roles], rest[roles], rest[roles + 1]
    tokens = xs[0].shape[0]
    rows = count * tokens // roles
    for b in range(count):
        x_v[pl.ds(pl.multiple_of(where_ref[b] * tokens, tokens), tokens), :] = xs[b][...]
    low = dot(x_v[...], down_ref[...], ((1,), (1,)))
    for j in range(roles):
        s = where_ref[count + j]
        low_ref[s] = (low[j * rows : (j + 1) * rows] * mask_ref[s].astype(jnp.float32)).astype(jnp.bfloat16)

    @pl.loop(0, w_ref.shape[1] // tile)
    def _(i):
        at = pl.ds(pl.multiple_of(i * tile, tile), tile)
        y = dot(x_v[...], w_ref[:, at]).astype(jnp.bfloat16)
        for j in range(roles):
            outs[j][:, at] = y[j * rows : (j + 1) * rows, :]


def project(where, xs, w, down, mask, roles):
    count = len(xs)
    tokens, width = xs[0].shape
    columns = w.shape[1]
    rows = count * tokens // roles
    return pl.pallas_call(
        functools.partial(project_kernel, count, roles, min(256, columns)),
        out_shape=[jax.ShapeDtypeStruct((rows, columns), jnp.bfloat16)] * roles
        + [jax.ShapeDtypeStruct((roles, rows, down.shape[0]), jnp.bfloat16)],
        in_specs=[SMEM] + [VMEM] * (count + 3),
        out_specs=[VMEM] * (roles + 1),
        scratch_shapes=[pltpu.VMEM((count * tokens, width), jnp.bfloat16)],
        compiler_params=params(),
        cost_estimate=SMALL,
        name="project",
    )(where, *xs, w, down, mask)


def add_kernel(a_ref, b_ref, o_ref):
    o_ref[...] = (a_ref[...].astype(jnp.float32) + b_ref[...].astype(jnp.float32)).astype(jnp.bfloat16)


def add(a, b):
    return pl.pallas_call(
        add_kernel,
        out_shape=jax.ShapeDtypeStruct(a.shape, a.dtype),
        in_specs=[VMEM, VMEM],
        out_specs=VMEM,
        compiler_params=params(),
        cost_estimate=SMALL,
        name="add",
    )(a, b)


def adapt_kernel(low_ref, up_ref, o_ref):
    low = jnp.concatenate([low_ref[a] for a in range(low_ref.shape[0])], axis=1)
    o_ref[...] = dot(low, up_ref[...])


def adapt(low, up):
    return pl.pallas_call(
        adapt_kernel,
        out_shape=jax.ShapeDtypeStruct((low.shape[1], up.shape[1]), jnp.float32),
        in_specs=[VMEM, VMEM],
        out_specs=VMEM,
        compiler_params=params(),
        cost_estimate=SMALL,
        name="adapt",
    )(low, up)


def finish_kernel(counts, cores, extra_ref, *refs):
    terms, o_ref = refs[:-1], refs[-1]
    rows = terms[0].shape[0]
    tokens = rows // cores
    first = 0
    for h, count in enumerate(counts):
        total = extra_ref[h * rows : (h + 1) * rows, :]
        for term in terms[first : first + count]:
            total = total + term[...].astype(jnp.float32)
        first = first + count
        for c in range(cores):
            at = (c * len(counts) + h) * tokens
            o_ref[at : at + tokens, :] = total[c * tokens : (c + 1) * tokens].astype(jnp.bfloat16)


def finish(terms, cores, extra):
    flat = [t for half in terms for t in half]
    return pl.pallas_call(
        functools.partial(finish_kernel, tuple(len(half) for half in terms), cores),
        out_shape=jax.ShapeDtypeStruct(extra.shape, jnp.bfloat16),
        in_specs=[VMEM] * (1 + len(flat)),
        out_specs=VMEM,
        compiler_params=params(),
        cost_estimate=SMALL,
        name="finish",
    )(extra, *flat)


def exchange(x, axis, distance):
    count = lax.axis_size(axis)
    return lax.ppermute(x, axis, [(i, i ^ distance) for i in range(count)])


def after(x, *others):
    return lax.optimization_barrier((x, *others))[0]


def gather(x, gates):
    my_req = lax.axis_index("req").astype(jnp.int32)
    count = lax.axis_size("req")
    if count != 8:
        whole = lax.all_gather(x, "req", axis=0)
        return [whole[b] for b in range(count)], [jnp.int32(b) for b in range(count)], []
    far = [exchange(x, "req", d) for d in (2, 4, 6)]
    held = [x] + [after(block, *gates) for block in far] if gates else [x] + far
    near = [exchange(block, "req", 1) for block in held]
    return held + near, [my_req ^ d for d in (0, 2, 4, 6, 1, 3, 5, 7)], far


def scatter(blocks):
    if len(blocks) != 4:
        return [lax.psum_scatter(jnp.stack(blocks), "tp", scatter_dimension=0, tiled=False)], blocks[0]
    own, one, two, three = blocks
    onward = lax.ppermute(three, "tp", [(0, 1), (3, 2)])
    middle = lax.ppermute(three, "tp", [(1, 2), (2, 1)])
    passed = add(two, onward)
    return [own, exchange(one, "tp", 1), middle, exchange(passed, "tp", 2)], passed


def split_heads(x):
    return x.reshape(*x.shape[:3], -1, HEAD_WIDTH).transpose(0, 1, 3, 2, 4)


def on_device(
    queries,
    incoming_key_value,
    key_value_pages,
    page_request_home,
    lengths,
    request_adapter_index,
    adapter_storage_slot,
    adapter_down_factor,
    adapter_up_factor,
    output_projection_weight,
):
    req_count = lax.axis_size("req")
    tp_count = lax.axis_size("tp")
    my_req = lax.axis_index("req").astype(jnp.int32)
    my_lane = lax.axis_index("tp").astype(jnp.int32)
    me = my_req.reshape(1)
    requests = lengths.shape[0]
    half = requests // HALVES
    columns = key_value_pages.shape[-1]
    heads = columns // HEAD_WIDTH * GROUP
    own_slots, rank, model = adapter_up_factor.shape
    cores = req_count // tp_count

    outbox = pack(me, page_request_home, request_adapter_index, key_value_pages, req_count)
    inbox = lax.all_to_all(outbox, "req", split_axis=0, concat_axis=0, tiled=True)

    table, order = build_table(me, page_request_home, lengths)
    q = queries.reshape(requests, STEP_COUNT, heads, HEAD_WIDTH).transpose(0, 2, 1, 3)
    q = q.reshape(requests * heads * STEP_COUNT, HEAD_WIDTH)
    up_blocks = split_columns(adapter_up_factor.reshape(own_slots * rank, model), req_count)
    new = incoming_key_value.reshape(2, requests * STEP_COUNT, -1, HEAD_WIDTH).transpose(1, 2, 0, 3)
    new = new.reshape(-1, HEAD_WIDTH)
    pages = stage(split_heads(after(key_value_pages, outbox)))
    inbox_pages = split_heads(inbox)
    down = adapter_down_factor.transpose(0, 2, 1).reshape(own_slots * rank, -1)

    up = lax.all_to_all(up_blocks, "req", split_axis=0, concat_axis=0, tiled=True)
    up = up.reshape(req_count * own_slots * rank, -1)
    slot_count = adapter_storage_slot.shape[0]
    ids = inbox[:, BLOCK - 1, 0, :requests].astype(jnp.int32)
    match = ids[:, :, None] == jnp.arange(slot_count, dtype=jnp.int32)
    slot = jnp.sum(jnp.where(match, adapter_storage_slot, 0), axis=2)
    mine = my_req * own_slots + jnp.arange(own_slots * rank, dtype=jnp.int32) // rank

    special = tp_count == 4
    roles = [my_lane ^ j if special else jnp.int32(j) for j in range(tp_count)]
    terms, lows, early, gates = [], [], [], []
    mixed = [attend(h, order, lengths, table, q, new, pages, inbox_pages) for h in range(HALVES)]
    gates = [mixed[-1]]
    for h in range(HALVES):
        blocks, origins, far = gather(after(mixed[h], *early), gates)
        early = far
        where = []
        for origin in origins:
            s = origin // cores
            where.append((s ^ my_lane if special else s) * cores + origin % cores)
        where = jnp.stack(where + roles)
        token_slot = jnp.repeat(slot[:, h * half : (h + 1) * half], STEP_COUNT, axis=1)
        mask = (token_slot.reshape(tp_count, -1)[:, :, None] == mine).astype(jnp.bfloat16)
        mask = after(mask, *([passed, *terms[0][:3]] if h else [up]))
        *parts, low = project(where, blocks, output_projection_weight, down, mask, tp_count)
        gates = [low]
        lows.append(low)
        sums, passed = scatter(parts)
        terms.append(sums)

    low = after(jnp.concatenate(lows, axis=1), passed, *terms[0])
    low = lax.all_to_all(low, "tp", split_axis=0, concat_axis=0, tiled=True)
    low = jnp.sum(low.astype(jnp.float32), axis=0).astype(jnp.bfloat16)
    low = after(low, *terms[1][:3])
    low = after(lax.all_gather(low, "req", axis=0), *terms[1])
    return finish(terms, cores, adapt(low, up))


def solution(mesh):
    return jax.shard_map(
        on_device,
        mesh=mesh,
        in_specs=(
            P("req", "tp"),
            P(None, "req", "tp"),
            P("req", None, None, "tp"),
            P("req"),
            P("req"),
            P("req"),
            P(),
            P("req", "tp", None),
            P("req", None, None),
            P("tp", "req"),
        ),
        out_specs=P("tp", "req"),
        check_vma=False,
    )
```

```python
import functools
import math

import jax
import jax.numpy as jnp
from jax import lax
from jax.experimental import pallas as pl
from jax.experimental.pallas import tpu as pltpu
from jax.sharding import PartitionSpec as P

QUERY_HEADS = 64
KEY_VALUE_HEADS = 8
GROUP = QUERY_HEADS // KEY_VALUE_HEADS
HEAD_WIDTH = 128
STEP_COUNT = 4
PAGE_LENGTH = 32
MAXP = 16
CAP = 2
BLOCK = CAP * PAGE_LENGTH + 1
LABEL_LANE = 64
DIGIT = 16
CHUNK_PAGES = 4
CHUNKS = MAXP // CHUNK_PAGES
CHUNK_POSITIONS = CHUNK_PAGES * PAGE_LENGTH
LANES = 128
SLOTS = 6
HALVES = 2
VMEM_LIMIT = 24 * 1024 * 1024
WHOLE_VMEM = 60 * 1024 * 1024
ATTEND_VMEM = 48 * 1024 * 1024

SMALL = pl.CostEstimate(flops=1, bytes_accessed=1, transcendentals=0)

ANY = pl.BlockSpec(memory_space=pl.ANY)
HBM = pl.BlockSpec(memory_space=pltpu.HBM)
VMEM = pl.BlockSpec(memory_space=pltpu.VMEM)
SMEM = pl.BlockSpec(memory_space=pltpu.SMEM)


def params(limit=VMEM_LIMIT):
    return pltpu.CompilerParams(vmem_limit_bytes=limit)


def dot(a, b, contract=((1,), (0,))):
    return lax.dot_general(a, b, (contract, ((), ())), preferred_element_type=jnp.float32)


def pack_kernel(req_count, per_dev, me_ref, home_ref, ids_ref, pages, outbox, info_v, info_s, ids_v, rows_v, sem, sems):
    me = me_ref[0]
    page = lax.broadcasted_iota(jnp.int32, (req_count, per_dev), 1)
    want = lax.broadcasted_iota(jnp.int32, (req_count, per_dev), 0)
    slots = jnp.broadcast_to(home_ref[...], (req_count, per_dev)) - want * per_dev
    hit = (slots >= 0) & (slots < per_dev) & (want != me)
    lane = lax.broadcasted_iota(jnp.int32, (req_count, 128), 1)
    info = jnp.full((req_count, 128), -1, jnp.int32)
    for k in range(CAP):
        first = jnp.min(jnp.where(hit, page, per_dev), axis=1, keepdims=True)
        here = hit & (page == first)
        slot = jnp.max(jnp.where(here, slots, -1), axis=1, keepdims=True)
        info = jnp.where(lane == k, first, info)
        info = jnp.where(lane == CAP + k, slot, info)
        hit = hit & (page != first)
    info_v[...] = info
    fetch = pltpu.make_async_copy(info_v, info_s, sem)
    fetch.start()
    ids_v[...] = jnp.zeros_like(ids_v)
    ids_v[:, 0:ids_ref.shape[1]] = ids_ref[...].astype(jnp.float32)
    ids = jnp.broadcast_to(ids_v[...], (2, 128))
    fetch.wait()

    def copy(d, k):
        return pltpu.make_async_copy(
            pages.at[info_s[d, k]],
            outbox.at[d, pl.ds(k * PAGE_LENGTH, PAGE_LENGTH)],
            sems.at[d, k],
        )

    for d in range(req_count):
        for k in range(CAP):

            @pl.when(info_s[d, k] < per_dev)
            def _():
                copy(d, k).start()

    at = lax.broadcasted_iota(jnp.int32, (2, 128), 1)
    row = lax.broadcasted_iota(jnp.int32, (2, 128), 0)
    for d in range(req_count):
        value = jnp.where(row == 0, ids, 0.0)
        for k in range(CAP):
            slot = info_s[d, CAP + k]
            high = ((slot + DIGIT) >> 4) - 1
            low = slot - high * DIGIT
            digit = jnp.where(row == 0, high, low).astype(jnp.float32)
            value = jnp.where(at == LABEL_LANE + k, digit, value)
        rows_v[d, 0, :, :] = jnp.zeros(rows_v.shape[2:], jnp.bfloat16)
        rows_v[d, 0, :, 0:128] = value.astype(jnp.bfloat16)
    rows = pltpu.make_async_copy(rows_v, outbox.at[:, pl.ds(BLOCK - 1, 1)], sem)
    rows.start()
    rows.wait()
    for d in range(req_count):
        for k in range(CAP):

            @pl.when(info_s[d, k] < per_dev)
            def _():
                copy(d, k).wait()


def pack(me, page_request_home, ids, key_value_pages, req_count):
    per_dev = key_value_pages.shape[0]
    columns = key_value_pages.shape[-1]
    return pl.pallas_call(
        functools.partial(pack_kernel, req_count, per_dev),
        out_shape=jax.ShapeDtypeStruct((req_count, BLOCK, 2, columns), jnp.bfloat16),
        in_specs=[SMEM, VMEM, VMEM, HBM],
        out_specs=VMEM,
        scratch_shapes=[
            pltpu.VMEM((req_count, 128), jnp.int32),
            pltpu.SMEM((req_count, 128), jnp.int32),
            pltpu.VMEM((1, 128), jnp.float32),
            pltpu.VMEM((req_count, 1, 2, columns), jnp.bfloat16),
            pltpu.SemaphoreType.DMA,
            pltpu.SemaphoreType.DMA((req_count, CAP)),
        ],
        compiler_params=params(WHOLE_VMEM),
        cost_estimate=SMALL,
        name="pack_outbox",
    )(me, page_request_home.reshape(1, per_dev), ids.reshape(1, -1), key_value_pages)


def table_kernel(per_dev, requests, pack_size, me_ref, home_ref, lengths_ref, table_ref, order_ref, len_v):
    base = me_ref[0] * per_dev
    lane = lax.broadcasted_iota(jnp.int32, (128, 128), 1)
    row = lax.broadcasted_iota(jnp.int32, (128, 128), 0)
    tiles = per_dev // 128
    columns = [
        jnp.transpose(jnp.broadcast_to(home_ref[i : i + 1, :] - base, (128, 128)).astype(jnp.float32))
        for i in range(tiles)
    ]
    for j in range(tiles):
        total = jnp.zeros((128, 128), jnp.float32)
        slot = (lane + j * 128).astype(jnp.float32)
        for i in range(tiles):
            total = total + jnp.where(columns[i] == slot, (row + i * 128).astype(jnp.float32), 0.0)
        table_ref[j : j + 1, :] = jnp.sum(total, axis=0, keepdims=True).astype(jnp.int32)
    half = requests // HALVES
    len_v[...] = jnp.zeros_like(len_v)
    len_v[:, 0:requests] = lengths_ref[...].astype(jnp.float32)
    along = jnp.broadcast_to(len_v[...], (128, 128))
    along = ((along.astype(jnp.int32) + (CHUNK_POSITIONS - 1)) >> 7).astype(jnp.float32)
    down = jnp.transpose(along)
    same = ((lane // half) == (row // half)) & (lane % pack_size == row % pack_size)
    before = same & ((along > down) | ((along == down) & (lane < row)))
    rank = jnp.sum(jnp.where(before, 1.0, 0.0), axis=1, keepdims=True)
    place = rank * pack_size + ((row // half) * half + row % pack_size).astype(jnp.float32)
    at = place == lane.astype(jnp.float32)
    order = jnp.sum(jnp.where(at, row.astype(jnp.float32), 0.0), axis=0, keepdims=True)
    chunks = jnp.sum(jnp.where(at, down, 0.0), axis=0, keepdims=True)
    order_ref[0:1, :] = order.astype(jnp.int32)
    order_ref[1:2, :] = chunks.astype(jnp.int32)


def build_table(me, page_request_home, lengths, pack_size):
    per_dev = page_request_home.shape[0]
    requests = lengths.shape[0]
    return pl.pallas_call(
        functools.partial(table_kernel, per_dev, requests, pack_size),
        out_shape=(
            jax.ShapeDtypeStruct((per_dev // 128, 128), jnp.int32),
            jax.ShapeDtypeStruct((2, 128), jnp.int32),
        ),
        in_specs=[SMEM, VMEM, VMEM],
        out_specs=(VMEM, VMEM),
        scratch_shapes=[pltpu.VMEM((1, 128), jnp.float32)],
        compiler_params=params(),
        cost_estimate=SMALL,
        name="page_table",
    )(me, page_request_home.reshape(per_dev // 128, 128), lengths.reshape(1, requests))


def attend_kernel(
    req_count,
    per_dev,
    base,
    requests,
    order_ref,
    lengths_ref,
    table_in,
    q_ref,
    new_ref,
    pages,
    inbox,
    out_ref,
    table,
    labels_v,
    labels_w,
    labels_s,
    buf,
    acc,
    sem,
    sems,
):
    columns = pages.shape[-1]
    heads_kv = columns // HEAD_WIDTH
    heads = heads_kv * GROUP
    span = STEP_COUNT * heads
    pack_size = LANES // span
    page_size = PAGE_LENGTH * 2
    chunk_size = CHUNK_PAGES * page_size
    new_rows = STEP_COUNT * 2
    tokens = requests * STEP_COUNT
    scale = math.log2(math.e) / math.sqrt(HEAD_WIDTH)
    page_rows = pages.reshape(per_dev, page_size, columns)
    inbox_rows = inbox.reshape(req_count, BLOCK * 2, columns)

    tab = pltpu.make_async_copy(table_in, table, sem)
    tab.start()
    tab.wait()
    first = pltpu.make_async_copy(inbox.at[:, pl.ds(BLOCK - 1, 1)], labels_v, sem)
    first.start()
    first.wait()
    row = lax.broadcasted_iota(jnp.int32, (2, 128), 0)
    weight = jnp.where(row == 0, float(DIGIT), 1.0)
    for d in range(req_count):
        digits = labels_v[d, 0, :, 0:128].astype(jnp.float32) * weight
        labels_w[d : d + 1, :] = jnp.sum(digits, axis=0, keepdims=True).astype(jnp.int32)
    back = pltpu.make_async_copy(labels_w, labels_s, sem)
    back.start()
    back.wait()
    for d in range(req_count):
        for k in range(CAP):
            slot = labels_s[d, LABEL_LANE + k]

            @pl.when(slot >= 0)
            def _():
                table[lax.shift_right_logical(slot, 7), slot & 127] = per_dev + d * CAP + k

    steps = requests // pack_size

    def most_chunks(step):
        counts = [order_ref[1, base + step * pack_size + u] for u in range(pack_size)]
        return functools.reduce(jnp.maximum, counts)

    def fetch(step):
        place = lax.rem(step, SLOTS)
        count = most_chunks(step)
        for u in range(pack_size):
            slot = order_ref[0, base + step * pack_size + u] * MAXP
            line = lax.shift_right_logical(slot, 7)
            at = slot & 127

            @pl.loop(0, count)
            def _(c):
                sources = [table[line, at + c * CHUNK_PAGES + j] for j in range(CHUNK_PAGES)]
                most = functools.reduce(jnp.maximum, sources)

                def target(j):
                    start = pl.multiple_of(c * chunk_size + j * page_size, page_size)
                    return buf.at[place, u, pl.ds(start, page_size)]

                @pl.when(most < per_dev)
                def _():
                    for j in range(CHUNK_PAGES):
                        pltpu.make_async_copy(page_rows.at[sources[j]], target(j), sems.at[place, u]).start()

                @pl.when(most >= per_dev)
                def _():
                    for j in range(CHUNK_PAGES):
                        source = sources[j]

                        @pl.when(source < per_dev)
                        def _():
                            pltpu.make_async_copy(page_rows.at[source], target(j), sems.at[place, u]).start()

                        @pl.when(source >= per_dev)
                        def _():
                            e = source - per_dev
                            d = lax.shift_right_logical(e, 1)
                            start = pl.multiple_of((e - d * CAP) * page_size, page_size)
                            pltpu.make_async_copy(
                                inbox_rows.at[d, pl.ds(start, page_size)], target(j), sems.at[place, u]
                            ).start()

    for s in range(min(SLOTS - 1, steps)):
        fetch(jnp.int32(s))

    def compute(step, n):
        place = lax.rem(step, SLOTS)
        width = n * chunk_size
        for u in range(pack_size):
            whole = buf.at[place, u, pl.ds(0, width)]
            pltpu.make_async_copy(whole, whole, sems.at[place, u]).wait()
        lane = lax.broadcasted_iota(jnp.int32, (HEAD_WIDTH, LANES), 1)
        part = lane // span
        lane_head = (lane % heads) // GROUP
        one = lax.broadcasted_iota(jnp.int32, (1, LANES), 1)
        limit = jnp.zeros((1, LANES), jnp.int32)
        owner = jnp.zeros((1, LANES), jnp.int32)
        rows, kvs, rights = [], [], []
        for u in range(pack_size):
            r = order_ref[0, base + step * pack_size + u]
            rows.append(r)
            q = q_ref[:, pl.ds(pl.multiple_of((r // pack_size) * LANES, LANES), LANES)].astype(jnp.float32)
            own = part == u
            rights.append(
                jnp.concatenate(
                    [jnp.where(own & (lane_head == g), q, 0.0).astype(jnp.bfloat16) for g in range(heads_kv)], axis=0
                )
            )
            kvs.append(buf[place, u, 0:width, :])
            limit = jnp.where(one // span == u, 2 * lengths_ref[r], limit)
            owner = jnp.where(one // span == u, r - base, owner)
        new = new_ref[base * new_rows : (base + requests) * new_rows, :]
        s = dot(jnp.concatenate(kvs, axis=1), jnp.concatenate(rights, axis=0))
        sn = dot(new, functools.reduce(jnp.add, rights))
        row = lax.broadcasted_iota(jnp.int32, (width, LANES), 0)
        s = jnp.where(((row & 1) == 0) & (row < limit), s * scale, -jnp.inf)
        row = lax.broadcasted_iota(jnp.int32, sn.shape, 0)
        step_of = (one % span) // heads
        seen = ((row & 1) == 0) & (row // new_rows == owner) & ((row % new_rows) // 2 <= step_of)
        sn = jnp.where(seen, sn * scale, -jnp.inf)
        top = jnp.maximum(jnp.max(s, axis=0, keepdims=True), jnp.max(sn, axis=0, keepdims=True))
        w = jnp.exp2(s - top)
        wn = jnp.exp2(sn - top)
        inverse = 1.0 / (jnp.sum(w, axis=0, keepdims=True) + jnp.sum(wn, axis=0, keepdims=True))
        p = jnp.transpose(pltpu.roll(w * inverse, 1, 0)).astype(jnp.bfloat16)
        pn = jnp.transpose(pltpu.roll(wn * inverse, 1, 0)).astype(jnp.bfloat16)
        head = (lax.broadcasted_iota(jnp.int32, (span, HEAD_WIDTH), 0) % heads) // GROUP
        for u in range(pack_size):
            at = slice(u * span, (u + 1) * span)
            full = dot(p[at], kvs[u]) + dot(pn[at], new)
            o = full[:, :HEAD_WIDTH]
            for g in range(1, heads_kv):
                o = jnp.where(head == g, full[:, g * HEAD_WIDTH : (g + 1) * HEAD_WIDTH], o)
            token = (rows[u] - base) * STEP_COUNT
            for t in range(STEP_COUNT):
                acc[pl.ds(token + t, heads, stride=tokens), :] = o[t * heads : (t + 1) * heads]

    @pl.loop(0, steps)
    def _(step):
        @pl.when(step + (SLOTS - 1) < steps)
        def _():
            fetch(step + (SLOTS - 1))

        count = most_chunks(step)
        for n in range(1, CHUNKS + 1):

            @pl.when(count == n)
            def _():
                compute(step, n)

    for h in range(heads):
        out_ref[:, h * HEAD_WIDTH : (h + 1) * HEAD_WIDTH] = acc[h * tokens : (h + 1) * tokens].astype(jnp.bfloat16)


def attend(part, order, lengths, table, q, new, pages, inbox):
    per_dev, _, _, columns = pages.shape
    req_count = inbox.shape[0]
    requests = lengths.shape[0] // HALVES
    heads = columns // HEAD_WIDTH * GROUP
    tokens = requests * STEP_COUNT
    pack_size = LANES // (STEP_COUNT * heads)
    extent = MAXP * PAGE_LENGTH * 2
    return pl.pallas_call(
        functools.partial(attend_kernel, req_count, per_dev, part * requests, requests),
        out_shape=jax.ShapeDtypeStruct((tokens, heads * HEAD_WIDTH), jnp.bfloat16),
        in_specs=[SMEM, SMEM, ANY, VMEM, VMEM, HBM, ANY],
        out_specs=VMEM,
        scratch_shapes=[
            pltpu.SMEM((per_dev // 128, 128), jnp.int32),
            pltpu.VMEM((req_count, 1, 2, columns), jnp.bfloat16),
            pltpu.VMEM((req_count, 128), jnp.int32),
            pltpu.SMEM((req_count, 128), jnp.int32),
            pltpu.VMEM((SLOTS, pack_size, extent, columns), jnp.bfloat16),
            pltpu.VMEM((heads * tokens, HEAD_WIDTH), jnp.float32),
            pltpu.SemaphoreType.DMA,
            pltpu.SemaphoreType.DMA((SLOTS, pack_size)),
        ],
        compiler_params=params(ATTEND_VMEM),
        cost_estimate=pl.CostEstimate(
            flops=16 * tokens * heads * HEAD_WIDTH * MAXP * PAGE_LENGTH,
            bytes_accessed=requests * extent * columns * 2,
            transcendentals=2 * tokens * heads * MAXP * PAGE_LENGTH,
        ),
        name="attend",
    )(order, lengths, table, q, new, pages, inbox)


def split_kernel(x_ref, o_ref, sems):
    parts, _, block = o_ref.shape
    copies = [
        pltpu.make_async_copy(x_ref.at[:, pl.ds(i * block, block)], o_ref.at[i], sems.at[i]) for i in range(parts)
    ]
    for copy in copies:
        copy.start()
    for copy in copies:
        copy.wait()


def split_columns(x, parts):
    rows, columns = x.shape
    return pl.pallas_call(
        split_kernel,
        out_shape=jax.ShapeDtypeStruct((parts, rows, columns // parts), x.dtype),
        in_specs=[HBM],
        out_specs=VMEM,
        scratch_shapes=[pltpu.SemaphoreType.DMA((parts,))],
        compiler_params=params(),
        cost_estimate=SMALL,
        name="split_columns",
    )(x)


def project_kernel(count, roles, tile, counts, where_ref, *refs):
    xs, (w_ref, down_ref, mask_ref), rest = refs[: len(counts)], refs[len(counts) : len(counts) + 3], refs[len(counts) + 3 :]
    outs, low_ref, x_v = rest[:-2], rest[-2], rest[-1]
    tokens = xs[0].shape[-2]
    rows = count * tokens // roles
    b = 0
    for x_ref, blocks in zip(xs, counts):
        for k in range(blocks):
            x = x_ref[...] if len(x_ref.shape) == 2 else x_ref[k]
            x_v[pl.ds(pl.multiple_of(where_ref[b] * tokens, tokens), tokens), :] = x
            b = b + 1
    low = dot(x_v[...], down_ref[...], ((1,), (1,)))
    for j in range(roles):
        s = where_ref[count + j]
        low_ref[s] = (low[j * rows : (j + 1) * rows] * mask_ref[s].astype(jnp.float32)).astype(jnp.bfloat16)

    @pl.loop(0, w_ref.shape[1] // tile)
    def _(i):
        at = pl.ds(pl.multiple_of(i * tile, tile), tile)
        y = dot(x_v[...], w_ref[:, at]).astype(jnp.bfloat16)
        parts = [y[j * rows : (j + 1) * rows, :] for j in range(roles)]
        if roles == 4:
            own, pair, two, three = outs
            own[:, at] = parts[0]
            pair[0, :, at] = parts[1]
            pair[1, :, at] = parts[3]
            two[:, at] = parts[2]
            three[:, at] = parts[3]
        else:
            for j in range(roles):
                outs[j][:, at] = parts[j]


def project(where, xs, w, down, mask, roles):
    counts = tuple(1 if len(x.shape) == 2 else x.shape[0] for x in xs)
    count = sum(counts)
    tokens, width = xs[0].shape
    columns = w.shape[1]
    rows = count * tokens // roles
    one = jax.ShapeDtypeStruct((rows, columns), jnp.bfloat16)
    outs = [one] * roles
    if roles == 4:
        outs[1] = jax.ShapeDtypeStruct((2, rows, columns), jnp.bfloat16)
    outs = outs + [jax.ShapeDtypeStruct((roles, rows, down.shape[0]), jnp.bfloat16)]
    return pl.pallas_call(
        functools.partial(project_kernel, count, roles, min(256, columns), counts),
        out_shape=outs,
        in_specs=[SMEM] + [VMEM] * (len(xs) + 3),
        out_specs=[VMEM] * len(outs),
        scratch_shapes=[pltpu.VMEM((count * tokens, width), jnp.bfloat16)],
        compiler_params=params(),
        cost_estimate=SMALL,
        name="project",
    )(where, *xs, w, down, mask)


def add_kernel(lane_ref, own_ref, passed_ref, o_ref):
    middle = (lane_ref[0] == 1) | (lane_ref[0] == 2)

    @pl.when(middle)
    def _():
        o_ref[...] = (own_ref[...].astype(jnp.float32) + passed_ref[1].astype(jnp.float32)).astype(jnp.bfloat16)

    @pl.when(jnp.logical_not(middle))
    def _():
        o_ref[...] = own_ref[...]


def add(lane, own, passed):
    return pl.pallas_call(
        add_kernel,
        out_shape=jax.ShapeDtypeStruct(own.shape, own.dtype),
        in_specs=[SMEM, VMEM, VMEM],
        out_specs=VMEM,
        compiler_params=params(),
        cost_estimate=SMALL,
        name="add",
    )(lane, own, passed)


def adapt_kernel(low_ref, up_ref, o_ref):
    low = jnp.concatenate([low_ref[a] for a in range(low_ref.shape[0])], axis=1)
    o_ref[...] = dot(low, up_ref[...])


def adapt(low, up):
    return pl.pallas_call(
        adapt_kernel,
        out_shape=jax.ShapeDtypeStruct((low.shape[1], up.shape[1]), jnp.float32),
        in_specs=[VMEM, VMEM],
        out_specs=VMEM,
        compiler_params=params(),
        cost_estimate=SMALL,
        name="adapt",
    )(low, up)


def finish_kernel(counts, cores, extra_ref, *refs):
    terms, o_ref = refs[:-1], refs[-1]
    rows = terms[0].shape[0]
    tokens = rows // cores
    first = 0
    for h, count in enumerate(counts):
        total = extra_ref[h * rows : (h + 1) * rows, :]
        for term in terms[first : first + count]:
            total = total + (term[...] if len(term.shape) == 2 else term[0]).astype(jnp.float32)
        first = first + count
        for c in range(cores):
            at = (c * len(counts) + h) * tokens
            o_ref[at : at + tokens, :] = total[c * tokens : (c + 1) * tokens].astype(jnp.bfloat16)


def finish(terms, cores, extra):
    flat = [t for half in terms for t in half]
    return pl.pallas_call(
        functools.partial(finish_kernel, tuple(len(half) for half in terms), cores),
        out_shape=jax.ShapeDtypeStruct(extra.shape, jnp.bfloat16),
        in_specs=[VMEM] * (1 + len(flat)),
        out_specs=VMEM,
        compiler_params=params(),
        cost_estimate=SMALL,
        name="finish",
    )(extra, *flat)


def exchange(x, axis, distance):
    count = lax.axis_size(axis)
    return lax.ppermute(x, axis, [(i, i ^ distance) for i in range(count)])


def after(x, *others):
    return lax.optimization_barrier((x, *others))[0]


def gather(x, gates):
    my_req = lax.axis_index("req").astype(jnp.int32)
    count = lax.axis_size("req")
    if count != 8:
        whole = lax.all_gather(x, "req", axis=0)
        return [whole[b] for b in range(count)], [jnp.int32(b) for b in range(count)], []
    near = exchange(x, "req", 1)
    far = [exchange(x, "req", d) for d in (2, 4, 6)]
    group = jnp.stack([after(block, *gates) for block in far] if gates else far)
    return [x, group, near, exchange(group, "req", 1)], [my_req ^ d for d in (0, 2, 4, 6, 1, 3, 5, 7)], far


def scatter(blocks):
    if len(blocks) != 4:
        return [lax.psum_scatter(jnp.stack(blocks), "tp", scatter_dimension=0, tiled=False)], blocks[0]
    own, pair, two, three = blocks
    lane = lax.axis_index("tp").astype(jnp.int32).reshape(1)
    pair = exchange(pair, "tp", 1)
    middle = lax.ppermute(three, "tp", [(1, 2), (2, 1)])
    passed = add(lane, two, pair)
    return [own, pair, middle, exchange(passed, "tp", 2)], passed


def on_device(
    queries,
    incoming_key_value,
    key_value_pages,
    page_request_home,
    lengths,
    request_adapter_index,
    adapter_storage_slot,
    adapter_down_factor,
    adapter_up_factor,
    output_projection_weight,
):
    req_count = lax.axis_size("req")
    tp_count = lax.axis_size("tp")
    my_req = lax.axis_index("req").astype(jnp.int32)
    my_lane = lax.axis_index("tp").astype(jnp.int32)
    me = my_req.reshape(1)
    requests = lengths.shape[0]
    half = requests // HALVES
    columns = key_value_pages.shape[-1]
    heads = columns // HEAD_WIDTH * GROUP
    own_slots, rank, model = adapter_up_factor.shape
    cores = req_count // tp_count

    outbox = pack(me, page_request_home, request_adapter_index, key_value_pages, req_count)
    inbox = lax.all_to_all(outbox, "req", split_axis=0, concat_axis=0, tiled=True)

    table, order = build_table(me, page_request_home, lengths, LANES // (STEP_COUNT * heads))
    q = queries.reshape(requests * STEP_COUNT * heads, HEAD_WIDTH).T
    up_blocks = split_columns(adapter_up_factor.reshape(own_slots * rank, model), req_count)
    new = incoming_key_value.transpose(1, 0, 2).reshape(-1, columns)
    down = adapter_down_factor.transpose(0, 2, 1).reshape(own_slots * rank, -1)

    up = lax.all_to_all(up_blocks, "req", split_axis=0, concat_axis=0, tiled=True)
    up = up.reshape(req_count * own_slots * rank, -1)
    slot_count = adapter_storage_slot.shape[0]
    ids = inbox[:, BLOCK - 1, 0, :requests].astype(jnp.int32)
    match = ids[:, :, None] == jnp.arange(slot_count, dtype=jnp.int32)
    slot = jnp.sum(jnp.where(match, adapter_storage_slot, 0), axis=2)
    mine = my_req * own_slots + jnp.arange(own_slots * rank, dtype=jnp.int32) // rank

    special = tp_count == 4
    roles = [my_lane ^ j if special else jnp.int32(j) for j in range(tp_count)]
    terms, lows, early, gates = [], [], [], []
    mixed = [attend(h, order, lengths, table, q, new, key_value_pages, inbox) for h in range(HALVES)]
    gates = [mixed[-1]]
    for h in range(HALVES):
        blocks, origins, far = gather(after(mixed[h], *early), gates)
        early = far
        where = []
        for origin in origins:
            s = origin // cores
            where.append((s ^ my_lane if special else s) * cores + origin % cores)
        where = jnp.stack(where + roles)
        token_slot = jnp.repeat(slot[:, h * half : (h + 1) * half], STEP_COUNT, axis=1)
        mask = (token_slot.reshape(tp_count, -1)[:, :, None] == mine).astype(jnp.bfloat16)
        mask = after(mask, *([passed] if h else [up]))
        *parts, low = project(where, blocks, output_projection_weight, down, mask, tp_count)
        gates = [low]
        lows.append(low)
        sums, passed = scatter(parts)
        terms.append(sums)

    low = after(jnp.concatenate(lows, axis=1), passed)
    low = lax.all_to_all(low, "tp", split_axis=0, concat_axis=0, tiled=True)
    low = jnp.sum(low.astype(jnp.float32), axis=0).astype(jnp.bfloat16)
    low = after(low, *terms[1][:3])
    low = after(lax.all_gather(low, "req", axis=0), *terms[1])
    return finish(terms, cores, adapt(low, up))


def solution(mesh):
    return jax.shard_map(
        on_device,
        mesh=mesh,
        in_specs=(
            P("req", "tp"),
            P(None, "req", "tp"),
            P("req", None, None, "tp"),
            P("req"),
            P("req"),
            P("req"),
            P(),
            P("req", "tp", None),
            P("req", None, None),
            P("tp", "req"),
        ),
        out_specs=P("tp", "req"),
        check_vma=False,
    )
```

```python
import functools
import math

import jax
import jax.numpy as jnp
from jax import lax
from jax.experimental import pallas as pl
from jax.experimental.pallas import tpu as pltpu
from jax.sharding import PartitionSpec as P

QUERY_HEADS = 64
KEY_VALUE_HEADS = 8
GROUP = QUERY_HEADS // KEY_VALUE_HEADS
HEAD_WIDTH = 128
STEP_COUNT = 4
PAGE_LENGTH = 32
MAXP = 16
CAP = 2
BLOCK = CAP * PAGE_LENGTH + 1
LABEL_LANE = 64
DIGIT = 16
CHUNK_PAGES = 4
CHUNKS = MAXP // CHUNK_PAGES
CHUNK_POSITIONS = CHUNK_PAGES * PAGE_LENGTH
LANES = 128
SLOTS = 6
HALVES = 2
VMEM_LIMIT = 24 * 1024 * 1024
WHOLE_VMEM = 60 * 1024 * 1024
ATTEND_VMEM = 48 * 1024 * 1024

SMALL = pl.CostEstimate(flops=1, bytes_accessed=1, transcendentals=0)

ANY = pl.BlockSpec(memory_space=pl.ANY)
HBM = pl.BlockSpec(memory_space=pltpu.HBM)
VMEM = pl.BlockSpec(memory_space=pltpu.VMEM)
SMEM = pl.BlockSpec(memory_space=pltpu.SMEM)


def params(limit=VMEM_LIMIT):
    return pltpu.CompilerParams(vmem_limit_bytes=limit)


def dot(a, b, contract=((1,), (0,))):
    return lax.dot_general(a, b, (contract, ((), ())), preferred_element_type=jnp.float32)


def pack_kernel(req_count, per_dev, me_ref, home_ref, ids_ref, pages, outbox, info_v, info_s, ids_v, rows_v, sem, sems):
    me = me_ref[0]
    page = lax.broadcasted_iota(jnp.int32, (req_count, per_dev), 1)
    want = lax.broadcasted_iota(jnp.int32, (req_count, per_dev), 0)
    slots = jnp.broadcast_to(home_ref[...], (req_count, per_dev)) - want * per_dev
    hit = (slots >= 0) & (slots < per_dev) & (want != me)
    lane = lax.broadcasted_iota(jnp.int32, (req_count, 128), 1)
    info = jnp.full((req_count, 128), -1, jnp.int32)
    for k in range(CAP):
        first = jnp.min(jnp.where(hit, page, per_dev), axis=1, keepdims=True)
        here = hit & (page == first)
        slot = jnp.max(jnp.where(here, slots, -1), axis=1, keepdims=True)
        info = jnp.where(lane == k, first, info)
        info = jnp.where(lane == CAP + k, slot, info)
        hit = hit & (page != first)
    info_v[...] = info
    fetch = pltpu.make_async_copy(info_v, info_s, sem)
    fetch.start()
    ids_v[...] = jnp.zeros_like(ids_v)
    ids_v[:, 0:ids_ref.shape[1]] = ids_ref[...].astype(jnp.float32)
    ids = jnp.broadcast_to(ids_v[...], (2, 128))
    fetch.wait()

    def copy(d, k):
        return pltpu.make_async_copy(
            pages.at[info_s[d, k]],
            outbox.at[d, pl.ds(k * PAGE_LENGTH, PAGE_LENGTH)],
            sems.at[d, k],
        )

    for d in range(req_count):
        for k in range(CAP):

            @pl.when(info_s[d, k] < per_dev)
            def _():
                copy(d, k).start()

    at = lax.broadcasted_iota(jnp.int32, (2, 128), 1)
    row = lax.broadcasted_iota(jnp.int32, (2, 128), 0)
    for d in range(req_count):
        value = jnp.where(row == 0, ids, 0.0)
        for k in range(CAP):
            slot = info_s[d, CAP + k]
            high = ((slot + DIGIT) >> 4) - 1
            low = slot - high * DIGIT
            digit = jnp.where(row == 0, high, low).astype(jnp.float32)
            value = jnp.where(at == LABEL_LANE + k, digit, value)
        rows_v[d, 0, :, :] = jnp.zeros(rows_v.shape[2:], jnp.bfloat16)
        rows_v[d, 0, :, 0:128] = value.astype(jnp.bfloat16)
    rows = pltpu.make_async_copy(rows_v, outbox.at[:, pl.ds(BLOCK - 1, 1)], sem)
    rows.start()
    rows.wait()
    for d in range(req_count):
        for k in range(CAP):

            @pl.when(info_s[d, k] < per_dev)
            def _():
                copy(d, k).wait()


def pack(me, page_request_home, ids, key_value_pages, req_count):
    per_dev = key_value_pages.shape[0]
    columns = key_value_pages.shape[-1]
    return pl.pallas_call(
        functools.partial(pack_kernel, req_count, per_dev),
        out_shape=jax.ShapeDtypeStruct((req_count, BLOCK, 2, columns), jnp.bfloat16),
        in_specs=[SMEM, VMEM, VMEM, HBM],
        out_specs=VMEM,
        scratch_shapes=[
            pltpu.VMEM((req_count, 128), jnp.int32),
            pltpu.SMEM((req_count, 128), jnp.int32),
            pltpu.VMEM((1, 128), jnp.float32),
            pltpu.VMEM((req_count, 1, 2, columns), jnp.bfloat16),
            pltpu.SemaphoreType.DMA,
            pltpu.SemaphoreType.DMA((req_count, CAP)),
        ],
        compiler_params=params(WHOLE_VMEM),
        cost_estimate=SMALL,
        name="pack_outbox",
    )(me, page_request_home.reshape(1, per_dev), ids.reshape(1, -1), key_value_pages)


def table_kernel(per_dev, requests, pack_size, me_ref, home_ref, lengths_ref, table_ref, order_ref, len_v):
    base = me_ref[0] * per_dev
    lane = lax.broadcasted_iota(jnp.int32, (128, 128), 1)
    row = lax.broadcasted_iota(jnp.int32, (128, 128), 0)
    tiles = per_dev // 128
    columns = [
        jnp.transpose(jnp.broadcast_to(home_ref[i : i + 1, :] - base, (128, 128)).astype(jnp.float32))
        for i in range(tiles)
    ]
    for j in range(tiles):
        total = jnp.zeros((128, 128), jnp.float32)
        slot = (lane + j * 128).astype(jnp.float32)
        for i in range(tiles):
            total = total + jnp.where(columns[i] == slot, (row + i * 128).astype(jnp.float32), 0.0)
        table_ref[j : j + 1, :] = jnp.sum(total, axis=0, keepdims=True).astype(jnp.int32)
    half = requests // HALVES
    len_v[...] = jnp.zeros_like(len_v)
    len_v[:, 0:requests] = lengths_ref[...].astype(jnp.float32)
    along = jnp.broadcast_to(len_v[...], (128, 128))
    along = ((along.astype(jnp.int32) + (CHUNK_POSITIONS - 1)) >> 7).astype(jnp.float32)
    down = jnp.transpose(along)
    same = ((lane // half) == (row // half)) & (lane % pack_size == row % pack_size)
    before = same & ((along > down) | ((along == down) & (lane < row)))
    rank = jnp.sum(jnp.where(before, 1.0, 0.0), axis=1, keepdims=True)
    place = rank * pack_size + ((row // half) * half + row % pack_size).astype(jnp.float32)
    at = place == lane.astype(jnp.float32)
    order = jnp.sum(jnp.where(at, row.astype(jnp.float32), 0.0), axis=0, keepdims=True)
    chunks = jnp.sum(jnp.where(at, down, 0.0), axis=0, keepdims=True)
    order_ref[0:1, :] = order.astype(jnp.int32)
    order_ref[1:2, :] = chunks.astype(jnp.int32)


def build_table(me, page_request_home, lengths, pack_size):
    per_dev = page_request_home.shape[0]
    requests = lengths.shape[0]
    return pl.pallas_call(
        functools.partial(table_kernel, per_dev, requests, pack_size),
        out_shape=(
            jax.ShapeDtypeStruct((per_dev // 128, 128), jnp.int32),
            jax.ShapeDtypeStruct((2, 128), jnp.int32),
        ),
        in_specs=[SMEM, VMEM, VMEM],
        out_specs=(VMEM, VMEM),
        scratch_shapes=[pltpu.VMEM((1, 128), jnp.float32)],
        compiler_params=params(),
        cost_estimate=SMALL,
        name="page_table",
    )(me, page_request_home.reshape(per_dev // 128, 128), lengths.reshape(1, requests))


def attend_kernel(
    req_count,
    per_dev,
    base,
    requests,
    order_ref,
    lengths_ref,
    table_in,
    q_ref,
    new_ref,
    pages,
    inbox,
    out_ref,
    table,
    labels_v,
    labels_w,
    labels_s,
    buf,
    acc,
    sem,
    sems,
):
    columns = pages.shape[-1]
    heads_kv = columns // HEAD_WIDTH
    heads = heads_kv * GROUP
    span = STEP_COUNT * heads
    pack_size = LANES // span
    page_size = PAGE_LENGTH * 2
    chunk_size = CHUNK_PAGES * page_size
    new_rows = STEP_COUNT * 2
    tokens = requests * STEP_COUNT
    scale = math.log2(math.e) / math.sqrt(HEAD_WIDTH)
    page_rows = pages.reshape(per_dev, page_size, columns)
    inbox_rows = inbox.reshape(req_count, BLOCK * 2, columns)

    if base == 0:
        first = pltpu.make_async_copy(inbox.at[:, pl.ds(BLOCK - 1, 1)], labels_v, sem)
        first.start()
        first.wait()
        row = lax.broadcasted_iota(jnp.int32, (2, 128), 0)
        weight = jnp.where(row == 0, float(DIGIT), 1.0)
        for d in range(req_count):
            digits = labels_v[d, 0, :, 0:128].astype(jnp.float32) * weight
            labels_w[d : d + 1, :] = jnp.sum(digits, axis=0, keepdims=True).astype(jnp.int32)
        back = pltpu.make_async_copy(labels_w, labels_s, sem)
        back.start()

        @pl.loop(0, per_dev // 128)
        def _(i):
            @pl.loop(0, 128, unroll=8)
            def _(j):
                table[i, j] = table_in[i, j]

        back.wait()
        for d in range(req_count):
            for k in range(CAP):
                slot = labels_s[d, LABEL_LANE + k]

                @pl.when(slot >= 0)
                def _():
                    table[lax.shift_right_logical(slot, 7), slot & 127] = per_dev + d * CAP + k

    else:
        table[0, 0] = 0
        table = table_in

    steps = requests // pack_size

    def most_chunks(step):
        counts = [order_ref[1, base + step * pack_size + u] for u in range(pack_size)]
        return functools.reduce(jnp.maximum, counts)

    def fetch(step):
        place = lax.rem(step, SLOTS)
        count = most_chunks(step)
        for u in range(pack_size):
            slot = order_ref[0, base + step * pack_size + u] * MAXP
            line = lax.shift_right_logical(slot, 7)
            at = slot & 127

            @pl.loop(0, count)
            def _(c):
                sources = [table[line, at + c * CHUNK_PAGES + j] for j in range(CHUNK_PAGES)]
                most = functools.reduce(jnp.maximum, sources)

                def target(j):
                    start = pl.multiple_of(c * chunk_size + j * page_size, page_size)
                    return buf.at[place, u, pl.ds(start, page_size)]

                @pl.when(most < per_dev)
                def _():
                    for j in range(CHUNK_PAGES):
                        pltpu.make_async_copy(page_rows.at[sources[j]], target(j), sems.at[place, u]).start()

                @pl.when(most >= per_dev)
                def _():
                    for j in range(CHUNK_PAGES):
                        source = sources[j]

                        @pl.when(source < per_dev)
                        def _():
                            pltpu.make_async_copy(page_rows.at[source], target(j), sems.at[place, u]).start()

                        @pl.when(source >= per_dev)
                        def _():
                            e = source - per_dev
                            d = lax.shift_right_logical(e, 1)
                            start = pl.multiple_of((e - d * CAP) * page_size, page_size)
                            pltpu.make_async_copy(
                                inbox_rows.at[d, pl.ds(start, page_size)], target(j), sems.at[place, u]
                            ).start()

    for s in range(min(SLOTS - 1, steps)):
        fetch(jnp.int32(s))

    def compute(step, n):
        place = lax.rem(step, SLOTS)
        width = n * chunk_size
        for u in range(pack_size):
            whole = buf.at[place, u, pl.ds(0, width)]
            pltpu.make_async_copy(whole, whole, sems.at[place, u]).wait()
        lane = lax.broadcasted_iota(jnp.int32, (HEAD_WIDTH, LANES), 1)
        part = lane // span
        lane_head = (lane % heads) // GROUP
        one = lax.broadcasted_iota(jnp.int32, (1, LANES), 1)
        limit = jnp.zeros((1, LANES), jnp.int32)
        owner = jnp.zeros((1, LANES), jnp.int32)
        rows, kvs, rights = [], [], []
        for u in range(pack_size):
            r = order_ref[0, base + step * pack_size + u]
            rows.append(r)
            q = q_ref[:, pl.ds(pl.multiple_of((r // pack_size) * LANES, LANES), LANES)].astype(jnp.float32)
            own = part == u
            rights.append(
                jnp.concatenate(
                    [jnp.where(own & (lane_head == g), q, 0.0).astype(jnp.bfloat16) for g in range(heads_kv)], axis=0
                )
            )
            kvs.append(buf[place, u, 0:width, :])
            limit = jnp.where(one // span == u, 2 * lengths_ref[r], limit)
            owner = jnp.where(one // span == u, r - base, owner)
        new = new_ref[base * new_rows : (base + requests) * new_rows, :]
        s = dot(jnp.concatenate(kvs, axis=1), jnp.concatenate(rights, axis=0))
        sn = dot(new, functools.reduce(jnp.add, rights))
        row = lax.broadcasted_iota(jnp.int32, (width, LANES), 0)
        s = jnp.where(((row & 1) == 0) & (row < limit), s * scale, -jnp.inf)
        row = lax.broadcasted_iota(jnp.int32, sn.shape, 0)
        step_of = (one % span) // heads
        seen = ((row & 1) == 0) & (row // new_rows == owner) & ((row % new_rows) // 2 <= step_of)
        sn = jnp.where(seen, sn * scale, -jnp.inf)
        top = jnp.maximum(jnp.max(s, axis=0, keepdims=True), jnp.max(sn, axis=0, keepdims=True))
        w = jnp.exp2(s - top)
        wn = jnp.exp2(sn - top)
        inverse = 1.0 / (jnp.sum(w, axis=0, keepdims=True) + jnp.sum(wn, axis=0, keepdims=True))
        p = jnp.transpose(pltpu.roll(w * inverse, 1, 0)).astype(jnp.bfloat16)
        pn = jnp.transpose(pltpu.roll(wn * inverse, 1, 0)).astype(jnp.bfloat16)
        head = (lax.broadcasted_iota(jnp.int32, (span, HEAD_WIDTH), 0) % heads) // GROUP
        for u in range(pack_size):
            at = slice(u * span, (u + 1) * span)
            full = dot(p[at], kvs[u]) + dot(pn[at], new)
            o = full[:, :HEAD_WIDTH]
            for g in range(1, heads_kv):
                o = jnp.where(head == g, full[:, g * HEAD_WIDTH : (g + 1) * HEAD_WIDTH], o)
            token = (rows[u] - base) * STEP_COUNT
            for t in range(STEP_COUNT):
                acc[pl.ds(token + t, heads, stride=tokens), :] = o[t * heads : (t + 1) * heads]

    @pl.loop(0, steps)
    def _(step):
        @pl.when(step + (SLOTS - 1) < steps)
        def _():
            fetch(step + (SLOTS - 1))

        count = most_chunks(step)
        for n in range(1, CHUNKS + 1):

            @pl.when(count == n)
            def _():
                compute(step, n)

    for h in range(heads):
        out_ref[:, h * HEAD_WIDTH : (h + 1) * HEAD_WIDTH] = acc[h * tokens : (h + 1) * tokens].astype(jnp.bfloat16)


def attend(part, order, lengths, table, q, new, pages, inbox):
    per_dev, _, _, columns = pages.shape
    req_count = inbox.shape[0]
    requests = lengths.shape[0] // HALVES
    heads = columns // HEAD_WIDTH * GROUP
    tokens = requests * STEP_COUNT
    pack_size = LANES // (STEP_COUNT * heads)
    extent = MAXP * PAGE_LENGTH * 2
    return pl.pallas_call(
        functools.partial(attend_kernel, req_count, per_dev, part * requests, requests),
        out_shape=(
            jax.ShapeDtypeStruct((tokens, heads * HEAD_WIDTH), jnp.bfloat16),
            jax.ShapeDtypeStruct(table.shape, jnp.int32),
        ),
        in_specs=[SMEM, SMEM, SMEM, VMEM, VMEM, HBM, ANY],
        out_specs=(VMEM, SMEM),
        scratch_shapes=[
            pltpu.VMEM((req_count, 1, 2, columns), jnp.bfloat16),
            pltpu.VMEM((req_count, 128), jnp.int32),
            pltpu.SMEM((req_count, 128), jnp.int32),
            pltpu.VMEM((SLOTS, pack_size, extent, columns), jnp.bfloat16),
            pltpu.VMEM((heads * tokens, HEAD_WIDTH), jnp.float32),
            pltpu.SemaphoreType.DMA,
            pltpu.SemaphoreType.DMA((SLOTS, pack_size)),
        ],
        compiler_params=params(ATTEND_VMEM),
        cost_estimate=pl.CostEstimate(
            flops=16 * tokens * heads * HEAD_WIDTH * MAXP * PAGE_LENGTH,
            bytes_accessed=requests * extent * columns * 2,
            transcendentals=2 * tokens * heads * MAXP * PAGE_LENGTH,
        ),
        name="attend",
    )(order, lengths, table, q, new, pages, inbox)


def split_kernel(x_ref, o_ref, sems):
    parts, _, block = o_ref.shape
    copies = [
        pltpu.make_async_copy(x_ref.at[:, pl.ds(i * block, block)], o_ref.at[i], sems.at[i]) for i in range(parts)
    ]
    for copy in copies:
        copy.start()
    for copy in copies:
        copy.wait()


def split_columns(x, parts):
    rows, columns = x.shape
    return pl.pallas_call(
        split_kernel,
        out_shape=jax.ShapeDtypeStruct((parts, rows, columns // parts), x.dtype),
        in_specs=[HBM],
        out_specs=VMEM,
        scratch_shapes=[pltpu.SemaphoreType.DMA((parts,))],
        compiler_params=params(),
        cost_estimate=SMALL,
        name="split_columns",
    )(x)


def project_kernel(counts, roles, tile, earlier, where_ref, *refs):
    xs, refs = refs[: len(counts)], refs[len(counts) :]
    (w_ref, down_ref, mask_ref), refs = refs[:3], refs[3:]
    before, refs = refs[:earlier], refs[earlier:]
    out_ref, lows, x_v, low_v = refs[0], refs[1 : 1 + roles], refs[-2], refs[-1]
    tokens = xs[0].shape[-2]
    count = sum(counts)
    rows = count * tokens // roles
    b = 0
    for x_ref, blocks in zip(xs, counts):
        for k in range(blocks):
            x = x_ref[...] if len(x_ref.shape) == 2 else x_ref[k]
            x_v[pl.ds(pl.multiple_of(where_ref[b] * tokens, tokens), tokens), :] = x
            b = b + 1
    low_v[...] = dot(x_v[...], down_ref[...], ((1,), (1,)))
    for j in range(roles):
        s = where_ref[count + j]
        low = low_v[pl.ds(pl.multiple_of(s * rows, rows), rows), :] * mask_ref[s].astype(jnp.float32)
        start = before[j].shape[0] if earlier else 0
        if earlier:
            lows[j][0:start, :] = before[j][...]
        lows[j][start : start + rows, :] = low.astype(jnp.bfloat16)

    @pl.loop(0, w_ref.shape[1] // tile)
    def _(i):
        at = pl.ds(pl.multiple_of(i * tile, tile), tile)
        y = dot(x_v[...], w_ref[:, at]).astype(jnp.bfloat16)
        for j in range(roles):
            out_ref[j, :, at] = y[j * rows : (j + 1) * rows, :]


def project(where, xs, w, down, mask, roles, before):
    counts = tuple(1 if len(x.shape) == 2 else x.shape[0] for x in xs)
    count = sum(counts)
    tokens, width = xs[0].shape
    columns = w.shape[1]
    rows = count * tokens // roles
    height = rows + (before[0].shape[0] if before else 0)
    ranks = down.shape[0]
    out, *lows = pl.pallas_call(
        functools.partial(project_kernel, counts, roles, min(256, columns), len(before)),
        out_shape=[jax.ShapeDtypeStruct((roles, rows, columns), jnp.bfloat16)]
        + [jax.ShapeDtypeStruct((height, ranks), jnp.bfloat16)] * roles,
        in_specs=[SMEM] + [VMEM] * (len(xs) + 3 + len(before)),
        out_specs=[VMEM] * (1 + roles),
        scratch_shapes=[
            pltpu.VMEM((count * tokens, width), jnp.bfloat16),
            pltpu.VMEM((count * tokens, ranks), jnp.float32),
        ],
        compiler_params=params(),
        cost_estimate=SMALL,
        name="project",
    )(where, *xs, w, down, mask, *before)
    return out, lows


def adapt_kernel(low_ref, up_ref, o_ref):
    low = jnp.concatenate([low_ref[a] for a in range(low_ref.shape[0])], axis=1)
    o_ref[...] = dot(low, up_ref[...])


def adapt(low, up):
    return pl.pallas_call(
        adapt_kernel,
        out_shape=jax.ShapeDtypeStruct((low.shape[1], up.shape[1]), jnp.float32),
        in_specs=[VMEM, VMEM],
        out_specs=VMEM,
        compiler_params=params(),
        cost_estimate=SMALL,
        name="adapt",
    )(low, up)


def finish_kernel(cores, extra_ref, *refs):
    sums, o_ref = refs[:-1], refs[-1]
    roles, rows, _ = sums[0].shape
    tokens = rows // cores
    for h, sum_ref in enumerate(sums):
        total = extra_ref[h * rows : (h + 1) * rows, :]
        for j in range(roles):
            total = total + sum_ref[j].astype(jnp.float32)
        for c in range(cores):
            at = (c * len(sums) + h) * tokens
            o_ref[at : at + tokens, :] = total[c * tokens : (c + 1) * tokens].astype(jnp.bfloat16)


def finish(sums, cores, extra):
    return pl.pallas_call(
        functools.partial(finish_kernel, cores),
        out_shape=jax.ShapeDtypeStruct(extra.shape, jnp.bfloat16),
        in_specs=[VMEM] * (1 + len(sums)),
        out_specs=VMEM,
        compiler_params=params(),
        cost_estimate=SMALL,
        name="finish",
    )(extra, *sums)


def exchange(x, axis, distance):
    count = lax.axis_size(axis)
    return lax.ppermute(x, axis, [(i, i ^ distance) for i in range(count)])


def after(x, *others):
    return lax.optimization_barrier((x, *others))[0]


def gather(x, gates):
    my_req = lax.axis_index("req").astype(jnp.int32)
    count = lax.axis_size("req")
    if count != 8:
        whole = lax.all_gather(x, "req", axis=0)
        return [whole[b] for b in range(count)], [jnp.int32(b) for b in range(count)], []
    near = exchange(x, "req", 1)
    far = [exchange(x, "req", d) for d in (2, 4, 6)]
    group = jnp.stack([after(block, *gates) for block in far] if gates else far)
    return [x, group, near, exchange(group, "req", 1)], [my_req ^ d for d in (0, 2, 4, 6, 1, 3, 5, 7)], far


def on_device(
    queries,
    incoming_key_value,
    key_value_pages,
    page_request_home,
    lengths,
    request_adapter_index,
    adapter_storage_slot,
    adapter_down_factor,
    adapter_up_factor,
    output_projection_weight,
):
    req_count = lax.axis_size("req")
    tp_count = lax.axis_size("tp")
    my_req = lax.axis_index("req").astype(jnp.int32)
    my_lane = lax.axis_index("tp").astype(jnp.int32)
    me = my_req.reshape(1)
    requests = lengths.shape[0]
    half = requests // HALVES
    columns = key_value_pages.shape[-1]
    heads = columns // HEAD_WIDTH * GROUP
    own_slots, rank, model = adapter_up_factor.shape
    cores = req_count // tp_count

    outbox = pack(me, page_request_home, request_adapter_index, key_value_pages, req_count)
    inbox = lax.all_to_all(outbox, "req", split_axis=0, concat_axis=0, tiled=True)

    table, order = build_table(me, page_request_home, lengths, LANES // (STEP_COUNT * heads))
    q = queries.reshape(requests * STEP_COUNT * heads, HEAD_WIDTH).T
    up_blocks = split_columns(adapter_up_factor.reshape(own_slots * rank, model), req_count)
    new = incoming_key_value.transpose(1, 0, 2).reshape(-1, columns)
    down = adapter_down_factor.transpose(0, 2, 1).reshape(own_slots * rank, -1)

    up = lax.all_to_all(up_blocks, "req", split_axis=0, concat_axis=0, tiled=True)
    up = up.reshape(req_count * own_slots * rank, -1)
    slot_count = adapter_storage_slot.shape[0]
    ids = inbox[:, BLOCK - 1, 0, :requests].astype(jnp.int32)
    match = ids[:, :, None] == jnp.arange(slot_count, dtype=jnp.int32)
    slot = jnp.sum(jnp.where(match, adapter_storage_slot, 0), axis=2)
    mine = my_req * own_slots + jnp.arange(own_slots * rank, dtype=jnp.int32) // rank

    roles = [my_lane ^ j for j in range(tp_count)]
    first, table = attend(0, order, lengths, table, q, new, key_value_pages, inbox)
    second, table = attend(1, order, lengths, table, q, new, key_value_pages, inbox)
    up = lax.all_to_all(after(up_blocks, first), "req", split_axis=0, concat_axis=0, tiled=True)
    up = up.reshape(req_count * own_slots * rank, -1)
    sums, lows, early, gates = [], [], [], [second]
    for h, mixed in enumerate((first, second)):
        blocks, origins, far = gather(after(mixed, *early), gates)
        early = far
        where = jnp.stack(origins + roles)
        token_slot = jnp.repeat(slot[:, h * half : (h + 1) * half], STEP_COUNT, axis=1)
        mask = (token_slot.reshape(tp_count, -1)[:, :, None] == mine).astype(jnp.bfloat16)
        if h == 0:
            mask = after(mask, up)
        parts, lows = project(where, blocks, output_projection_weight, down, mask, tp_count, lows)
        gates = [lows[0]]
        sums.append(lax.all_to_all(parts, "tp", split_axis=0, concat_axis=0, tiled=True))

    terms = [lows[0]] + [exchange(lows[j], "tp", j) for j in range(1, tp_count)]
    low = functools.reduce(jnp.add, [term.astype(jnp.float32) for term in terms]).astype(jnp.bfloat16)
    low = lax.all_gather(low, "req", axis=0)
    return finish(sums, cores, adapt(low, up))


def solution(mesh):
    return jax.shard_map(
        on_device,
        mesh=mesh,
        in_specs=(
            P("req", "tp"),
            P(None, "req", "tp"),
            P("req", None, None, "tp"),
            P("req"),
            P("req"),
            P("req"),
            P(),
            P("req", "tp", None),
            P("req", None, None),
            P("tp", "req"),
        ),
        out_specs=P("tp", "req"),
        check_vma=False,
    )
```

```python
import functools
import math

import jax
import jax.numpy as jnp
from jax import lax
from jax.experimental import pallas as pl
from jax.experimental.pallas import tpu as pltpu
from jax.sharding import PartitionSpec as P

QUERY_HEADS = 64
KEY_VALUE_HEADS = 8
GROUP = QUERY_HEADS // KEY_VALUE_HEADS
HEAD_WIDTH = 128
STEP_COUNT = 4
PAGE_LENGTH = 32
MAXP = 16
CAP = 2
BLOCK = CAP * PAGE_LENGTH + 1
LABEL_LANE = 64
DIGIT = 16
CHUNK_PAGES = 4
CHUNKS = MAXP // CHUNK_PAGES
CHUNK_POSITIONS = CHUNK_PAGES * PAGE_LENGTH
LANES = 128
NEW_GROUP = 128 // (2 * STEP_COUNT)
SLOTS = 6
VMEM_LIMIT = 24 * 1024 * 1024
WHOLE_VMEM = 60 * 1024 * 1024
ATTEND_VMEM = 48 * 1024 * 1024

SMALL = pl.CostEstimate(flops=1, bytes_accessed=1, transcendentals=0)

ANY = pl.BlockSpec(memory_space=pl.ANY)
HBM = pl.BlockSpec(memory_space=pltpu.HBM)
VMEM = pl.BlockSpec(memory_space=pltpu.VMEM)
SMEM = pl.BlockSpec(memory_space=pltpu.SMEM)


def params(limit=VMEM_LIMIT):
    return pltpu.CompilerParams(vmem_limit_bytes=limit)


def dot(a, b, contract=((1,), (0,))):
    return lax.dot_general(a, b, (contract, ((), ())), preferred_element_type=jnp.float32)


def pack_kernel(req_count, per_dev, me_ref, home_ref, ids_ref, pages, outbox, info_v, info_s, ids_v, rows_v, sem, sems):
    me = me_ref[0]
    page = lax.broadcasted_iota(jnp.int32, (req_count, per_dev), 1)
    want = lax.broadcasted_iota(jnp.int32, (req_count, per_dev), 0)
    slots = jnp.broadcast_to(home_ref[...], (req_count, per_dev)) - want * per_dev
    hit = (slots >= 0) & (slots < per_dev) & (want != me)
    lane = lax.broadcasted_iota(jnp.int32, (req_count, 128), 1)
    info = jnp.full((req_count, 128), -1, jnp.int32)
    for k in range(CAP):
        first = jnp.min(jnp.where(hit, page, per_dev), axis=1, keepdims=True)
        here = hit & (page == first)
        slot = jnp.max(jnp.where(here, slots, -1), axis=1, keepdims=True)
        info = jnp.where(lane == k, first, info)
        info = jnp.where(lane == CAP + k, slot, info)
        hit = hit & (page != first)
    info_v[...] = info
    fetch = pltpu.make_async_copy(info_v, info_s, sem)
    fetch.start()
    ids_v[...] = jnp.zeros_like(ids_v)
    ids_v[:, 0:ids_ref.shape[1]] = ids_ref[...].astype(jnp.float32)
    ids = jnp.broadcast_to(ids_v[...], (2, 128))
    fetch.wait()

    def copy(d, k):
        return pltpu.make_async_copy(
            pages.at[info_s[d, k]],
            outbox.at[d, pl.ds(k * PAGE_LENGTH, PAGE_LENGTH)],
            sems.at[d, k],
        )

    for d in range(req_count):
        for k in range(CAP):

            @pl.when(info_s[d, k] < per_dev)
            def _():
                copy(d, k).start()

    at = lax.broadcasted_iota(jnp.int32, (2, 128), 1)
    row = lax.broadcasted_iota(jnp.int32, (2, 128), 0)
    for d in range(req_count):
        value = jnp.where(row == 0, ids, 0.0)
        for k in range(CAP):
            slot = info_s[d, CAP + k]
            high = ((slot + DIGIT) >> 4) - 1
            low = slot - high * DIGIT
            digit = jnp.where(row == 0, high, low).astype(jnp.float32)
            value = jnp.where(at == LABEL_LANE + k, digit, value)
        rows_v[d, 0, :, :] = jnp.zeros(rows_v.shape[2:], jnp.bfloat16)
        rows_v[d, 0, :, 0:128] = value.astype(jnp.bfloat16)
    rows = pltpu.make_async_copy(rows_v, outbox.at[:, pl.ds(BLOCK - 1, 1)], sem)
    rows.start()
    rows.wait()
    for d in range(req_count):
        for k in range(CAP):

            @pl.when(info_s[d, k] < per_dev)
            def _():
                copy(d, k).wait()


def pack(me, page_request_home, ids, key_value_pages, req_count):
    per_dev = key_value_pages.shape[0]
    columns = key_value_pages.shape[-1]
    return pl.pallas_call(
        functools.partial(pack_kernel, req_count, per_dev),
        out_shape=jax.ShapeDtypeStruct((req_count, BLOCK, 2, columns), jnp.bfloat16),
        in_specs=[SMEM, VMEM, VMEM, HBM],
        out_specs=VMEM,
        scratch_shapes=[
            pltpu.VMEM((req_count, 128), jnp.int32),
            pltpu.SMEM((req_count, 128), jnp.int32),
            pltpu.VMEM((1, 128), jnp.float32),
            pltpu.VMEM((req_count, 1, 2, columns), jnp.bfloat16),
            pltpu.SemaphoreType.DMA,
            pltpu.SemaphoreType.DMA((req_count, CAP)),
        ],
        compiler_params=params(WHOLE_VMEM),
        cost_estimate=SMALL,
        name="pack_outbox",
    )(me, page_request_home.reshape(1, per_dev), ids.reshape(1, -1), key_value_pages)


def table_kernel(per_dev, requests, pack_size, me_ref, home_ref, lengths_ref, table_ref, order_ref, len_v):
    base = me_ref[0] * per_dev
    lane = lax.broadcasted_iota(jnp.int32, (128, 128), 1)
    row = lax.broadcasted_iota(jnp.int32, (128, 128), 0)
    tiles = per_dev // 128
    columns = [
        jnp.transpose(jnp.broadcast_to(home_ref[i : i + 1, :] - base, (128, 128)).astype(jnp.float32))
        for i in range(tiles)
    ]
    for j in range(tiles):
        total = jnp.zeros((128, 128), jnp.float32)
        slot = (lane + j * 128).astype(jnp.float32)
        for i in range(tiles):
            total = total + jnp.where(columns[i] == slot, (row + i * 128).astype(jnp.float32), 0.0)
        table_ref[j : j + 1, :] = jnp.sum(total, axis=0, keepdims=True).astype(jnp.int32)
    half = NEW_GROUP
    len_v[...] = jnp.zeros_like(len_v)
    len_v[:, 0:requests] = lengths_ref[...].astype(jnp.float32)
    along = jnp.broadcast_to(len_v[...], (128, 128))
    along = ((along.astype(jnp.int32) + (CHUNK_POSITIONS - 1)) >> 7).astype(jnp.float32)
    down = jnp.transpose(along)
    same = ((lane // half) == (row // half)) & (lane % pack_size == row % pack_size)
    before = same & ((along > down) | ((along == down) & (lane < row)))
    rank = jnp.sum(jnp.where(before, 1.0, 0.0), axis=1, keepdims=True)
    place = rank * pack_size + ((row // half) * half + row % pack_size).astype(jnp.float32)
    at = place == lane.astype(jnp.float32)
    order = jnp.sum(jnp.where(at, row.astype(jnp.float32), 0.0), axis=0, keepdims=True)
    chunks = jnp.sum(jnp.where(at, down, 0.0), axis=0, keepdims=True)
    order_ref[0:1, :] = order.astype(jnp.int32)
    order_ref[1:2, :] = chunks.astype(jnp.int32)


def build_table(me, page_request_home, lengths, pack_size):
    per_dev = page_request_home.shape[0]
    requests = lengths.shape[0]
    return pl.pallas_call(
        functools.partial(table_kernel, per_dev, requests, pack_size),
        out_shape=(
            jax.ShapeDtypeStruct((per_dev // 128, 128), jnp.int32),
            jax.ShapeDtypeStruct((2, 128), jnp.int32),
        ),
        in_specs=[SMEM, VMEM, VMEM],
        out_specs=(VMEM, VMEM),
        scratch_shapes=[pltpu.VMEM((1, 128), jnp.float32)],
        compiler_params=params(),
        cost_estimate=SMALL,
        name="page_table",
    )(me, page_request_home.reshape(per_dev // 128, 128), lengths.reshape(1, requests))


def attend_kernel(
    req_count,
    per_dev,
    requests,
    order_ref,
    lengths_ref,
    table_in,
    q_ref,
    new_ref,
    pages,
    inbox,
    out_ref,
    table,
    labels_v,
    labels_w,
    labels_s,
    buf,
    acc,
    sem,
    sems,
):
    columns = pages.shape[-1]
    heads_kv = columns // HEAD_WIDTH
    heads = heads_kv * GROUP
    span = STEP_COUNT * heads
    pack_size = LANES // span
    page_size = PAGE_LENGTH * 2
    chunk_size = CHUNK_PAGES * page_size
    new_rows = STEP_COUNT * 2
    tokens = requests * STEP_COUNT
    scale = math.log2(math.e) / math.sqrt(HEAD_WIDTH)
    page_rows = pages.reshape(per_dev, page_size, columns)
    inbox_rows = inbox.reshape(req_count, BLOCK * 2, columns)

    first = pltpu.make_async_copy(inbox.at[:, pl.ds(BLOCK - 1, 1)], labels_v, sem)
    first.start()
    first.wait()
    row = lax.broadcasted_iota(jnp.int32, (2, 128), 0)
    weight = jnp.where(row == 0, float(DIGIT), 1.0)
    for d in range(req_count):
        digits = labels_v[d, 0, :, 0:128].astype(jnp.float32) * weight
        labels_w[d : d + 1, :] = jnp.sum(digits, axis=0, keepdims=True).astype(jnp.int32)
    back = pltpu.make_async_copy(labels_w, labels_s, sem)
    back.start()

    @pl.loop(0, per_dev // 128)
    def _(i):
        @pl.loop(0, 128, unroll=8)
        def _(j):
            table[i, j] = table_in[i, j]

    back.wait()
    for d in range(req_count):
        for k in range(CAP):
            slot = labels_s[d, LABEL_LANE + k]

            @pl.when(slot >= 0)
            def _():
                table[lax.shift_right_logical(slot, 7), slot & 127] = per_dev + d * CAP + k

    steps = requests // pack_size

    def most_chunks(step):
        counts = [order_ref[1, step * pack_size + u] for u in range(pack_size)]
        return functools.reduce(jnp.maximum, counts)

    def fetch(step):
        place = lax.rem(step, SLOTS)
        count = most_chunks(step)
        for u in range(pack_size):
            slot = order_ref[0, step * pack_size + u] * MAXP
            line = lax.shift_right_logical(slot, 7)
            at = slot & 127

            @pl.loop(0, count)
            def _(c):
                sources = [table[line, at + c * CHUNK_PAGES + j] for j in range(CHUNK_PAGES)]
                most = functools.reduce(jnp.maximum, sources)

                def target(j):
                    start = pl.multiple_of(c * chunk_size + j * page_size, page_size)
                    return buf.at[place, u, pl.ds(start, page_size)]

                @pl.when(most < per_dev)
                def _():
                    for j in range(CHUNK_PAGES):
                        pltpu.make_async_copy(page_rows.at[sources[j]], target(j), sems.at[place, u]).start()

                @pl.when(most >= per_dev)
                def _():
                    for j in range(CHUNK_PAGES):
                        source = sources[j]

                        @pl.when(source < per_dev)
                        def _():
                            pltpu.make_async_copy(page_rows.at[source], target(j), sems.at[place, u]).start()

                        @pl.when(source >= per_dev)
                        def _():
                            e = source - per_dev
                            d = lax.shift_right_logical(e, 1)
                            start = pl.multiple_of((e - d * CAP) * page_size, page_size)
                            pltpu.make_async_copy(
                                inbox_rows.at[d, pl.ds(start, page_size)], target(j), sems.at[place, u]
                            ).start()

    for s in range(min(SLOTS - 1, steps)):
        fetch(jnp.int32(s))

    def compute(step, n):
        place = lax.rem(step, SLOTS)
        width = n * chunk_size
        for u in range(pack_size):
            whole = buf.at[place, u, pl.ds(0, width)]
            pltpu.make_async_copy(whole, whole, sems.at[place, u]).wait()
        lane = lax.broadcasted_iota(jnp.int32, (HEAD_WIDTH, LANES), 1)
        part = lane // span
        lane_head = (lane % heads) // GROUP
        one = lax.broadcasted_iota(jnp.int32, (1, LANES), 1)
        limit = jnp.zeros((1, LANES), jnp.int32)
        owner = jnp.zeros((1, LANES), jnp.int32)
        rows, kvs, rights = [], [], []
        for u in range(pack_size):
            r = order_ref[0, step * pack_size + u]
            rows.append(r)
            q = q_ref[:, pl.ds(pl.multiple_of((r // pack_size) * LANES, LANES), LANES)].astype(jnp.float32)
            own = part == u
            rights.append(
                jnp.concatenate(
                    [jnp.where(own & (lane_head == g), q, 0.0).astype(jnp.bfloat16) for g in range(heads_kv)], axis=0
                )
            )
            kvs.append(buf[place, u, 0:width, :])
            limit = jnp.where(one // span == u, 2 * lengths_ref[r], limit)
            owner = jnp.where(one // span == u, r & (NEW_GROUP - 1), owner)
        group = rows[0] // NEW_GROUP
        new = new_ref[pl.ds(pl.multiple_of(group * 128, 128), 128), :]
        s = dot(jnp.concatenate(kvs, axis=1), jnp.concatenate(rights, axis=0))
        sn = dot(new, functools.reduce(jnp.add, rights))
        row = lax.broadcasted_iota(jnp.int32, (width, LANES), 0)
        s = jnp.where(((row & 1) == 0) & (row < limit), s * scale, -jnp.inf)
        row = lax.broadcasted_iota(jnp.int32, sn.shape, 0)
        step_of = (one % span) // heads
        seen = ((row & 1) == 0) & (row // new_rows == owner) & ((row % new_rows) // 2 <= step_of)
        sn = jnp.where(seen, sn * scale, -jnp.inf)
        top = jnp.maximum(jnp.max(s, axis=0, keepdims=True), jnp.max(sn, axis=0, keepdims=True))
        w = jnp.exp2(s - top)
        wn = jnp.exp2(sn - top)
        inverse = 1.0 / (jnp.sum(w, axis=0, keepdims=True) + jnp.sum(wn, axis=0, keepdims=True))
        p = jnp.transpose(pltpu.roll(w * inverse, 1, 0)).astype(jnp.bfloat16)
        pn = jnp.transpose(pltpu.roll(wn * inverse, 1, 0)).astype(jnp.bfloat16)
        head = (lax.broadcasted_iota(jnp.int32, (span, HEAD_WIDTH), 0) % heads) // GROUP
        for u in range(pack_size):
            at = slice(u * span, (u + 1) * span)
            full = dot(p[at], kvs[u]) + dot(pn[at], new)
            o = full[:, :HEAD_WIDTH]
            for g in range(1, heads_kv):
                o = jnp.where(head == g, full[:, g * HEAD_WIDTH : (g + 1) * HEAD_WIDTH], o)
            token = rows[u] * STEP_COUNT
            for t in range(STEP_COUNT):
                acc[pl.ds(token + t, heads, stride=tokens), :] = o[t * heads : (t + 1) * heads]

    @pl.loop(0, steps)
    def _(step):
        @pl.when(step + (SLOTS - 1) < steps)
        def _():
            fetch(step + (SLOTS - 1))

        count = most_chunks(step)
        for n in range(1, CHUNKS + 1):

            @pl.when(count == n)
            def _():
                compute(step, n)

    for h in range(heads):
        out_ref[:, h * HEAD_WIDTH : (h + 1) * HEAD_WIDTH] = acc[h * tokens : (h + 1) * tokens].astype(jnp.bfloat16)


def attend(order, lengths, table, q, new, pages, inbox):
    per_dev, _, _, columns = pages.shape
    req_count = inbox.shape[0]
    requests = lengths.shape[0]
    heads = columns // HEAD_WIDTH * GROUP
    tokens = requests * STEP_COUNT
    pack_size = LANES // (STEP_COUNT * heads)
    extent = MAXP * PAGE_LENGTH * 2
    return pl.pallas_call(
        functools.partial(attend_kernel, req_count, per_dev, requests),
        out_shape=jax.ShapeDtypeStruct((tokens, heads * HEAD_WIDTH), jnp.bfloat16),
        in_specs=[SMEM, SMEM, SMEM, VMEM, VMEM, HBM, ANY],
        out_specs=VMEM,
        scratch_shapes=[
            pltpu.SMEM(table.shape, jnp.int32),
            pltpu.VMEM((req_count, 1, 2, columns), jnp.bfloat16),
            pltpu.VMEM((req_count, 128), jnp.int32),
            pltpu.SMEM((req_count, 128), jnp.int32),
            pltpu.VMEM((SLOTS, pack_size, extent, columns), jnp.bfloat16),
            pltpu.VMEM((heads * tokens, HEAD_WIDTH), jnp.float32),
            pltpu.SemaphoreType.DMA,
            pltpu.SemaphoreType.DMA((SLOTS, pack_size)),
        ],
        compiler_params=params(ATTEND_VMEM),
        cost_estimate=pl.CostEstimate(
            flops=16 * tokens * heads * HEAD_WIDTH * MAXP * PAGE_LENGTH,
            bytes_accessed=requests * extent * columns * 2,
            transcendentals=2 * tokens * heads * MAXP * PAGE_LENGTH,
        ),
        name="attend",
    )(order, lengths, table, q, new, pages, inbox)


def split_kernel(x_ref, o_ref, sems):
    parts, _, block = o_ref.shape
    copies = [
        pltpu.make_async_copy(x_ref.at[:, pl.ds(i * block, block)], o_ref.at[i], sems.at[i]) for i in range(parts)
    ]
    for copy in copies:
        copy.start()
    for copy in copies:
        copy.wait()


def split_columns(x, parts):
    rows, columns = x.shape
    return pl.pallas_call(
        split_kernel,
        out_shape=jax.ShapeDtypeStruct((parts, rows, columns // parts), x.dtype),
        in_specs=[HBM],
        out_specs=VMEM,
        scratch_shapes=[pltpu.SemaphoreType.DMA((parts,))],
        compiler_params=params(),
        cost_estimate=SMALL,
        name="split_columns",
    )(x)


def collect_kernel(count, roles, where_ref, *refs):
    xs, (down_ref, mask_ref), (x_ref, *lows) = refs[:count], refs[count : count + 2], refs[count + 2 :]
    tokens = xs[0].shape[0]
    rows = count * tokens // roles
    per_role = count // roles
    for b in range(count):
        at = where_ref[b]
        if roles == 4:
            at = (at // per_role ^ where_ref[count]) * per_role + at % per_role
        x_ref[pl.ds(pl.multiple_of(at * tokens, tokens), tokens), :] = xs[b][...]
    for j in range(roles):
        s = where_ref[count + j]
        at = j if roles == 4 else s
        x = x_ref[pl.ds(pl.multiple_of(at * rows, rows), rows), :]
        lows[j][...] = (dot(x, down_ref[...], ((1,), (1,))) * mask_ref[s].astype(jnp.float32)).astype(jnp.bfloat16)


def collect(where, xs, down, mask, roles):
    count = len(xs)
    tokens, width = xs[0].shape
    rows = count * tokens // roles
    x, *lows = pl.pallas_call(
        functools.partial(collect_kernel, count, roles),
        out_shape=[jax.ShapeDtypeStruct((count * tokens, width), jnp.bfloat16)]
        + [jax.ShapeDtypeStruct((rows, down.shape[0]), jnp.bfloat16)] * roles,
        in_specs=[SMEM] + [VMEM] * (count + 2),
        out_specs=[VMEM] * (1 + roles),
        compiler_params=params(),
        cost_estimate=SMALL,
        name="collect",
    )(where, *xs, down, mask)
    return x, lows


def project_kernel(roles, tile, x_ref, w_ref, *outs):
    rows = x_ref.shape[0] // roles

    @pl.loop(0, w_ref.shape[1] // tile)
    def _(i):
        at = pl.ds(pl.multiple_of(i * tile, tile), tile)
        y = dot(x_ref[...], w_ref[:, at]).astype(jnp.bfloat16)
        parts = [y[j * rows : (j + 1) * rows, :] for j in range(roles)]
        if roles == 4:
            own, pair, two, three = outs
            own[:, at] = parts[0]
            pair[0, :, at] = parts[1]
            pair[1, :, at] = parts[3]
            two[:, at] = parts[2]
            three[:, at] = parts[3]
        else:
            for j in range(roles):
                outs[0][j, :, at] = parts[j]


def project(x, w, roles):
    columns = w.shape[1]
    rows = x.shape[0] // roles
    one = jax.ShapeDtypeStruct((rows, columns), jnp.bfloat16)
    if roles == 4:
        outs = [one, jax.ShapeDtypeStruct((2, rows, columns), jnp.bfloat16), one, one]
    else:
        outs = [jax.ShapeDtypeStruct((roles, rows, columns), jnp.bfloat16)]
    return pl.pallas_call(
        functools.partial(project_kernel, roles, min(256, columns)),
        out_shape=outs,
        in_specs=[VMEM, VMEM],
        out_specs=[VMEM] * len(outs),
        compiler_params=params(),
        cost_estimate=SMALL,
        name="project",
    )(x, w)


def add_kernel(lane_ref, own_ref, passed_ref, o_ref):
    middle = (lane_ref[0] == 1) | (lane_ref[0] == 2)

    @pl.when(middle)
    def _():
        o_ref[...] = (own_ref[...].astype(jnp.float32) + passed_ref[1].astype(jnp.float32)).astype(jnp.bfloat16)

    @pl.when(jnp.logical_not(middle))
    def _():
        o_ref[...] = own_ref[...]


def add(lane, own, passed):
    return pl.pallas_call(
        add_kernel,
        out_shape=jax.ShapeDtypeStruct(own.shape, own.dtype),
        in_specs=[SMEM, VMEM, VMEM],
        out_specs=VMEM,
        compiler_params=params(),
        cost_estimate=SMALL,
        name="add",
    )(lane, own, passed)


def adapt_kernel(low_ref, up_ref, o_ref):
    low = jnp.concatenate([low_ref[a] for a in range(low_ref.shape[0])], axis=1)
    o_ref[...] = dot(low, up_ref[...])


def adapt(low, up):
    return pl.pallas_call(
        adapt_kernel,
        out_shape=jax.ShapeDtypeStruct((low.shape[1], up.shape[1]), jnp.float32),
        in_specs=[VMEM, VMEM],
        out_specs=VMEM,
        compiler_params=params(),
        cost_estimate=SMALL,
        name="adapt",
    )(low, up)


def finish_kernel(every, extra_ref, *refs):
    terms, o_ref = refs[:-1], refs[-1]
    total = extra_ref[...]
    for term in terms:
        if len(term.shape) == 2:
            total = total + term[...].astype(jnp.float32)
        else:
            for j in range(term.shape[0] if every else 1):
                total = total + term[j].astype(jnp.float32)
    o_ref[...] = total.astype(jnp.bfloat16)


def finish(terms, every, extra):
    return pl.pallas_call(
        functools.partial(finish_kernel, every),
        out_shape=jax.ShapeDtypeStruct(extra.shape, jnp.bfloat16),
        in_specs=[VMEM] * (1 + len(terms)),
        out_specs=VMEM,
        compiler_params=params(),
        cost_estimate=SMALL,
        name="finish",
    )(extra, *terms)


def exchange(x, axis, distance):
    count = lax.axis_size(axis)
    return lax.ppermute(x, axis, [(i, i ^ distance) for i in range(count)])


def after(x, *others):
    return lax.optimization_barrier((x, *others))[0]


def gather(x):
    my_req = lax.axis_index("req").astype(jnp.int32)
    count = lax.axis_size("req")
    if count != 8:
        whole = lax.all_gather(x, "req", axis=0)
        return [whole[b] for b in range(count)], [jnp.int32(b) for b in range(count)]
    held = [x] + [exchange(x, "req", d) for d in (2, 4, 6)]
    near = [exchange(block, "req", 1) for block in held]
    return held + near, [my_req ^ d for d in (0, 2, 4, 6, 1, 3, 5, 7)]


def scatter(parts):
    if len(parts) == 1:
        return [lax.all_to_all(parts[0], "tp", split_axis=0, concat_axis=0, tiled=True)], parts[0]
    own, pair, two, three = parts
    lane = lax.axis_index("tp").astype(jnp.int32).reshape(1)
    pair = exchange(pair, "tp", 1)
    middle = lax.ppermute(three, "tp", [(1, 2), (2, 1)])
    passed = add(lane, after(two, middle), pair)
    return [own, pair, middle, exchange(passed, "tp", 2)], middle


def on_device(
    queries,
    incoming_key_value,
    key_value_pages,
    page_request_home,
    lengths,
    request_adapter_index,
    adapter_storage_slot,
    adapter_down_factor,
    adapter_up_factor,
    output_projection_weight,
):
    req_count = lax.axis_size("req")
    tp_count = lax.axis_size("tp")
    my_req = lax.axis_index("req").astype(jnp.int32)
    my_lane = lax.axis_index("tp").astype(jnp.int32)
    me = my_req.reshape(1)
    requests = lengths.shape[0]
    columns = key_value_pages.shape[-1]
    heads = columns // HEAD_WIDTH * GROUP
    own_slots, rank, model = adapter_up_factor.shape

    outbox = pack(me, page_request_home, request_adapter_index, key_value_pages, req_count)
    inbox = lax.all_to_all(outbox, "req", split_axis=0, concat_axis=0, tiled=True)

    table, order = build_table(me, page_request_home, lengths, LANES // (STEP_COUNT * heads))
    q = queries.reshape(requests * STEP_COUNT * heads, HEAD_WIDTH).T
    up_blocks = split_columns(adapter_up_factor.reshape(own_slots * rank, model), req_count)
    new = incoming_key_value.transpose(1, 0, 2).reshape(-1, columns)
    down = adapter_down_factor.transpose(0, 2, 1).reshape(own_slots * rank, -1)

    up = lax.all_to_all(up_blocks, "req", split_axis=0, concat_axis=0, tiled=True)
    up = up.reshape(req_count * own_slots * rank, -1)
    slot_count = adapter_storage_slot.shape[0]
    ids = inbox[:, BLOCK - 1, 0, :requests].astype(jnp.int32)
    match = ids[:, :, None] == jnp.arange(slot_count, dtype=jnp.int32)
    slot = jnp.sum(jnp.where(match, adapter_storage_slot, 0), axis=2)
    mine = my_req * own_slots + jnp.arange(own_slots * rank, dtype=jnp.int32) // rank

    roles = [my_lane ^ j for j in range(tp_count)]
    mixed = attend(order, lengths, table, q, new, key_value_pages, inbox)
    blocks, origins = gather(mixed)
    where = jnp.stack(origins + roles)
    token_slot = jnp.repeat(slot, STEP_COUNT, axis=1)
    mask = (token_slot.reshape(tp_count, -1)[:, :, None] == mine).astype(jnp.bfloat16)
    up = lax.all_to_all(after(up_blocks, table, q, new), "req", split_axis=0, concat_axis=0, tiled=True)
    up = up.reshape(req_count * own_slots * rank, -1)
    mask = after(mask, up)
    x, lows = collect(where, blocks, down, mask, tp_count)
    parts = project(x, output_projection_weight, tp_count)
    terms, moved = scatter(parts)
    low = [lows[0]] + [exchange(lows[j], "tp", j) for j in range(1, tp_count)]
    low = functools.reduce(jnp.add, [term.astype(jnp.float32) for term in low]).astype(jnp.bfloat16)
    low = lax.all_gather(after(low, moved), "req", axis=0)
    return finish(terms, tp_count != 4, adapt(low, up))


def solution(mesh):
    return jax.shard_map(
        on_device,
        mesh=mesh,
        in_specs=(
            P("req", "tp"),
            P(None, "req", "tp"),
            P("req", None, None, "tp"),
            P("req"),
            P("req"),
            P("req"),
            P(),
            P("req", "tp", None),
            P("req", None, None),
            P("tp", "req"),
        ),
        out_specs=P("tp", "req"),
        check_vma=False,
    )
```

```python
import functools
import math

import jax
import jax.numpy as jnp
from jax import lax
from jax.experimental import pallas as pl
from jax.experimental.pallas import tpu as pltpu
from jax.sharding import PartitionSpec as P

QUERY_HEADS = 64
KEY_VALUE_HEADS = 8
GROUP = QUERY_HEADS // KEY_VALUE_HEADS
HEAD_WIDTH = 128
STEP_COUNT = 4
PAGE_LENGTH = 32
MAXP = 16
CAP = 2
BLOCK = CAP * PAGE_LENGTH + 1
LABEL_LANE = 64
DIGIT = 16
CHUNK_PAGES = 4
CHUNKS = MAXP // CHUNK_PAGES
CHUNK_POSITIONS = CHUNK_PAGES * PAGE_LENGTH
LANES = 128
PARTS = 2
NEW_GROUP = 128 // (2 * STEP_COUNT)
SLOTS = 6
VMEM_LIMIT = 24 * 1024 * 1024
WHOLE_VMEM = 60 * 1024 * 1024
ATTEND_VMEM = 48 * 1024 * 1024

SMALL = pl.CostEstimate(flops=1, bytes_accessed=1, transcendentals=0)

ANY = pl.BlockSpec(memory_space=pl.ANY)
HBM = pl.BlockSpec(memory_space=pltpu.HBM)
VMEM = pl.BlockSpec(memory_space=pltpu.VMEM)
SMEM = pl.BlockSpec(memory_space=pltpu.SMEM)


def params(limit=VMEM_LIMIT):
    return pltpu.CompilerParams(vmem_limit_bytes=limit)


def dot(a, b, contract=((1,), (0,))):
    return lax.dot_general(a, b, (contract, ((), ())), preferred_element_type=jnp.float32)


def pack_kernel(req_count, per_dev, me_ref, home_ref, ids_ref, pages, outbox, info_v, info_s, ids_v, rows_v, sem, sems):
    me = me_ref[0]
    page = lax.broadcasted_iota(jnp.int32, (req_count, per_dev), 1)
    want = lax.broadcasted_iota(jnp.int32, (req_count, per_dev), 0)
    slots = jnp.broadcast_to(home_ref[...], (req_count, per_dev)) - want * per_dev
    hit = (slots >= 0) & (slots < per_dev) & (want != me)
    lane = lax.broadcasted_iota(jnp.int32, (req_count, 128), 1)
    info = jnp.full((req_count, 128), -1, jnp.int32)
    for k in range(CAP):
        first = jnp.min(jnp.where(hit, page, per_dev), axis=1, keepdims=True)
        here = hit & (page == first)
        slot = jnp.max(jnp.where(here, slots, -1), axis=1, keepdims=True)
        info = jnp.where(lane == k, first, info)
        info = jnp.where(lane == CAP + k, slot, info)
        hit = hit & (page != first)
    info_v[...] = info
    fetch = pltpu.make_async_copy(info_v, info_s, sem)
    fetch.start()
    ids_v[...] = jnp.zeros_like(ids_v)
    ids_v[:, 0:ids_ref.shape[1]] = ids_ref[...].astype(jnp.float32)
    ids = jnp.broadcast_to(ids_v[...], (2, 128))
    fetch.wait()

    def copy(d, k):
        return pltpu.make_async_copy(
            pages.at[info_s[d, k]],
            outbox.at[d, pl.ds(k * PAGE_LENGTH, PAGE_LENGTH)],
            sems.at[d, k],
        )

    for d in range(req_count):
        for k in range(CAP):

            @pl.when(info_s[d, k] < per_dev)
            def _():
                copy(d, k).start()

    at = lax.broadcasted_iota(jnp.int32, (2, 128), 1)
    row = lax.broadcasted_iota(jnp.int32, (2, 128), 0)
    for d in range(req_count):
        value = jnp.where(row == 0, ids, 0.0)
        for k in range(CAP):
            slot = info_s[d, CAP + k]
            high = ((slot + DIGIT) >> 4) - 1
            low = slot - high * DIGIT
            digit = jnp.where(row == 0, high, low).astype(jnp.float32)
            value = jnp.where(at == LABEL_LANE + k, digit, value)
        rows_v[d, 0, :, :] = jnp.zeros(rows_v.shape[2:], jnp.bfloat16)
        rows_v[d, 0, :, 0:128] = value.astype(jnp.bfloat16)
    rows = pltpu.make_async_copy(rows_v, outbox.at[:, pl.ds(BLOCK - 1, 1)], sem)
    rows.start()
    rows.wait()
    for d in range(req_count):
        for k in range(CAP):

            @pl.when(info_s[d, k] < per_dev)
            def _():
                copy(d, k).wait()


def pack(me, page_request_home, ids, key_value_pages, req_count):
    per_dev = key_value_pages.shape[0]
    columns = key_value_pages.shape[-1]
    return pl.pallas_call(
        functools.partial(pack_kernel, req_count, per_dev),
        out_shape=jax.ShapeDtypeStruct((req_count, BLOCK, 2, columns), jnp.bfloat16),
        in_specs=[SMEM, VMEM, VMEM, HBM],
        out_specs=VMEM,
        scratch_shapes=[
            pltpu.VMEM((req_count, 128), jnp.int32),
            pltpu.SMEM((req_count, 128), jnp.int32),
            pltpu.VMEM((1, 128), jnp.float32),
            pltpu.VMEM((req_count, 1, 2, columns), jnp.bfloat16),
            pltpu.SemaphoreType.DMA,
            pltpu.SemaphoreType.DMA((req_count, CAP)),
        ],
        compiler_params=params(WHOLE_VMEM),
        cost_estimate=SMALL,
        name="pack_outbox",
    )(me, page_request_home.reshape(1, per_dev), ids.reshape(1, -1), key_value_pages)


def table_kernel(per_dev, requests, pack_size, me_ref, home_ref, lengths_ref, table_ref, order_ref, len_v):
    base = me_ref[0] * per_dev
    lane = lax.broadcasted_iota(jnp.int32, (128, 128), 1)
    row = lax.broadcasted_iota(jnp.int32, (128, 128), 0)
    tiles = per_dev // 128
    columns = [
        jnp.transpose(jnp.broadcast_to(home_ref[i : i + 1, :] - base, (128, 128)).astype(jnp.float32))
        for i in range(tiles)
    ]
    for j in range(tiles):
        total = jnp.zeros((128, 128), jnp.float32)
        slot = (lane + j * 128).astype(jnp.float32)
        for i in range(tiles):
            total = total + jnp.where(columns[i] == slot, (row + i * 128).astype(jnp.float32), 0.0)
        table_ref[j : j + 1, :] = jnp.sum(total, axis=0, keepdims=True).astype(jnp.int32)
    half = NEW_GROUP
    len_v[...] = jnp.zeros_like(len_v)
    len_v[:, 0:requests] = lengths_ref[...].astype(jnp.float32)
    along = jnp.broadcast_to(len_v[...], (128, 128))
    along = ((along.astype(jnp.int32) + (CHUNK_POSITIONS - 1)) >> 7).astype(jnp.float32)
    down = jnp.transpose(along)
    same = ((lane // half) == (row // half)) & (lane % pack_size == row % pack_size)
    before = same & ((along > down) | ((along == down) & (lane < row)))
    rank = jnp.sum(jnp.where(before, 1.0, 0.0), axis=1, keepdims=True)
    place = rank * pack_size + ((row // half) * half + row % pack_size).astype(jnp.float32)
    at = place == lane.astype(jnp.float32)
    order = jnp.sum(jnp.where(at, row.astype(jnp.float32), 0.0), axis=0, keepdims=True)
    chunks = jnp.sum(jnp.where(at, down, 0.0), axis=0, keepdims=True)
    order_ref[0:1, :] = order.astype(jnp.int32)
    order_ref[1:2, :] = chunks.astype(jnp.int32)


def build_table(me, page_request_home, lengths, pack_size):
    per_dev = page_request_home.shape[0]
    requests = lengths.shape[0]
    return pl.pallas_call(
        functools.partial(table_kernel, per_dev, requests, pack_size),
        out_shape=(
            jax.ShapeDtypeStruct((per_dev // 128, 128), jnp.int32),
            jax.ShapeDtypeStruct((2, 128), jnp.int32),
        ),
        in_specs=[SMEM, VMEM, VMEM],
        out_specs=(VMEM, VMEM),
        scratch_shapes=[pltpu.VMEM((1, 128), jnp.float32)],
        compiler_params=params(),
        cost_estimate=SMALL,
        name="page_table",
    )(me, page_request_home.reshape(per_dev // 128, 128), lengths.reshape(1, requests))


def attend_kernel(
    req_count,
    per_dev,
    requests,
    order_ref,
    lengths_ref,
    table_in,
    q_ref,
    new_ref,
    pages,
    inbox,
    out_ref,
    table,
    labels_v,
    labels_w,
    labels_s,
    buf,
    acc,
    sem,
    sems,
):
    columns = pages.shape[-1]
    heads_kv = columns // HEAD_WIDTH
    heads = heads_kv * GROUP
    span = STEP_COUNT * heads
    pack_size = LANES // span
    page_size = PAGE_LENGTH * 2
    chunk_size = CHUNK_PAGES * page_size
    new_rows = STEP_COUNT * 2
    tokens = requests * STEP_COUNT
    scale = math.log2(math.e) / math.sqrt(HEAD_WIDTH)
    page_rows = pages.reshape(per_dev, page_size, columns)
    inbox_rows = inbox.reshape(req_count, BLOCK * 2, columns)

    first = pltpu.make_async_copy(inbox.at[:, pl.ds(BLOCK - 1, 1)], labels_v, sem)
    first.start()
    first.wait()
    row = lax.broadcasted_iota(jnp.int32, (2, 128), 0)
    weight = jnp.where(row == 0, float(DIGIT), 1.0)
    for d in range(req_count):
        digits = labels_v[d, 0, :, 0:128].astype(jnp.float32) * weight
        labels_w[d : d + 1, :] = jnp.sum(digits, axis=0, keepdims=True).astype(jnp.int32)
    back = pltpu.make_async_copy(labels_w, labels_s, sem)
    back.start()

    @pl.loop(0, per_dev // 128)
    def _(i):
        @pl.loop(0, 128, unroll=8)
        def _(j):
            table[i, j] = table_in[i, j]

    back.wait()
    for d in range(req_count):
        for k in range(CAP):
            slot = labels_s[d, LABEL_LANE + k]

            @pl.when(slot >= 0)
            def _():
                table[lax.shift_right_logical(slot, 7), slot & 127] = per_dev + d * CAP + k

    steps = requests // pack_size

    def most_chunks(step):
        counts = [order_ref[1, step * pack_size + u] for u in range(pack_size)]
        return functools.reduce(jnp.maximum, counts)

    def page_count(step, u):
        length = lengths_ref[order_ref[0, step * pack_size + u]]
        return lax.shift_right_logical(length + (PAGE_LENGTH - 1), PAGE_LENGTH.bit_length() - 1)

    def fetch(step):
        place = lax.rem(step, SLOTS)
        for u in range(pack_size):
            slot = order_ref[0, step * pack_size + u] * MAXP
            line = lax.shift_right_logical(slot, 7)
            at = slot & 127

            def target(j):
                return buf.at[place, u, pl.ds(pl.multiple_of(j * page_size, page_size), page_size)]

            def copy(source, j):
                @pl.when(source < per_dev)
                def _():
                    pltpu.make_async_copy(page_rows.at[source], target(j), sems.at[place, u]).start()

                @pl.when(source >= per_dev)
                def _():
                    e = source - per_dev
                    d = lax.shift_right_logical(e, 1)
                    start = pl.multiple_of((e - d * CAP) * page_size, page_size)
                    pltpu.make_async_copy(
                        inbox_rows.at[d, pl.ds(start, page_size)], target(j), sems.at[place, u]
                    ).start()

            count = page_count(step, u)
            full = lax.shift_right_logical(count, 2)

            @pl.loop(0, full)
            def _(c):
                sources = [table[line, at + c * CHUNK_PAGES + j] for j in range(CHUNK_PAGES)]
                most = functools.reduce(jnp.maximum, sources)

                @pl.when(most < per_dev)
                def _():
                    for j in range(CHUNK_PAGES):
                        pltpu.make_async_copy(
                            page_rows.at[sources[j]], target(c * CHUNK_PAGES + j), sems.at[place, u]
                        ).start()

                @pl.when(most >= per_dev)
                def _():
                    for j in range(CHUNK_PAGES):
                        copy(sources[j], c * CHUNK_PAGES + j)

            @pl.loop(full * CHUNK_PAGES, count)
            def _(j):
                copy(table[line, at + j], j)

    for s in range(min(SLOTS - 1, steps)):
        fetch(jnp.int32(s))

    def compute(step, n):
        place = lax.rem(step, SLOTS)
        width = n * chunk_size
        for u in range(pack_size):
            one = buf.at[place, u, pl.ds(0, page_size)]
            count = page_count(step, u)

            @pl.loop(0, count)
            def _(_):
                pltpu.make_async_copy(one, one, sems.at[place, u]).wait()

            @pl.loop(count, n * CHUNK_PAGES)
            def _(j):
                buf[place, u, pl.ds(pl.multiple_of(j * page_size, page_size), page_size), :] = jnp.zeros(
                    (page_size, columns), jnp.bfloat16
                )

        lane = lax.broadcasted_iota(jnp.int32, (HEAD_WIDTH, LANES), 1)
        part = lane // span
        lane_head = (lane % heads) // GROUP
        one = lax.broadcasted_iota(jnp.int32, (1, LANES), 1)
        limit = jnp.zeros((1, LANES), jnp.int32)
        owner = jnp.zeros((1, LANES), jnp.int32)
        rows, kvs, rights = [], [], []
        for u in range(pack_size):
            r = order_ref[0, step * pack_size + u]
            rows.append(r)
            q = q_ref[:, pl.ds(pl.multiple_of((r // pack_size) * LANES, LANES), LANES)].astype(jnp.float32)
            own = part == u
            rights.append(
                jnp.concatenate(
                    [jnp.where(own & (lane_head == g), q, 0.0).astype(jnp.bfloat16) for g in range(heads_kv)], axis=0
                )
            )
            kvs.append(buf[place, u, 0:width, :])
            limit = jnp.where(one // span == u, 2 * lengths_ref[r], limit)
            owner = jnp.where(one // span == u, r & (NEW_GROUP - 1), owner)
        group = rows[0] // NEW_GROUP
        new = new_ref[pl.ds(pl.multiple_of(group * 128, 128), 128), :]
        s = dot(jnp.concatenate(kvs, axis=1), jnp.concatenate(rights, axis=0))
        sn = dot(new, functools.reduce(jnp.add, rights))
        row = lax.broadcasted_iota(jnp.int32, (width, LANES), 0)
        s = jnp.where(((row & 1) == 0) & (row < limit), s * scale, -jnp.inf)
        row = lax.broadcasted_iota(jnp.int32, sn.shape, 0)
        step_of = (one % span) // heads
        seen = ((row & 1) == 0) & (row // new_rows == owner) & ((row % new_rows) // 2 <= step_of)
        sn = jnp.where(seen, sn * scale, -jnp.inf)
        top = jnp.maximum(jnp.max(s, axis=0, keepdims=True), jnp.max(sn, axis=0, keepdims=True))
        w = jnp.exp2(s - top)
        wn = jnp.exp2(sn - top)
        inverse = 1.0 / (jnp.sum(w, axis=0, keepdims=True) + jnp.sum(wn, axis=0, keepdims=True))
        p = jnp.transpose(pltpu.roll(w * inverse, 1, 0)).astype(jnp.bfloat16)
        pn = jnp.transpose(pltpu.roll(wn * inverse, 1, 0)).astype(jnp.bfloat16)
        head = (lax.broadcasted_iota(jnp.int32, (span, HEAD_WIDTH), 0) % heads) // GROUP
        for u in range(pack_size):
            at = slice(u * span, (u + 1) * span)
            full = dot(p[at], kvs[u]) + dot(pn[at], new)
            o = full[:, :HEAD_WIDTH]
            for g in range(1, heads_kv):
                o = jnp.where(head == g, full[:, g * HEAD_WIDTH : (g + 1) * HEAD_WIDTH], o)
            token = rows[u] * STEP_COUNT
            for t in range(STEP_COUNT):
                acc[pl.ds(token + t, heads, stride=tokens), :] = o[t * heads : (t + 1) * heads]

    @pl.loop(0, steps)
    def _(step):
        @pl.when(step + (SLOTS - 1) < steps)
        def _():
            fetch(step + (SLOTS - 1))

        count = most_chunks(step)
        for n in range(1, CHUNKS + 1):

            @pl.when(count == n)
            def _():
                compute(step, n)

    for h in range(heads):
        out_ref[:, h * HEAD_WIDTH : (h + 1) * HEAD_WIDTH] = acc[h * tokens : (h + 1) * tokens].astype(jnp.bfloat16)


def attend(order, lengths, table, q, new, pages, inbox):
    per_dev, _, _, columns = pages.shape
    req_count = inbox.shape[0]
    requests = lengths.shape[0]
    heads = columns // HEAD_WIDTH * GROUP
    tokens = requests * STEP_COUNT
    pack_size = LANES // (STEP_COUNT * heads)
    extent = MAXP * PAGE_LENGTH * 2
    return pl.pallas_call(
        functools.partial(attend_kernel, req_count, per_dev, requests),
        out_shape=jax.ShapeDtypeStruct((tokens, heads * HEAD_WIDTH), jnp.bfloat16),
        in_specs=[SMEM, SMEM, SMEM, VMEM, VMEM, HBM, ANY],
        out_specs=VMEM,
        scratch_shapes=[
            pltpu.SMEM(table.shape, jnp.int32),
            pltpu.VMEM((req_count, 1, 2, columns), jnp.bfloat16),
            pltpu.VMEM((req_count, 128), jnp.int32),
            pltpu.SMEM((req_count, 128), jnp.int32),
            pltpu.VMEM((SLOTS, pack_size, extent, columns), jnp.bfloat16),
            pltpu.VMEM((heads * tokens, HEAD_WIDTH), jnp.float32),
            pltpu.SemaphoreType.DMA,
            pltpu.SemaphoreType.DMA((SLOTS, pack_size)),
        ],
        compiler_params=params(ATTEND_VMEM),
        cost_estimate=pl.CostEstimate(
            flops=16 * tokens * heads * HEAD_WIDTH * MAXP * PAGE_LENGTH,
            bytes_accessed=requests * extent * columns * 2,
            transcendentals=2 * tokens * heads * MAXP * PAGE_LENGTH,
        ),
        name="attend",
    )(order, lengths, table, q, new, pages, inbox)


def split_kernel(x_ref, o_ref, sems):
    parts, _, block = o_ref.shape
    copies = [
        pltpu.make_async_copy(x_ref.at[:, pl.ds(i * block, block)], o_ref.at[i], sems.at[i]) for i in range(parts)
    ]
    for copy in copies:
        copy.start()
    for copy in copies:
        copy.wait()


def split_columns(x, parts):
    rows, columns = x.shape
    return pl.pallas_call(
        split_kernel,
        out_shape=jax.ShapeDtypeStruct((parts, rows, columns // parts), x.dtype),
        in_specs=[HBM],
        out_specs=VMEM,
        scratch_shapes=[pltpu.SemaphoreType.DMA((parts,))],
        compiler_params=params(),
        cost_estimate=SMALL,
        name="split_columns",
    )(x)


def collect_kernel(count, roles, where_ref, *refs):
    xs, (down_ref, mask_ref), (x_ref, *lows) = refs[:count], refs[count : count + 2], refs[count + 2 :]
    tokens = xs[0].shape[0]
    rows = count * tokens // roles
    per_role = count // roles
    for b in range(count):
        at = where_ref[b]
        if roles == 4:
            at = (at // per_role ^ where_ref[count]) * per_role + at % per_role
        x_ref[pl.ds(pl.multiple_of(at * tokens, tokens), tokens), :] = xs[b][...]
    for j in range(roles):
        s = where_ref[count + j]
        at = j if roles == 4 else s
        x = x_ref[pl.ds(pl.multiple_of(at * rows, rows), rows), :]
        lows[j][...] = (dot(x, down_ref[...], ((1,), (1,))) * mask_ref[s].astype(jnp.float32)).astype(jnp.bfloat16)


def collect(where, xs, down, mask, roles):
    count = len(xs)
    tokens, width = xs[0].shape
    rows = count * tokens // roles
    x, *lows = pl.pallas_call(
        functools.partial(collect_kernel, count, roles),
        out_shape=[jax.ShapeDtypeStruct((count * tokens, width), jnp.bfloat16)]
        + [jax.ShapeDtypeStruct((rows, down.shape[0]), jnp.bfloat16)] * roles,
        in_specs=[SMEM] + [VMEM] * (count + 2),
        out_specs=[VMEM] * (1 + roles),
        compiler_params=params(),
        cost_estimate=SMALL,
        name="collect",
    )(where, *xs, down, mask)
    return x, lows


def project_kernel(roles, tile, x_ref, w_ref, *outs):
    rows = x_ref.shape[0] // roles
    columns = w_ref.shape[1]
    count = PARTS if roles == 4 else 1
    width = columns // count
    for c in range(count):

        @pl.loop(0, width // tile)
        def _(i):
            inner = pl.ds(pl.multiple_of(i * tile, tile), tile)
            at = pl.ds(pl.multiple_of(c * width + i * tile, tile), tile)
            y = dot(x_ref[...], w_ref[:, at]).astype(jnp.bfloat16)
            parts = [y[j * rows : (j + 1) * rows, :] for j in range(roles)]
            if roles == 4:
                own, three, pair, two = outs[0], outs[1], outs[2 + c], outs[2 + count + c]
                own[:, at] = parts[0]
                three[:, at] = parts[3]
                pair[0, :, inner] = parts[1]
                pair[1, :, inner] = parts[3]
                two[:, inner] = parts[2]
            else:
                for j in range(roles):
                    outs[0][j, :, at] = parts[j]


def project(x, w, roles):
    columns = w.shape[1]
    rows = x.shape[0] // roles
    if roles == 4:
        one = jax.ShapeDtypeStruct((rows, columns), jnp.bfloat16)
        outs = [one, one]
        outs = outs + [jax.ShapeDtypeStruct((2, rows, columns // PARTS), jnp.bfloat16)] * PARTS
        outs = outs + [jax.ShapeDtypeStruct((rows, columns // PARTS), jnp.bfloat16)] * PARTS
    else:
        outs = [jax.ShapeDtypeStruct((roles, rows, columns), jnp.bfloat16)]
    return pl.pallas_call(
        functools.partial(project_kernel, roles, min(256, columns)),
        out_shape=outs,
        in_specs=[VMEM, VMEM],
        out_specs=[VMEM] * len(outs),
        compiler_params=params(),
        cost_estimate=SMALL,
        name="project",
    )(x, w)


def add_kernel(lane_ref, own_ref, passed_ref, o_ref):
    middle = (lane_ref[0] == 1) | (lane_ref[0] == 2)

    @pl.when(middle)
    def _():
        o_ref[...] = (own_ref[...].astype(jnp.float32) + passed_ref[1].astype(jnp.float32)).astype(jnp.bfloat16)

    @pl.when(jnp.logical_not(middle))
    def _():
        o_ref[...] = own_ref[...]


def add(lane, own, passed):
    return pl.pallas_call(
        add_kernel,
        out_shape=jax.ShapeDtypeStruct(own.shape, own.dtype),
        in_specs=[SMEM, VMEM, VMEM],
        out_specs=VMEM,
        compiler_params=params(),
        cost_estimate=SMALL,
        name="add",
    )(lane, own, passed)


def adapt_kernel(low_ref, up_ref, o_ref):
    low = jnp.concatenate([low_ref[a] for a in range(low_ref.shape[0])], axis=1)
    o_ref[...] = dot(low, up_ref[...])


def adapt(low, up):
    return pl.pallas_call(
        adapt_kernel,
        out_shape=jax.ShapeDtypeStruct((low.shape[1], up.shape[1]), jnp.float32),
        in_specs=[VMEM, VMEM],
        out_specs=VMEM,
        compiler_params=params(),
        cost_estimate=SMALL,
        name="adapt",
    )(low, up)


def finish_kernel(whole, extra_ref, *refs):
    terms, parts, o_ref = refs[:whole], refs[whole:-1], refs[-1]
    total = extra_ref[...]
    for term in terms:
        if len(term.shape) == 2:
            total = total + term[...].astype(jnp.float32)
        else:
            for j in range(term.shape[0]):
                total = total + term[j].astype(jnp.float32)
    if not parts:
        o_ref[...] = total.astype(jnp.bfloat16)
    width = total.shape[1] // PARTS
    for c in range(PARTS if parts else 0):
        at = slice(c * width, (c + 1) * width)
        piece = total[:, at]
        for term in parts[c::PARTS]:
            piece = piece + (term[...] if len(term.shape) == 2 else term[0]).astype(jnp.float32)
        o_ref[:, at] = piece.astype(jnp.bfloat16)


def finish(terms, parts, extra):
    return pl.pallas_call(
        functools.partial(finish_kernel, len(terms)),
        out_shape=jax.ShapeDtypeStruct(extra.shape, jnp.bfloat16),
        in_specs=[VMEM] * (1 + len(terms) + len(parts)),
        out_specs=VMEM,
        compiler_params=params(),
        cost_estimate=SMALL,
        name="finish",
    )(extra, *terms, *parts)


def exchange(x, axis, distance):
    count = lax.axis_size(axis)
    return lax.ppermute(x, axis, [(i, i ^ distance) for i in range(count)])


def after(x, *others):
    return lax.optimization_barrier((x, *others))[0]


def gather(x):
    my_req = lax.axis_index("req").astype(jnp.int32)
    count = lax.axis_size("req")
    if count != 8:
        whole = lax.all_gather(x, "req", axis=0)
        return [whole[b] for b in range(count)], [jnp.int32(b) for b in range(count)]
    held = [x] + [exchange(x, "req", d) for d in (2, 4, 6)]
    near = [exchange(block, "req", 1) for block in held]
    return held + near, [my_req ^ d for d in (0, 2, 4, 6, 1, 3, 5, 7)]


def scatter(made, low):
    if len(made) == 1:
        moved = lax.all_to_all(made[0], "tp", split_axis=0, concat_axis=0, tiled=True)
        return [moved], [], made[0]
    own, three, pairs, twos = made[0], made[1], made[2 : 2 + PARTS], made[2 + PARTS :]
    lane = lax.axis_index("tp").astype(jnp.int32).reshape(1)
    pairs = [exchange(after(pair, low), "tp", 1) for pair in pairs]
    middle = lax.ppermute(after(three, low), "tp", [(1, 2), (2, 1)])
    passed, gates = [], [middle]
    for pair, two in zip(pairs, twos):
        passed.append(exchange(add(lane, after(two, *gates), pair), "tp", 2))
        gates = [passed[-1]]
    return [own, middle], pairs + passed, middle


def on_device(
    queries,
    incoming_key_value,
    key_value_pages,
    page_request_home,
    lengths,
    request_adapter_index,
    adapter_storage_slot,
    adapter_down_factor,
    adapter_up_factor,
    output_projection_weight,
):
    req_count = lax.axis_size("req")
    tp_count = lax.axis_size("tp")
    my_req = lax.axis_index("req").astype(jnp.int32)
    my_lane = lax.axis_index("tp").astype(jnp.int32)
    me = my_req.reshape(1)
    requests = lengths.shape[0]
    columns = key_value_pages.shape[-1]
    heads = columns // HEAD_WIDTH * GROUP
    own_slots, rank, model = adapter_up_factor.shape

    outbox = pack(me, page_request_home, request_adapter_index, key_value_pages, req_count)
    inbox = lax.all_to_all(outbox, "req", split_axis=0, concat_axis=0, tiled=True)

    table, order = build_table(me, page_request_home, lengths, LANES // (STEP_COUNT * heads))
    q = queries.reshape(requests * STEP_COUNT * heads, HEAD_WIDTH).T
    up_blocks = split_columns(adapter_up_factor.reshape(own_slots * rank, model), req_count)
    new = incoming_key_value.transpose(1, 0, 2).reshape(-1, columns)
    down = adapter_down_factor.transpose(0, 2, 1).reshape(own_slots * rank, -1)

    up = lax.all_to_all(up_blocks, "req", split_axis=0, concat_axis=0, tiled=True)
    up = up.reshape(req_count * own_slots * rank, -1)
    slot_count = adapter_storage_slot.shape[0]
    ids = inbox[:, BLOCK - 1, 0, :requests].astype(jnp.int32)
    match = ids[:, :, None] == jnp.arange(slot_count, dtype=jnp.int32)
    slot = jnp.sum(jnp.where(match, adapter_storage_slot, 0), axis=2)
    mine = my_req * own_slots + jnp.arange(own_slots * rank, dtype=jnp.int32) // rank

    roles = [my_lane ^ j for j in range(tp_count)]
    mixed = attend(order, lengths, table, q, new, key_value_pages, inbox)
    blocks, origins = gather(mixed)
    where = jnp.stack(origins + roles)
    token_slot = jnp.repeat(slot, STEP_COUNT, axis=1)
    mask = (token_slot.reshape(tp_count, -1)[:, :, None] == mine).astype(jnp.bfloat16)
    up = lax.all_to_all(after(up_blocks, table, q, new), "req", split_axis=0, concat_axis=0, tiled=True)
    up = up.reshape(req_count * own_slots * rank, -1)
    mask = after(mask, up)
    x, lows = collect(where, blocks, down, mask, tp_count)
    low = [lows[0]] + [exchange(lows[j], "tp", j) for j in range(1, tp_count)]
    low = functools.reduce(jnp.add, [term.astype(jnp.float32) for term in low]).astype(jnp.bfloat16)
    terms, parts, moved = scatter(project(x, output_projection_weight, tp_count), low)
    low = lax.all_gather(after(low, moved), "req", axis=0)
    return finish(terms, parts, adapt(low, up))


def solution(mesh):
    return jax.shard_map(
        on_device,
        mesh=mesh,
        in_specs=(
            P("req", "tp"),
            P(None, "req", "tp"),
            P("req", None, None, "tp"),
            P("req"),
            P("req"),
            P("req"),
            P(),
            P("req", "tp", None),
            P("req", None, None),
            P("tp", "req"),
        ),
        out_specs=P("tp", "req"),
        check_vma=False,
    )
```

```python
import functools
import math

import jax
import jax.numpy as jnp
from jax import lax
from jax.experimental import pallas as pl
from jax.experimental.pallas import tpu as pltpu
from jax.sharding import PartitionSpec as P

QUERY_HEADS = 64
KEY_VALUE_HEADS = 8
GROUP = QUERY_HEADS // KEY_VALUE_HEADS
HEAD_WIDTH = 128
STEP_COUNT = 4
PAGE_LENGTH = 32
MAXP = 16
CAP = 2
BLOCK = CAP * PAGE_LENGTH + 1
LABEL_LANE = 64
DIGIT = 16
CHUNK_PAGES = 4
CHUNKS = MAXP // CHUNK_PAGES
CHUNK_POSITIONS = CHUNK_PAGES * PAGE_LENGTH
LANES = 128
PARTS = 2
NEW_GROUP = 128 // (2 * STEP_COUNT)
SLOTS = 4
PACKS = 2
VMEM_LIMIT = 24 * 1024 * 1024
WHOLE_VMEM = 60 * 1024 * 1024
ATTEND_VMEM = 48 * 1024 * 1024

SMALL = pl.CostEstimate(flops=1, bytes_accessed=1, transcendentals=0)

ANY = pl.BlockSpec(memory_space=pl.ANY)
HBM = pl.BlockSpec(memory_space=pltpu.HBM)
VMEM = pl.BlockSpec(memory_space=pltpu.VMEM)
SMEM = pl.BlockSpec(memory_space=pltpu.SMEM)


def params(limit=VMEM_LIMIT):
    return pltpu.CompilerParams(vmem_limit_bytes=limit)


def dot(a, b, contract=((1,), (0,))):
    return lax.dot_general(a, b, (contract, ((), ())), preferred_element_type=jnp.float32)


def pack_kernel(req_count, per_dev, me_ref, home_ref, ids_ref, pages, outbox, info_v, info_s, ids_v, rows_v, sem, sems):
    me = me_ref[0]
    page = lax.broadcasted_iota(jnp.int32, (req_count, per_dev), 1)
    want = lax.broadcasted_iota(jnp.int32, (req_count, per_dev), 0)
    slots = jnp.broadcast_to(home_ref[...], (req_count, per_dev)) - want * per_dev
    hit = (slots >= 0) & (slots < per_dev) & (want != me)
    lane = lax.broadcasted_iota(jnp.int32, (req_count, 128), 1)
    info = jnp.full((req_count, 128), -1, jnp.int32)
    for k in range(CAP):
        first = jnp.min(jnp.where(hit, page, per_dev), axis=1, keepdims=True)
        here = hit & (page == first)
        slot = jnp.max(jnp.where(here, slots, -1), axis=1, keepdims=True)
        info = jnp.where(lane == k, first, info)
        info = jnp.where(lane == CAP + k, slot, info)
        hit = hit & (page != first)
    info_v[...] = info
    fetch = pltpu.make_async_copy(info_v, info_s, sem)
    fetch.start()
    ids_v[...] = jnp.zeros_like(ids_v)
    ids_v[:, 0:ids_ref.shape[1]] = ids_ref[...].astype(jnp.float32)
    ids = jnp.broadcast_to(ids_v[...], (2, 128))
    fetch.wait()

    def copy(d, k):
        return pltpu.make_async_copy(
            pages.at[info_s[d, k]],
            outbox.at[d, pl.ds(k * PAGE_LENGTH, PAGE_LENGTH)],
            sems.at[d, k],
        )

    for d in range(req_count):
        for k in range(CAP):

            @pl.when(info_s[d, k] < per_dev)
            def _():
                copy(d, k).start()

    at = lax.broadcasted_iota(jnp.int32, (2, 128), 1)
    row = lax.broadcasted_iota(jnp.int32, (2, 128), 0)
    for d in range(req_count):
        value = jnp.where(row == 0, ids, 0.0)
        for k in range(CAP):
            slot = info_s[d, CAP + k]
            high = ((slot + DIGIT) >> 4) - 1
            low = slot - high * DIGIT
            digit = jnp.where(row == 0, high, low).astype(jnp.float32)
            value = jnp.where(at == LABEL_LANE + k, digit, value)
        rows_v[d, 0, :, :] = jnp.zeros(rows_v.shape[2:], jnp.bfloat16)
        rows_v[d, 0, :, 0:128] = value.astype(jnp.bfloat16)
    rows = pltpu.make_async_copy(rows_v, outbox.at[:, pl.ds(BLOCK - 1, 1)], sem)
    rows.start()
    rows.wait()
    for d in range(req_count):
        for k in range(CAP):

            @pl.when(info_s[d, k] < per_dev)
            def _():
                copy(d, k).wait()


def pack(me, page_request_home, ids, key_value_pages, req_count):
    per_dev = key_value_pages.shape[0]
    columns = key_value_pages.shape[-1]
    return pl.pallas_call(
        functools.partial(pack_kernel, req_count, per_dev),
        out_shape=jax.ShapeDtypeStruct((req_count, BLOCK, 2, columns), jnp.bfloat16),
        in_specs=[SMEM, VMEM, VMEM, HBM],
        out_specs=VMEM,
        scratch_shapes=[
            pltpu.VMEM((req_count, 128), jnp.int32),
            pltpu.SMEM((req_count, 128), jnp.int32),
            pltpu.VMEM((1, 128), jnp.float32),
            pltpu.VMEM((req_count, 1, 2, columns), jnp.bfloat16),
            pltpu.SemaphoreType.DMA,
            pltpu.SemaphoreType.DMA((req_count, CAP)),
        ],
        compiler_params=params(WHOLE_VMEM),
        cost_estimate=SMALL,
        name="pack_outbox",
    )(me, page_request_home.reshape(1, per_dev), ids.reshape(1, -1), key_value_pages)


def table_kernel(per_dev, requests, pack_size, me_ref, home_ref, lengths_ref, table_ref, order_ref, len_v):
    base = me_ref[0] * per_dev
    lane = lax.broadcasted_iota(jnp.int32, (128, 128), 1)
    row = lax.broadcasted_iota(jnp.int32, (128, 128), 0)
    tiles = per_dev // 128
    columns = [
        jnp.transpose(jnp.broadcast_to(home_ref[i : i + 1, :] - base, (128, 128)).astype(jnp.float32))
        for i in range(tiles)
    ]
    for j in range(tiles):
        total = jnp.zeros((128, 128), jnp.float32)
        slot = (lane + j * 128).astype(jnp.float32)
        for i in range(tiles):
            total = total + jnp.where(columns[i] == slot, (row + i * 128).astype(jnp.float32), 0.0)
        table_ref[j : j + 1, :] = jnp.sum(total, axis=0, keepdims=True).astype(jnp.int32)
    half = NEW_GROUP
    len_v[...] = jnp.zeros_like(len_v)
    len_v[:, 0:requests] = lengths_ref[...].astype(jnp.float32)
    along = jnp.broadcast_to(len_v[...], (128, 128))
    along = ((along.astype(jnp.int32) + (CHUNK_POSITIONS - 1)) >> 7).astype(jnp.float32)
    down = jnp.transpose(along)
    same = ((lane // half) == (row // half)) & (lane % pack_size == row % pack_size)
    before = same & ((along > down) | ((along == down) & (lane < row)))
    rank = jnp.sum(jnp.where(before, 1.0, 0.0), axis=1, keepdims=True)
    place = rank * pack_size + ((row // half) * half + row % pack_size).astype(jnp.float32)
    at = place == lane.astype(jnp.float32)
    order = jnp.sum(jnp.where(at, row.astype(jnp.float32), 0.0), axis=0, keepdims=True)
    chunks = jnp.sum(jnp.where(at, down, 0.0), axis=0, keepdims=True)
    order_ref[0:1, :] = order.astype(jnp.int32)
    order_ref[1:2, :] = chunks.astype(jnp.int32)


def build_table(me, page_request_home, lengths, pack_size):
    per_dev = page_request_home.shape[0]
    requests = lengths.shape[0]
    return pl.pallas_call(
        functools.partial(table_kernel, per_dev, requests, pack_size),
        out_shape=(
            jax.ShapeDtypeStruct((per_dev // 128, 128), jnp.int32),
            jax.ShapeDtypeStruct((2, 128), jnp.int32),
        ),
        in_specs=[SMEM, VMEM, VMEM],
        out_specs=(VMEM, VMEM),
        scratch_shapes=[pltpu.VMEM((1, 128), jnp.float32)],
        compiler_params=params(),
        cost_estimate=SMALL,
        name="page_table",
    )(me, page_request_home.reshape(per_dev // 128, 128), lengths.reshape(1, requests))


def attend_kernel(
    req_count,
    per_dev,
    requests,
    order_ref,
    lengths_ref,
    table_in,
    q_ref,
    new_ref,
    pages,
    inbox,
    out_ref,
    table,
    labels_v,
    labels_w,
    labels_s,
    buf,
    acc,
    sem,
    sems,
):
    columns = pages.shape[-1]
    heads_kv = columns // HEAD_WIDTH
    heads = heads_kv * GROUP
    span = STEP_COUNT * heads
    pack_size = LANES // span
    page_size = PAGE_LENGTH * 2
    chunk_size = CHUNK_PAGES * page_size
    new_rows = STEP_COUNT * 2
    tokens = requests * STEP_COUNT
    scale = math.log2(math.e) / math.sqrt(HEAD_WIDTH)
    page_rows = pages.reshape(per_dev, page_size, columns)
    inbox_rows = inbox.reshape(req_count, BLOCK * 2, columns)

    first = pltpu.make_async_copy(inbox.at[:, pl.ds(BLOCK - 1, 1)], labels_v, sem)
    first.start()
    first.wait()
    row = lax.broadcasted_iota(jnp.int32, (2, 128), 0)
    weight = jnp.where(row == 0, float(DIGIT), 1.0)
    for d in range(req_count):
        digits = labels_v[d, 0, :, 0:128].astype(jnp.float32) * weight
        labels_w[d : d + 1, :] = jnp.sum(digits, axis=0, keepdims=True).astype(jnp.int32)
    back = pltpu.make_async_copy(labels_w, labels_s, sem)
    back.start()

    @pl.loop(0, per_dev // 128)
    def _(i):
        @pl.loop(0, 128, unroll=8)
        def _(j):
            table[i, j] = table_in[i, j]

    back.wait()
    for d in range(req_count):
        for k in range(CAP):
            slot = labels_s[d, LABEL_LANE + k]

            @pl.when(slot >= 0)
            def _():
                table[lax.shift_right_logical(slot, 7), slot & 127] = per_dev + d * CAP + k

    batch = PACKS * pack_size
    steps = requests // batch

    def most_chunks(step):
        counts = [order_ref[1, step * batch + u] for u in range(batch)]
        return functools.reduce(jnp.maximum, counts)

    def fetch(step):
        place = lax.rem(step, SLOTS)
        count = most_chunks(step)
        for u in range(batch):
            slot = order_ref[0, step * batch + u] * MAXP
            line = lax.shift_right_logical(slot, 7)
            at = slot & 127

            @pl.loop(0, count)
            def _(c):
                sources = [table[line, at + c * CHUNK_PAGES + j] for j in range(CHUNK_PAGES)]
                most = functools.reduce(jnp.maximum, sources)

                def target(j):
                    start = pl.multiple_of(c * chunk_size + j * page_size, page_size)
                    return buf.at[place, u, pl.ds(start, page_size)]

                @pl.when(most < per_dev)
                def _():
                    for j in range(CHUNK_PAGES):
                        pltpu.make_async_copy(page_rows.at[sources[j]], target(j), sems.at[place, u]).start()

                @pl.when(most >= per_dev)
                def _():
                    for j in range(CHUNK_PAGES):
                        source = sources[j]

                        @pl.when(source < per_dev)
                        def _():
                            pltpu.make_async_copy(page_rows.at[source], target(j), sems.at[place, u]).start()

                        @pl.when(source >= per_dev)
                        def _():
                            e = source - per_dev
                            d = lax.shift_right_logical(e, 1)
                            start = pl.multiple_of((e - d * CAP) * page_size, page_size)
                            pltpu.make_async_copy(
                                inbox_rows.at[d, pl.ds(start, page_size)], target(j), sems.at[place, u]
                            ).start()

    for s in range(min(SLOTS - 1, steps)):
        fetch(jnp.int32(s))

    def compute(step, n):
        place = lax.rem(step, SLOTS)
        width = n * chunk_size
        for u in range(batch):
            whole = buf.at[place, u, pl.ds(0, width)]
            pltpu.make_async_copy(whole, whole, sems.at[place, u]).wait()
        for v in range(PACKS):
            attend_pack(step, place, width, v)

    def attend_pack(step, place, width, v):
        lane = lax.broadcasted_iota(jnp.int32, (HEAD_WIDTH, LANES), 1)
        part = lane // span
        lane_head = (lane % heads) // GROUP
        one = lax.broadcasted_iota(jnp.int32, (1, LANES), 1)
        limit = jnp.zeros((1, LANES), jnp.int32)
        owner = jnp.zeros((1, LANES), jnp.int32)
        rows, kvs, rights = [], [], []
        for u in range(pack_size):
            r = order_ref[0, step * batch + v * pack_size + u]
            rows.append(r)
            q = q_ref[:, pl.ds(pl.multiple_of((r // pack_size) * LANES, LANES), LANES)].astype(jnp.float32)
            own = part == u
            rights.append(
                jnp.concatenate(
                    [jnp.where(own & (lane_head == g), q, 0.0).astype(jnp.bfloat16) for g in range(heads_kv)], axis=0
                )
            )
            kvs.append(buf[place, v * pack_size + u, 0:width, :])
            limit = jnp.where(one // span == u, 2 * lengths_ref[r], limit)
            owner = jnp.where(one // span == u, r & (NEW_GROUP - 1), owner)
        group = rows[0] // NEW_GROUP
        new = new_ref[pl.ds(pl.multiple_of(group * 128, 128), 128), :]
        s = dot(jnp.concatenate(kvs, axis=1), jnp.concatenate(rights, axis=0))
        sn = dot(new, functools.reduce(jnp.add, rights))
        row = lax.broadcasted_iota(jnp.int32, (width, LANES), 0)
        s = jnp.where(((row & 1) == 0) & (row < limit), s * scale, -jnp.inf)
        row = lax.broadcasted_iota(jnp.int32, sn.shape, 0)
        step_of = (one % span) // heads
        seen = ((row & 1) == 0) & (row // new_rows == owner) & ((row % new_rows) // 2 <= step_of)
        sn = jnp.where(seen, sn * scale, -jnp.inf)
        top = jnp.maximum(jnp.max(s, axis=0, keepdims=True), jnp.max(sn, axis=0, keepdims=True))
        w = jnp.exp2(s - top)
        wn = jnp.exp2(sn - top)
        inverse = 1.0 / (jnp.sum(w, axis=0, keepdims=True) + jnp.sum(wn, axis=0, keepdims=True))
        p = jnp.transpose(pltpu.roll(w * inverse, 1, 0)).astype(jnp.bfloat16)
        pn = jnp.transpose(pltpu.roll(wn * inverse, 1, 0)).astype(jnp.bfloat16)
        head = (lax.broadcasted_iota(jnp.int32, (span, HEAD_WIDTH), 0) % heads) // GROUP
        for u in range(pack_size):
            at = slice(u * span, (u + 1) * span)
            full = dot(p[at], kvs[u]) + dot(pn[at], new)
            o = full[:, :HEAD_WIDTH]
            for g in range(1, heads_kv):
                o = jnp.where(head == g, full[:, g * HEAD_WIDTH : (g + 1) * HEAD_WIDTH], o)
            token = rows[u] * STEP_COUNT
            for t in range(STEP_COUNT):
                acc[pl.ds(token + t, heads, stride=tokens), :] = o[t * heads : (t + 1) * heads]

    @pl.loop(0, steps)
    def _(step):
        @pl.when(step + (SLOTS - 1) < steps)
        def _():
            fetch(step + (SLOTS - 1))

        count = most_chunks(step)
        for n in range(1, CHUNKS + 1):

            @pl.when(count == n)
            def _():
                compute(step, n)

    for h in range(heads):
        out_ref[:, h * HEAD_WIDTH : (h + 1) * HEAD_WIDTH] = acc[h * tokens : (h + 1) * tokens].astype(jnp.bfloat16)


def attend(order, lengths, table, q, new, pages, inbox):
    per_dev, _, _, columns = pages.shape
    req_count = inbox.shape[0]
    requests = lengths.shape[0]
    heads = columns // HEAD_WIDTH * GROUP
    tokens = requests * STEP_COUNT
    pack_size = LANES // (STEP_COUNT * heads)
    extent = MAXP * PAGE_LENGTH * 2
    return pl.pallas_call(
        functools.partial(attend_kernel, req_count, per_dev, requests),
        out_shape=jax.ShapeDtypeStruct((tokens, heads * HEAD_WIDTH), jnp.bfloat16),
        in_specs=[SMEM, SMEM, SMEM, VMEM, VMEM, HBM, ANY],
        out_specs=VMEM,
        scratch_shapes=[
            pltpu.SMEM(table.shape, jnp.int32),
            pltpu.VMEM((req_count, 1, 2, columns), jnp.bfloat16),
            pltpu.VMEM((req_count, 128), jnp.int32),
            pltpu.SMEM((req_count, 128), jnp.int32),
            pltpu.VMEM((SLOTS, PACKS * pack_size, extent, columns), jnp.bfloat16),
            pltpu.VMEM((heads * tokens, HEAD_WIDTH), jnp.float32),
            pltpu.SemaphoreType.DMA,
            pltpu.SemaphoreType.DMA((SLOTS, PACKS * pack_size)),
        ],
        compiler_params=params(ATTEND_VMEM),
        cost_estimate=pl.CostEstimate(
            flops=16 * tokens * heads * HEAD_WIDTH * MAXP * PAGE_LENGTH,
            bytes_accessed=requests * extent * columns * 2,
            transcendentals=2 * tokens * heads * MAXP * PAGE_LENGTH,
        ),
        name="attend",
    )(order, lengths, table, q, new, pages, inbox)


def split_kernel(x_ref, o_ref, sems):
    parts, _, block = o_ref.shape
    copies = [
        pltpu.make_async_copy(x_ref.at[:, pl.ds(i * block, block)], o_ref.at[i], sems.at[i]) for i in range(parts)
    ]
    for copy in copies:
        copy.start()
    for copy in copies:
        copy.wait()


def split_columns(x, parts):
    rows, columns = x.shape
    return pl.pallas_call(
        split_kernel,
        out_shape=jax.ShapeDtypeStruct((parts, rows, columns // parts), x.dtype),
        in_specs=[HBM],
        out_specs=VMEM,
        scratch_shapes=[pltpu.SemaphoreType.DMA((parts,))],
        compiler_params=params(),
        cost_estimate=SMALL,
        name="split_columns",
    )(x)


def collect_kernel(count, roles, where_ref, *refs):
    xs, (down_ref, mask_ref), (x_ref, *lows) = refs[:count], refs[count : count + 2], refs[count + 2 :]
    tokens = xs[0].shape[0]
    rows = count * tokens // roles
    per_role = count // roles
    for b in range(count):
        at = where_ref[b]
        if roles == 4:
            at = (at // per_role ^ where_ref[count]) * per_role + at % per_role
        x_ref[pl.ds(pl.multiple_of(at * tokens, tokens), tokens), :] = xs[b][...]
    for j in range(roles):
        s = where_ref[count + j]
        at = j if roles == 4 else s
        x = x_ref[pl.ds(pl.multiple_of(at * rows, rows), rows), :]
        lows[j][...] = (dot(x, down_ref[...], ((1,), (1,))) * mask_ref[s].astype(jnp.float32)).astype(jnp.bfloat16)


def collect(where, xs, down, mask, roles):
    count = len(xs)
    tokens, width = xs[0].shape
    rows = count * tokens // roles
    x, *lows = pl.pallas_call(
        functools.partial(collect_kernel, count, roles),
        out_shape=[jax.ShapeDtypeStruct((count * tokens, width), jnp.bfloat16)]
        + [jax.ShapeDtypeStruct((rows, down.shape[0]), jnp.bfloat16)] * roles,
        in_specs=[SMEM] + [VMEM] * (count + 2),
        out_specs=[VMEM] * (1 + roles),
        compiler_params=params(),
        cost_estimate=SMALL,
        name="collect",
    )(where, *xs, down, mask)
    return x, lows


def project_kernel(roles, tile, x_ref, w_ref, *outs):
    rows = x_ref.shape[0] // roles
    columns = w_ref.shape[1]
    count = PARTS if roles == 4 else 1
    width = columns // count
    for c in range(count):

        @pl.loop(0, width // tile)
        def _(i):
            inner = pl.ds(pl.multiple_of(i * tile, tile), tile)
            at = pl.ds(pl.multiple_of(c * width + i * tile, tile), tile)
            y = dot(x_ref[...], w_ref[:, at]).astype(jnp.bfloat16)
            parts = [y[j * rows : (j + 1) * rows, :] for j in range(roles)]
            if roles == 4:
                own, three, pair, two = outs[0], outs[1], outs[2 + c], outs[2 + count + c]
                own[:, at] = parts[0]
                three[:, at] = parts[3]
                pair[0, :, inner] = parts[1]
                pair[1, :, inner] = parts[3]
                two[:, inner] = parts[2]
            else:
                for j in range(roles):
                    outs[0][j, :, at] = parts[j]


def project(x, w, roles):
    columns = w.shape[1]
    rows = x.shape[0] // roles
    if roles == 4:
        one = jax.ShapeDtypeStruct((rows, columns), jnp.bfloat16)
        outs = [one, one]
        outs = outs + [jax.ShapeDtypeStruct((2, rows, columns // PARTS), jnp.bfloat16)] * PARTS
        outs = outs + [jax.ShapeDtypeStruct((rows, columns // PARTS), jnp.bfloat16)] * PARTS
    else:
        outs = [jax.ShapeDtypeStruct((roles, rows, columns), jnp.bfloat16)]
    return pl.pallas_call(
        functools.partial(project_kernel, roles, min(256, columns)),
        out_shape=outs,
        in_specs=[VMEM, VMEM],
        out_specs=[VMEM] * len(outs),
        compiler_params=params(),
        cost_estimate=SMALL,
        name="project",
    )(x, w)


def add_kernel(lane_ref, own_ref, passed_ref, o_ref):
    middle = (lane_ref[0] == 1) | (lane_ref[0] == 2)

    @pl.when(middle)
    def _():
        o_ref[...] = (own_ref[...].astype(jnp.float32) + passed_ref[1].astype(jnp.float32)).astype(jnp.bfloat16)

    @pl.when(jnp.logical_not(middle))
    def _():
        o_ref[...] = own_ref[...]


def add(lane, own, passed):
    return pl.pallas_call(
        add_kernel,
        out_shape=jax.ShapeDtypeStruct(own.shape, own.dtype),
        in_specs=[SMEM, VMEM, VMEM],
        out_specs=VMEM,
        compiler_params=params(),
        cost_estimate=SMALL,
        name="add",
    )(lane, own, passed)


def adapt_kernel(low_ref, up_ref, o_ref):
    low = jnp.concatenate([low_ref[a] for a in range(low_ref.shape[0])], axis=1)
    o_ref[...] = dot(low, up_ref[...])


def adapt(low, up):
    return pl.pallas_call(
        adapt_kernel,
        out_shape=jax.ShapeDtypeStruct((low.shape[1], up.shape[1]), jnp.float32),
        in_specs=[VMEM, VMEM],
        out_specs=VMEM,
        compiler_params=params(),
        cost_estimate=SMALL,
        name="adapt",
    )(low, up)


def finish_kernel(whole, extra_ref, *refs):
    terms, parts, o_ref = refs[:whole], refs[whole:-1], refs[-1]
    total = extra_ref[...]
    for term in terms:
        if len(term.shape) == 2:
            total = total + term[...].astype(jnp.float32)
        else:
            for j in range(term.shape[0]):
                total = total + term[j].astype(jnp.float32)
    if not parts:
        o_ref[...] = total.astype(jnp.bfloat16)
    width = total.shape[1] // PARTS
    for c in range(PARTS if parts else 0):
        at = slice(c * width, (c + 1) * width)
        piece = total[:, at]
        for term in parts[c::PARTS]:
            piece = piece + (term[...] if len(term.shape) == 2 else term[0]).astype(jnp.float32)
        o_ref[:, at] = piece.astype(jnp.bfloat16)


def finish(terms, parts, extra):
    return pl.pallas_call(
        functools.partial(finish_kernel, len(terms)),
        out_shape=jax.ShapeDtypeStruct(extra.shape, jnp.bfloat16),
        in_specs=[VMEM] * (1 + len(terms) + len(parts)),
        out_specs=VMEM,
        compiler_params=params(),
        cost_estimate=SMALL,
        name="finish",
    )(extra, *terms, *parts)


def exchange(x, axis, distance):
    count = lax.axis_size(axis)
    return lax.ppermute(x, axis, [(i, i ^ distance) for i in range(count)])


def after(x, *others):
    return lax.optimization_barrier((x, *others))[0]


def gather(x):
    my_req = lax.axis_index("req").astype(jnp.int32)
    count = lax.axis_size("req")
    if count != 8:
        whole = lax.all_gather(x, "req", axis=0)
        return [whole[b] for b in range(count)], [jnp.int32(b) for b in range(count)]
    held = [x] + [exchange(x, "req", d) for d in (2, 4, 6)]
    near = [exchange(block, "req", 1) for block in held]
    return held + near, [my_req ^ d for d in (0, 2, 4, 6, 1, 3, 5, 7)]


def scatter(made, low):
    if len(made) == 1:
        moved = lax.all_to_all(made[0], "tp", split_axis=0, concat_axis=0, tiled=True)
        return [moved], [], lax.all_gather(low, "req", axis=0)
    own, three, pairs, twos = made[0], made[1], made[2 : 2 + PARTS], made[2 + PARTS :]
    lane = lax.axis_index("tp").astype(jnp.int32).reshape(1)
    middle = lax.ppermute(after(three, low), "tp", [(1, 2), (2, 1)])
    gathered = lax.all_gather(after(low, middle), "req", axis=0)
    moved, passed = [], []
    for c in range(PARTS):
        moved.append(exchange(after(pairs[c], *([middle] if c else [low])), "tp", 1))
        two = after(twos[c], *([passed[-1], gathered] if c else [middle]))
        passed.append(exchange(add(lane, two, moved[c]), "tp", 2))
    return [own, middle], moved + passed, gathered


def on_device(
    queries,
    incoming_key_value,
    key_value_pages,
    page_request_home,
    lengths,
    request_adapter_index,
    adapter_storage_slot,
    adapter_down_factor,
    adapter_up_factor,
    output_projection_weight,
):
    req_count = lax.axis_size("req")
    tp_count = lax.axis_size("tp")
    my_req = lax.axis_index("req").astype(jnp.int32)
    my_lane = lax.axis_index("tp").astype(jnp.int32)
    me = my_req.reshape(1)
    requests = lengths.shape[0]
    columns = key_value_pages.shape[-1]
    heads = columns // HEAD_WIDTH * GROUP
    own_slots, rank, model = adapter_up_factor.shape

    outbox = pack(me, page_request_home, request_adapter_index, key_value_pages, req_count)
    inbox = lax.all_to_all(outbox, "req", split_axis=0, concat_axis=0, tiled=True)

    table, order = build_table(me, page_request_home, lengths, LANES // (STEP_COUNT * heads))
    q = queries.reshape(requests * STEP_COUNT * heads, HEAD_WIDTH).T
    up_blocks = split_columns(adapter_up_factor.reshape(own_slots * rank, model), req_count)
    new = incoming_key_value.transpose(1, 0, 2).reshape(-1, columns)
    down = adapter_down_factor.transpose(0, 2, 1).reshape(own_slots * rank, -1)

    up = lax.all_to_all(up_blocks, "req", split_axis=0, concat_axis=0, tiled=True)
    up = up.reshape(req_count * own_slots * rank, -1)
    slot_count = adapter_storage_slot.shape[0]
    ids = inbox[:, BLOCK - 1, 0, :requests].astype(jnp.int32)
    match = ids[:, :, None] == jnp.arange(slot_count, dtype=jnp.int32)
    slot = jnp.sum(jnp.where(match, adapter_storage_slot, 0), axis=2)
    mine = my_req * own_slots + jnp.arange(own_slots * rank, dtype=jnp.int32) // rank

    roles = [my_lane ^ j for j in range(tp_count)]
    mixed = attend(order, lengths, table, q, new, key_value_pages, inbox)
    blocks, origins = gather(mixed)
    where = jnp.stack(origins + roles)
    token_slot = jnp.repeat(slot, STEP_COUNT, axis=1)
    mask = (token_slot.reshape(tp_count, -1)[:, :, None] == mine).astype(jnp.bfloat16)
    up = lax.all_to_all(after(up_blocks, table, q, new), "req", split_axis=0, concat_axis=0, tiled=True)
    up = up.reshape(req_count * own_slots * rank, -1)
    mask = after(mask, up)
    x, lows = collect(where, blocks, down, mask, tp_count)
    low = [lows[0]] + [exchange(lows[j], "tp", j) for j in range(1, tp_count)]
    low = functools.reduce(jnp.add, [term.astype(jnp.float32) for term in low]).astype(jnp.bfloat16)
    terms, parts, low = scatter(project(x, output_projection_weight, tp_count), low)
    return finish(terms, parts, adapt(low, up))


def solution(mesh):
    return jax.shard_map(
        on_device,
        mesh=mesh,
        in_specs=(
            P("req", "tp"),
            P(None, "req", "tp"),
            P("req", None, None, "tp"),
            P("req"),
            P("req"),
            P("req"),
            P(),
            P("req", "tp", None),
            P("req", None, None),
            P("tp", "req"),
        ),
        out_specs=P("tp", "req"),
        check_vma=False,
    )
```

```python
import functools
import math

import jax
import jax.numpy as jnp
from jax import lax
from jax.experimental import pallas as pl
from jax.experimental.pallas import tpu as pltpu
from jax.sharding import PartitionSpec as P

QUERY_HEADS = 64
KEY_VALUE_HEADS = 8
GROUP = QUERY_HEADS // KEY_VALUE_HEADS
HEAD_WIDTH = 128
STEP_COUNT = 4
PAGE_LENGTH = 32
MAXP = 16
CAP = 2
BLOCK = CAP * PAGE_LENGTH + 1
LABEL_LANE = 64
DIGIT = 16
CHUNK_PAGES = 4
CHUNKS = MAXP // CHUNK_PAGES
CHUNK_POSITIONS = CHUNK_PAGES * PAGE_LENGTH
LANES = 128
PARTS = 2
NEW_GROUP = 128 // (2 * STEP_COUNT)
SLOTS = 6
PACKS = 1
VMEM_LIMIT = 24 * 1024 * 1024
WHOLE_VMEM = 60 * 1024 * 1024
ATTEND_VMEM = 48 * 1024 * 1024

SMALL = pl.CostEstimate(flops=1, bytes_accessed=1, transcendentals=0)

ANY = pl.BlockSpec(memory_space=pl.ANY)
HBM = pl.BlockSpec(memory_space=pltpu.HBM)
VMEM = pl.BlockSpec(memory_space=pltpu.VMEM)
SMEM = pl.BlockSpec(memory_space=pltpu.SMEM)


def params(limit=VMEM_LIMIT):
    return pltpu.CompilerParams(vmem_limit_bytes=limit)


def dot(a, b, contract=((1,), (0,))):
    return lax.dot_general(a, b, (contract, ((), ())), preferred_element_type=jnp.float32)


def pack_kernel(req_count, per_dev, me_ref, home_ref, ids_ref, pages, outbox, info_v, info_s, ids_v, rows_v, sem, sems):
    me = me_ref[0]
    page = lax.broadcasted_iota(jnp.int32, (req_count, per_dev), 1)
    want = lax.broadcasted_iota(jnp.int32, (req_count, per_dev), 0)
    slots = jnp.broadcast_to(home_ref[...], (req_count, per_dev)) - want * per_dev
    hit = (slots >= 0) & (slots < per_dev) & (want != me)
    lane = lax.broadcasted_iota(jnp.int32, (req_count, 128), 1)
    info = jnp.full((req_count, 128), -1, jnp.int32)
    for k in range(CAP):
        first = jnp.min(jnp.where(hit, page, per_dev), axis=1, keepdims=True)
        here = hit & (page == first)
        slot = jnp.max(jnp.where(here, slots, -1), axis=1, keepdims=True)
        info = jnp.where(lane == k, first, info)
        info = jnp.where(lane == CAP + k, slot, info)
        hit = hit & (page != first)
    info_v[...] = info
    fetch = pltpu.make_async_copy(info_v, info_s, sem)
    fetch.start()
    ids_v[...] = jnp.zeros_like(ids_v)
    ids_v[:, 0:ids_ref.shape[1]] = ids_ref[...].astype(jnp.float32)
    ids = jnp.broadcast_to(ids_v[...], (2, 128))
    fetch.wait()

    def copy(d, k):
        return pltpu.make_async_copy(
            pages.at[info_s[d, k]],
            outbox.at[d, pl.ds(k * PAGE_LENGTH, PAGE_LENGTH)],
            sems.at[d, k],
        )

    for d in range(req_count):
        for k in range(CAP):

            @pl.when(info_s[d, k] < per_dev)
            def _():
                copy(d, k).start()

    at = lax.broadcasted_iota(jnp.int32, (2, 128), 1)
    row = lax.broadcasted_iota(jnp.int32, (2, 128), 0)
    for d in range(req_count):
        value = jnp.where(row == 0, ids, 0.0)
        for k in range(CAP):
            slot = info_s[d, CAP + k]
            high = ((slot + DIGIT) >> 4) - 1
            low = slot - high * DIGIT
            digit = jnp.where(row == 0, high, low).astype(jnp.float32)
            value = jnp.where(at == LABEL_LANE + k, digit, value)
        rows_v[d, 0, :, :] = jnp.zeros(rows_v.shape[2:], jnp.bfloat16)
        rows_v[d, 0, :, 0:128] = value.astype(jnp.bfloat16)
    rows = pltpu.make_async_copy(rows_v, outbox.at[:, pl.ds(BLOCK - 1, 1)], sem)
    rows.start()
    rows.wait()
    for d in range(req_count):
        for k in range(CAP):

            @pl.when(info_s[d, k] < per_dev)
            def _():
                copy(d, k).wait()


def pack(me, page_request_home, ids, key_value_pages, req_count):
    per_dev = key_value_pages.shape[0]
    columns = key_value_pages.shape[-1]
    return pl.pallas_call(
        functools.partial(pack_kernel, req_count, per_dev),
        out_shape=jax.ShapeDtypeStruct((req_count, BLOCK, 2, columns), jnp.bfloat16),
        in_specs=[SMEM, VMEM, VMEM, HBM],
        out_specs=VMEM,
        scratch_shapes=[
            pltpu.VMEM((req_count, 128), jnp.int32),
            pltpu.SMEM((req_count, 128), jnp.int32),
            pltpu.VMEM((1, 128), jnp.float32),
            pltpu.VMEM((req_count, 1, 2, columns), jnp.bfloat16),
            pltpu.SemaphoreType.DMA,
            pltpu.SemaphoreType.DMA((req_count, CAP)),
        ],
        compiler_params=params(WHOLE_VMEM),
        cost_estimate=SMALL,
        name="pack_outbox",
    )(me, page_request_home.reshape(1, per_dev), ids.reshape(1, -1), key_value_pages)


def table_kernel(per_dev, requests, pack_size, me_ref, home_ref, lengths_ref, table_ref, order_ref, len_v):
    base = me_ref[0] * per_dev
    lane = lax.broadcasted_iota(jnp.int32, (128, 128), 1)
    row = lax.broadcasted_iota(jnp.int32, (128, 128), 0)
    tiles = per_dev // 128
    columns = [
        jnp.transpose(jnp.broadcast_to(home_ref[i : i + 1, :] - base, (128, 128)).astype(jnp.float32))
        for i in range(tiles)
    ]
    for j in range(tiles):
        total = jnp.zeros((128, 128), jnp.float32)
        slot = (lane + j * 128).astype(jnp.float32)
        for i in range(tiles):
            total = total + jnp.where(columns[i] == slot, (row + i * 128).astype(jnp.float32), 0.0)
        table_ref[j : j + 1, :] = jnp.sum(total, axis=0, keepdims=True).astype(jnp.int32)
    half = NEW_GROUP
    len_v[...] = jnp.zeros_like(len_v)
    len_v[:, 0:requests] = lengths_ref[...].astype(jnp.float32)
    along = jnp.broadcast_to(len_v[...], (128, 128))
    along = ((along.astype(jnp.int32) + (CHUNK_POSITIONS - 1)) >> 7).astype(jnp.float32)
    down = jnp.transpose(along)
    same = ((lane // half) == (row // half)) & (lane % pack_size == row % pack_size)
    before = same & ((along > down) | ((along == down) & (lane < row)))
    rank = jnp.sum(jnp.where(before, 1.0, 0.0), axis=1, keepdims=True)
    place = rank * pack_size + ((row // half) * half + row % pack_size).astype(jnp.float32)
    at = place == lane.astype(jnp.float32)
    order = jnp.sum(jnp.where(at, row.astype(jnp.float32), 0.0), axis=0, keepdims=True)
    chunks = jnp.sum(jnp.where(at, down, 0.0), axis=0, keepdims=True)
    order_ref[0:1, :] = order.astype(jnp.int32)
    order_ref[1:2, :] = chunks.astype(jnp.int32)


def build_table(me, page_request_home, lengths, pack_size):
    per_dev = page_request_home.shape[0]
    requests = lengths.shape[0]
    return pl.pallas_call(
        functools.partial(table_kernel, per_dev, requests, pack_size),
        out_shape=(
            jax.ShapeDtypeStruct((per_dev // 128, 128), jnp.int32),
            jax.ShapeDtypeStruct((2, 128), jnp.int32),
        ),
        in_specs=[SMEM, VMEM, VMEM],
        out_specs=(VMEM, VMEM),
        scratch_shapes=[pltpu.VMEM((1, 128), jnp.float32)],
        compiler_params=params(),
        cost_estimate=SMALL,
        name="page_table",
    )(me, page_request_home.reshape(per_dev // 128, 128), lengths.reshape(1, requests))


def attend_kernel(
    req_count,
    per_dev,
    requests,
    order_ref,
    lengths_ref,
    table_in,
    q_ref,
    new_ref,
    pages,
    inbox,
    out_ref,
    table,
    labels_v,
    labels_w,
    labels_s,
    buf,
    acc,
    sem,
    sems,
):
    columns = pages.shape[-1]
    heads_kv = columns // HEAD_WIDTH
    heads = heads_kv * GROUP
    span = STEP_COUNT * heads
    pack_size = LANES // span
    page_size = PAGE_LENGTH * 2
    chunk_size = CHUNK_PAGES * page_size
    new_rows = STEP_COUNT * 2
    tokens = requests * STEP_COUNT
    scale = math.log2(math.e) / math.sqrt(HEAD_WIDTH)
    page_rows = pages.reshape(per_dev, page_size, columns)
    inbox_rows = inbox.reshape(req_count, BLOCK * 2, columns)

    first = pltpu.make_async_copy(inbox.at[:, pl.ds(BLOCK - 1, 1)], labels_v, sem)
    first.start()
    first.wait()
    row = lax.broadcasted_iota(jnp.int32, (2, 128), 0)
    weight = jnp.where(row == 0, float(DIGIT), 1.0)
    for d in range(req_count):
        digits = labels_v[d, 0, :, 0:128].astype(jnp.float32) * weight
        labels_w[d : d + 1, :] = jnp.sum(digits, axis=0, keepdims=True).astype(jnp.int32)
    back = pltpu.make_async_copy(labels_w, labels_s, sem)
    back.start()

    @pl.loop(0, per_dev // 128)
    def _(i):
        @pl.loop(0, 128, unroll=8)
        def _(j):
            table[i, j] = table_in[i, j]

    back.wait()
    for d in range(req_count):
        for k in range(CAP):
            slot = labels_s[d, LABEL_LANE + k]

            @pl.when(slot >= 0)
            def _():
                table[lax.shift_right_logical(slot, 7), slot & 127] = per_dev + d * CAP + k

    batch = PACKS * pack_size
    steps = requests // batch

    def most_chunks(step):
        counts = [order_ref[1, step * batch + u] for u in range(batch)]
        return functools.reduce(jnp.maximum, counts)

    def fetch(step):
        place = lax.rem(step, SLOTS)
        count = most_chunks(step)
        for u in range(batch):
            slot = order_ref[0, step * batch + u] * MAXP
            line = lax.shift_right_logical(slot, 7)
            at = slot & 127

            @pl.loop(0, count)
            def _(c):
                sources = [table[line, at + c * CHUNK_PAGES + j] for j in range(CHUNK_PAGES)]
                most = functools.reduce(jnp.maximum, sources)

                def target(j):
                    start = pl.multiple_of(c * chunk_size + j * page_size, page_size)
                    return buf.at[place, u, pl.ds(start, page_size)]

                @pl.when(most < per_dev)
                def _():
                    for j in range(CHUNK_PAGES):
                        pltpu.make_async_copy(page_rows.at[sources[j]], target(j), sems.at[place, u]).start()

                @pl.when(most >= per_dev)
                def _():
                    for j in range(CHUNK_PAGES):
                        source = sources[j]

                        @pl.when(source < per_dev)
                        def _():
                            pltpu.make_async_copy(page_rows.at[source], target(j), sems.at[place, u]).start()

                        @pl.when(source >= per_dev)
                        def _():
                            e = source - per_dev
                            d = lax.shift_right_logical(e, 1)
                            start = pl.multiple_of((e - d * CAP) * page_size, page_size)
                            pltpu.make_async_copy(
                                inbox_rows.at[d, pl.ds(start, page_size)], target(j), sems.at[place, u]
                            ).start()

    for s in range(min(SLOTS - 1, steps)):
        fetch(jnp.int32(s))

    def compute(step, n):
        place = lax.rem(step, SLOTS)
        width = n * chunk_size
        for u in range(batch):
            whole = buf.at[place, u, pl.ds(0, width)]
            pltpu.make_async_copy(whole, whole, sems.at[place, u]).wait()
        for v in range(PACKS):
            attend_pack(step, place, width, v)

    def attend_pack(step, place, width, v):
        lane = lax.broadcasted_iota(jnp.int32, (HEAD_WIDTH, LANES), 1)
        part = lane // span
        lane_head = (lane % heads) // GROUP
        one = lax.broadcasted_iota(jnp.int32, (1, LANES), 1)
        limit = jnp.zeros((1, LANES), jnp.int32)
        owner = jnp.zeros((1, LANES), jnp.int32)
        rows, kvs, rights = [], [], []
        for u in range(pack_size):
            r = order_ref[0, step * batch + v * pack_size + u]
            rows.append(r)
            q = q_ref[:, pl.ds(pl.multiple_of((r // pack_size) * LANES, LANES), LANES)].astype(jnp.float32)
            own = part == u
            rights.append(
                jnp.concatenate(
                    [jnp.where(own & (lane_head == g), q, 0.0).astype(jnp.bfloat16) for g in range(heads_kv)], axis=0
                )
            )
            kvs.append(buf[place, v * pack_size + u, 0:width, :])
            limit = jnp.where(one // span == u, 2 * lengths_ref[r], limit)
            owner = jnp.where(one // span == u, r & (NEW_GROUP - 1), owner)
        group = rows[0] // NEW_GROUP
        new = new_ref[pl.ds(pl.multiple_of(group * 128, 128), 128), :]
        s = dot(jnp.concatenate(kvs, axis=1), jnp.concatenate(rights, axis=0))
        sn = dot(new, functools.reduce(jnp.add, rights))
        row = lax.broadcasted_iota(jnp.int32, (width, LANES), 0)
        s = jnp.where(((row & 1) == 0) & (row < limit), s * scale, -jnp.inf)
        row = lax.broadcasted_iota(jnp.int32, sn.shape, 0)
        step_of = (one % span) // heads
        seen = ((row & 1) == 0) & (row // new_rows == owner) & ((row % new_rows) // 2 <= step_of)
        sn = jnp.where(seen, sn * scale, -jnp.inf)
        top = jnp.maximum(jnp.max(s, axis=0, keepdims=True), jnp.max(sn, axis=0, keepdims=True))
        w = jnp.exp2(s - top)
        wn = jnp.exp2(sn - top)
        inverse = 1.0 / (jnp.sum(w, axis=0, keepdims=True) + jnp.sum(wn, axis=0, keepdims=True))
        p = jnp.transpose(pltpu.roll(w * inverse, 1, 0)).astype(jnp.bfloat16)
        pn = jnp.transpose(pltpu.roll(wn * inverse, 1, 0)).astype(jnp.bfloat16)
        head = (lax.broadcasted_iota(jnp.int32, (span, HEAD_WIDTH), 0) % heads) // GROUP
        for u in range(pack_size):
            at = slice(u * span, (u + 1) * span)
            full = dot(p[at], kvs[u]) + dot(pn[at], new)
            o = full[:, :HEAD_WIDTH]
            for g in range(1, heads_kv):
                o = jnp.where(head == g, full[:, g * HEAD_WIDTH : (g + 1) * HEAD_WIDTH], o)
            token = rows[u] * STEP_COUNT
            for t in range(STEP_COUNT):
                acc[pl.ds(token + t, heads, stride=tokens), :] = o[t * heads : (t + 1) * heads]

    @pl.loop(0, steps)
    def _(step):
        @pl.when(step + (SLOTS - 1) < steps)
        def _():
            fetch(step + (SLOTS - 1))

        count = most_chunks(step)
        for n in range(1, CHUNKS + 1):

            @pl.when(count == n)
            def _():
                compute(step, n)

    for h in range(heads):
        out_ref[:, h * HEAD_WIDTH : (h + 1) * HEAD_WIDTH] = acc[h * tokens : (h + 1) * tokens].astype(jnp.bfloat16)


def attend(order, lengths, table, q, new, pages, inbox):
    per_dev, _, _, columns = pages.shape
    req_count = inbox.shape[0]
    requests = lengths.shape[0]
    heads = columns // HEAD_WIDTH * GROUP
    tokens = requests * STEP_COUNT
    pack_size = LANES // (STEP_COUNT * heads)
    extent = MAXP * PAGE_LENGTH * 2
    return pl.pallas_call(
        functools.partial(attend_kernel, req_count, per_dev, requests),
        out_shape=jax.ShapeDtypeStruct((tokens, heads * HEAD_WIDTH), jnp.bfloat16),
        in_specs=[SMEM, SMEM, SMEM, VMEM, VMEM, HBM, ANY],
        out_specs=VMEM,
        scratch_shapes=[
            pltpu.SMEM(table.shape, jnp.int32),
            pltpu.VMEM((req_count, 1, 2, columns), jnp.bfloat16),
            pltpu.VMEM((req_count, 128), jnp.int32),
            pltpu.SMEM((req_count, 128), jnp.int32),
            pltpu.VMEM((SLOTS, PACKS * pack_size, extent, columns), jnp.bfloat16),
            pltpu.VMEM((heads * tokens, HEAD_WIDTH), jnp.float32),
            pltpu.SemaphoreType.DMA,
            pltpu.SemaphoreType.DMA((SLOTS, PACKS * pack_size)),
        ],
        compiler_params=params(ATTEND_VMEM),
        cost_estimate=pl.CostEstimate(
            flops=16 * tokens * heads * HEAD_WIDTH * MAXP * PAGE_LENGTH,
            bytes_accessed=requests * extent * columns * 2,
            transcendentals=2 * tokens * heads * MAXP * PAGE_LENGTH,
        ),
        name="attend",
    )(order, lengths, table, q, new, pages, inbox)


def split_kernel(x_ref, o_ref, sems):
    parts, _, block = o_ref.shape
    copies = [
        pltpu.make_async_copy(x_ref.at[:, pl.ds(i * block, block)], o_ref.at[i], sems.at[i]) for i in range(parts)
    ]
    for copy in copies:
        copy.start()
    for copy in copies:
        copy.wait()


def split_columns(x, parts):
    rows, columns = x.shape
    return pl.pallas_call(
        split_kernel,
        out_shape=jax.ShapeDtypeStruct((parts, rows, columns // parts), x.dtype),
        in_specs=[HBM],
        out_specs=VMEM,
        scratch_shapes=[pltpu.SemaphoreType.DMA((parts,))],
        compiler_params=params(),
        cost_estimate=SMALL,
        name="split_columns",
    )(x)


def collect_kernel(count, roles, where_ref, *refs):
    xs, (down_ref, mask_ref), (x_ref, *lows) = refs[:count], refs[count : count + 2], refs[count + 2 :]
    tokens = xs[0].shape[0]
    rows = count * tokens // roles
    per_role = count // roles
    for b in range(count):
        at = where_ref[b]
        if roles == 4:
            at = (at // per_role ^ where_ref[count]) * per_role + at % per_role
        x_ref[pl.ds(pl.multiple_of(at * tokens, tokens), tokens), :] = xs[b][...]
    for j in range(roles):
        s = where_ref[count + j]
        at = j if roles == 4 else s
        x = x_ref[pl.ds(pl.multiple_of(at * rows, rows), rows), :]
        lows[j][...] = (dot(x, down_ref[...], ((1,), (1,))) * mask_ref[s].astype(jnp.float32)).astype(jnp.bfloat16)


def collect(where, xs, down, mask, roles):
    count = len(xs)
    tokens, width = xs[0].shape
    rows = count * tokens // roles
    x, *lows = pl.pallas_call(
        functools.partial(collect_kernel, count, roles),
        out_shape=[jax.ShapeDtypeStruct((count * tokens, width), jnp.bfloat16)]
        + [jax.ShapeDtypeStruct((rows, down.shape[0]), jnp.bfloat16)] * roles,
        in_specs=[SMEM] + [VMEM] * (count + 2),
        out_specs=[VMEM] * (1 + roles),
        compiler_params=params(),
        cost_estimate=SMALL,
        name="collect",
    )(where, *xs, down, mask)
    return x, lows


def project_kernel(roles, tile, x_ref, w_ref, *outs):
    rows = x_ref.shape[0] // roles
    columns = w_ref.shape[1]
    count = PARTS if roles == 4 else 1
    width = columns // count
    for c in range(count):

        @pl.loop(0, width // tile)
        def _(i):
            inner = pl.ds(pl.multiple_of(i * tile, tile), tile)
            at = pl.ds(pl.multiple_of(c * width + i * tile, tile), tile)
            y = dot(x_ref[...], w_ref[:, at]).astype(jnp.bfloat16)
            parts = [y[j * rows : (j + 1) * rows, :] for j in range(roles)]
            if roles == 4:
                own, three, pair, two = outs[0], outs[1], outs[2 + c], outs[2 + count + c]
                own[:, at] = parts[0]
                three[:, at] = parts[3]
                pair[0, :, inner] = parts[1]
                pair[1, :, inner] = parts[3]
                two[:, inner] = parts[2]
            else:
                for j in range(roles):
                    outs[0][j, :, at] = parts[j]


def project(x, w, roles):
    columns = w.shape[1]
    rows = x.shape[0] // roles
    if roles == 4:
        one = jax.ShapeDtypeStruct((rows, columns), jnp.bfloat16)
        outs = [one, one]
        outs = outs + [jax.ShapeDtypeStruct((2, rows, columns // PARTS), jnp.bfloat16)] * PARTS
        outs = outs + [jax.ShapeDtypeStruct((rows, columns // PARTS), jnp.bfloat16)] * PARTS
    else:
        outs = [jax.ShapeDtypeStruct((roles, rows, columns), jnp.bfloat16)]
    return pl.pallas_call(
        functools.partial(project_kernel, roles, min(256, columns)),
        out_shape=outs,
        in_specs=[VMEM, VMEM],
        out_specs=[VMEM] * len(outs),
        compiler_params=params(),
        cost_estimate=SMALL,
        name="project",
    )(x, w)


def add_kernel(lane_ref, own_ref, passed_ref, o_ref):
    middle = (lane_ref[0] == 1) | (lane_ref[0] == 2)

    @pl.when(middle)
    def _():
        o_ref[...] = (own_ref[...].astype(jnp.float32) + passed_ref[1].astype(jnp.float32)).astype(jnp.bfloat16)

    @pl.when(jnp.logical_not(middle))
    def _():
        o_ref[...] = own_ref[...]


def add(lane, own, passed):
    return pl.pallas_call(
        add_kernel,
        out_shape=jax.ShapeDtypeStruct(own.shape, own.dtype),
        in_specs=[SMEM, VMEM, VMEM],
        out_specs=VMEM,
        compiler_params=params(),
        cost_estimate=SMALL,
        name="add",
    )(lane, own, passed)


def adapt_kernel(low_ref, up_ref, o_ref):
    low = jnp.concatenate([low_ref[a] for a in range(low_ref.shape[0])], axis=1)
    o_ref[...] = dot(low, up_ref[...])


def adapt(low, up):
    return pl.pallas_call(
        adapt_kernel,
        out_shape=jax.ShapeDtypeStruct((low.shape[1], up.shape[1]), jnp.float32),
        in_specs=[VMEM, VMEM],
        out_specs=VMEM,
        compiler_params=params(),
        cost_estimate=SMALL,
        name="adapt",
    )(low, up)


def finish_kernel(whole, extra_ref, *refs):
    terms, parts, o_ref = refs[:whole], refs[whole:-1], refs[-1]
    total = extra_ref[...]
    for term in terms:
        if len(term.shape) == 2:
            total = total + term[...].astype(jnp.float32)
        else:
            for j in range(term.shape[0]):
                total = total + term[j].astype(jnp.float32)
    if not parts:
        o_ref[...] = total.astype(jnp.bfloat16)
    width = total.shape[1] // PARTS
    for c in range(PARTS if parts else 0):
        at = slice(c * width, (c + 1) * width)
        piece = total[:, at]
        for term in parts[c::PARTS]:
            piece = piece + (term[...] if len(term.shape) == 2 else term[0]).astype(jnp.float32)
        o_ref[:, at] = piece.astype(jnp.bfloat16)


def finish(terms, parts, extra):
    return pl.pallas_call(
        functools.partial(finish_kernel, len(terms)),
        out_shape=jax.ShapeDtypeStruct(extra.shape, jnp.bfloat16),
        in_specs=[VMEM] * (1 + len(terms) + len(parts)),
        out_specs=VMEM,
        compiler_params=params(),
        cost_estimate=SMALL,
        name="finish",
    )(extra, *terms, *parts)


def exchange(x, axis, distance):
    count = lax.axis_size(axis)
    return lax.ppermute(x, axis, [(i, i ^ distance) for i in range(count)])


def after(x, *others):
    return lax.optimization_barrier((x, *others))[0]


def gather(x):
    my_req = lax.axis_index("req").astype(jnp.int32)
    count = lax.axis_size("req")
    if count != 8:
        whole = lax.all_gather(x, "req", axis=0)
        return [whole[b] for b in range(count)], [jnp.int32(b) for b in range(count)]
    held = [x] + [exchange(x, "req", d) for d in (2, 4, 6)]
    near = [exchange(block, "req", 1) for block in held]
    return held + near, [my_req ^ d for d in (0, 2, 4, 6, 1, 3, 5, 7)]


def scatter(made, low):
    if len(made) == 1:
        moved = lax.all_to_all(made[0], "tp", split_axis=0, concat_axis=0, tiled=True)
        return [moved], [], lax.all_gather(low, "req", axis=0), low
    own, three, pairs, twos = made[0], made[1], made[2 : 2 + PARTS], made[2 + PARTS :]
    lane = lax.axis_index("tp").astype(jnp.int32).reshape(1)
    middle = lax.ppermute(after(three, low), "tp", [(1, 2), (2, 1)])
    moved, passed = [], []
    for c in range(PARTS):
        moved.append(exchange(after(pairs[c], *([middle] if c else [low])), "tp", 1))
        passed.append(exchange(add(lane, after(twos[c], middle), moved[c]), "tp", 2))
    gathered = lax.all_gather(after(low, *moved), "req", axis=0)
    return [own, middle], moved + passed, gathered, middle


def on_device(
    queries,
    incoming_key_value,
    key_value_pages,
    page_request_home,
    lengths,
    request_adapter_index,
    adapter_storage_slot,
    adapter_down_factor,
    adapter_up_factor,
    output_projection_weight,
):
    req_count = lax.axis_size("req")
    tp_count = lax.axis_size("tp")
    my_req = lax.axis_index("req").astype(jnp.int32)
    my_lane = lax.axis_index("tp").astype(jnp.int32)
    me = my_req.reshape(1)
    requests = lengths.shape[0]
    columns = key_value_pages.shape[-1]
    heads = columns // HEAD_WIDTH * GROUP
    own_slots, rank, model = adapter_up_factor.shape

    outbox = pack(me, page_request_home, request_adapter_index, key_value_pages, req_count)
    inbox = lax.all_to_all(outbox, "req", split_axis=0, concat_axis=0, tiled=True)

    table, order = build_table(me, page_request_home, lengths, LANES // (STEP_COUNT * heads))
    q = queries.reshape(requests * STEP_COUNT * heads, HEAD_WIDTH).T
    up_blocks = split_columns(adapter_up_factor.reshape(own_slots * rank, model), req_count)
    new = incoming_key_value.transpose(1, 0, 2).reshape(-1, columns)
    down = adapter_down_factor.transpose(0, 2, 1).reshape(own_slots * rank, -1)

    up = lax.all_to_all(up_blocks, "req", split_axis=0, concat_axis=0, tiled=True)
    up = up.reshape(req_count * own_slots * rank, -1)
    slot_count = adapter_storage_slot.shape[0]
    ids = inbox[:, BLOCK - 1, 0, :requests].astype(jnp.int32)
    match = ids[:, :, None] == jnp.arange(slot_count, dtype=jnp.int32)
    slot = jnp.sum(jnp.where(match, adapter_storage_slot, 0), axis=2)
    mine = my_req * own_slots + jnp.arange(own_slots * rank, dtype=jnp.int32) // rank

    roles = [my_lane ^ j for j in range(tp_count)]
    mixed = attend(order, lengths, table, q, new, key_value_pages, inbox)
    blocks, origins = gather(mixed)
    where = jnp.stack(origins + roles)
    token_slot = jnp.repeat(slot, STEP_COUNT, axis=1)
    mask = (token_slot.reshape(tp_count, -1)[:, :, None] == mine).astype(jnp.bfloat16)
    x, lows = collect(where, blocks, down, mask, tp_count)
    low = [lows[0]] + [exchange(lows[j], "tp", j) for j in range(1, tp_count)]
    low = functools.reduce(jnp.add, [term.astype(jnp.float32) for term in low]).astype(jnp.bfloat16)
    terms, parts, low, middle = scatter(project(x, output_projection_weight, tp_count), low)
    up = lax.all_to_all(after(up_blocks, middle), "req", split_axis=0, concat_axis=0, tiled=True)
    up = up.reshape(req_count * own_slots * rank, -1)
    return finish(terms, parts, adapt(low, up))


def solution(mesh):
    return jax.shard_map(
        on_device,
        mesh=mesh,
        in_specs=(
            P("req", "tp"),
            P(None, "req", "tp"),
            P("req", None, None, "tp"),
            P("req"),
            P("req"),
            P("req"),
            P(),
            P("req", "tp", None),
            P("req", None, None),
            P("tp", "req"),
        ),
        out_specs=P("tp", "req"),
        check_vma=False,
    )
```

```python
import functools
import math

import jax
import jax.numpy as jnp
from jax import lax
from jax.experimental import pallas as pl
from jax.experimental.pallas import tpu as pltpu
from jax.sharding import PartitionSpec as P

QUERY_HEADS = 64
KEY_VALUE_HEADS = 8
GROUP = QUERY_HEADS // KEY_VALUE_HEADS
HEAD_WIDTH = 128
STEP_COUNT = 4
PAGE_LENGTH = 32
MAXP = 16
CAP = 2
BLOCK = CAP * PAGE_LENGTH + 1
LABEL_LANE = 64
DIGIT = 16
CHUNK_PAGES = 4
CHUNKS = MAXP // CHUNK_PAGES
CHUNK_POSITIONS = CHUNK_PAGES * PAGE_LENGTH
LANES = 128
PARTS = 2
NEW_GROUP = 128 // (2 * STEP_COUNT)
SLOTS = 6
PACKS = 1
VMEM_LIMIT = 24 * 1024 * 1024
WHOLE_VMEM = 60 * 1024 * 1024
ATTEND_VMEM = 48 * 1024 * 1024

SMALL = pl.CostEstimate(flops=1, bytes_accessed=1, transcendentals=0)

ANY = pl.BlockSpec(memory_space=pl.ANY)
HBM = pl.BlockSpec(memory_space=pltpu.HBM)
VMEM = pl.BlockSpec(memory_space=pltpu.VMEM)
SMEM = pl.BlockSpec(memory_space=pltpu.SMEM)


def params(limit=VMEM_LIMIT):
    return pltpu.CompilerParams(vmem_limit_bytes=limit)


def dot(a, b, contract=((1,), (0,))):
    return lax.dot_general(a, b, (contract, ((), ())), preferred_element_type=jnp.float32)


def pack_kernel(req_count, per_dev, me_ref, home_ref, ids_ref, pages, outbox, info_v, info_s, ids_v, rows_v, sem, sems):
    me = me_ref[0]
    page = lax.broadcasted_iota(jnp.int32, (req_count, per_dev), 1)
    want = lax.broadcasted_iota(jnp.int32, (req_count, per_dev), 0)
    slots = jnp.broadcast_to(home_ref[...], (req_count, per_dev)) - want * per_dev
    hit = (slots >= 0) & (slots < per_dev) & (want != me)
    lane = lax.broadcasted_iota(jnp.int32, (req_count, 128), 1)
    info = jnp.full((req_count, 128), -1, jnp.int32)
    for k in range(CAP):
        first = jnp.min(jnp.where(hit, page, per_dev), axis=1, keepdims=True)
        here = hit & (page == first)
        slot = jnp.max(jnp.where(here, slots, -1), axis=1, keepdims=True)
        info = jnp.where(lane == k, first, info)
        info = jnp.where(lane == CAP + k, slot, info)
        hit = hit & (page != first)
    info_v[...] = info
    fetch = pltpu.make_async_copy(info_v, info_s, sem)
    fetch.start()
    ids_v[...] = jnp.zeros_like(ids_v)
    ids_v[:, 0:ids_ref.shape[1]] = ids_ref[...].astype(jnp.float32)
    ids = jnp.broadcast_to(ids_v[...], (2, 128))
    fetch.wait()

    def copy(d, k):
        return pltpu.make_async_copy(
            pages.at[info_s[d, k]],
            outbox.at[d, pl.ds(k * PAGE_LENGTH, PAGE_LENGTH)],
            sems.at[d, k],
        )

    for d in range(req_count):
        for k in range(CAP):

            @pl.when(info_s[d, k] < per_dev)
            def _():
                copy(d, k).start()

    at = lax.broadcasted_iota(jnp.int32, (2, 128), 1)
    row = lax.broadcasted_iota(jnp.int32, (2, 128), 0)
    for d in range(req_count):
        value = jnp.where(row == 0, ids, 0.0)
        for k in range(CAP):
            slot = info_s[d, CAP + k]
            high = ((slot + DIGIT) >> 4) - 1
            low = slot - high * DIGIT
            digit = jnp.where(row == 0, high, low).astype(jnp.float32)
            value = jnp.where(at == LABEL_LANE + k, digit, value)
        rows_v[d, 0, :, :] = jnp.zeros(rows_v.shape[2:], jnp.bfloat16)
        rows_v[d, 0, :, 0:128] = value.astype(jnp.bfloat16)
    rows = pltpu.make_async_copy(rows_v, outbox.at[:, pl.ds(BLOCK - 1, 1)], sem)
    rows.start()
    rows.wait()
    for d in range(req_count):
        for k in range(CAP):

            @pl.when(info_s[d, k] < per_dev)
            def _():
                copy(d, k).wait()


def pack(me, page_request_home, ids, key_value_pages, req_count):
    per_dev = key_value_pages.shape[0]
    columns = key_value_pages.shape[-1]
    return pl.pallas_call(
        functools.partial(pack_kernel, req_count, per_dev),
        out_shape=jax.ShapeDtypeStruct((req_count, BLOCK, 2, columns), jnp.bfloat16),
        in_specs=[SMEM, VMEM, VMEM, HBM],
        out_specs=VMEM,
        scratch_shapes=[
            pltpu.VMEM((req_count, 128), jnp.int32),
            pltpu.SMEM((req_count, 128), jnp.int32),
            pltpu.VMEM((1, 128), jnp.float32),
            pltpu.VMEM((req_count, 1, 2, columns), jnp.bfloat16),
            pltpu.SemaphoreType.DMA,
            pltpu.SemaphoreType.DMA((req_count, CAP)),
        ],
        compiler_params=params(WHOLE_VMEM),
        cost_estimate=SMALL,
        name="pack_outbox",
    )(me, page_request_home.reshape(1, per_dev), ids.reshape(1, -1), key_value_pages)


def table_kernel(per_dev, requests, pack_size, me_ref, home_ref, lengths_ref, table_ref, order_ref, len_v):
    base = me_ref[0] * per_dev
    lane = lax.broadcasted_iota(jnp.int32, (128, 128), 1)
    row = lax.broadcasted_iota(jnp.int32, (128, 128), 0)
    tiles = per_dev // 128
    columns = [
        jnp.transpose(jnp.broadcast_to(home_ref[i : i + 1, :] - base, (128, 128)).astype(jnp.float32))
        for i in range(tiles)
    ]
    for j in range(tiles):
        total = jnp.zeros((128, 128), jnp.float32)
        slot = (lane + j * 128).astype(jnp.float32)
        for i in range(tiles):
            total = total + jnp.where(columns[i] == slot, (row + i * 128).astype(jnp.float32), 0.0)
        table_ref[j : j + 1, :] = jnp.sum(total, axis=0, keepdims=True).astype(jnp.int32)
    half = NEW_GROUP
    len_v[...] = jnp.zeros_like(len_v)
    len_v[:, 0:requests] = lengths_ref[...].astype(jnp.float32)
    along = jnp.broadcast_to(len_v[...], (128, 128))
    along = ((along.astype(jnp.int32) + (CHUNK_POSITIONS - 1)) >> 7).astype(jnp.float32)
    down = jnp.transpose(along)
    same = ((lane // half) == (row // half)) & (lane % pack_size == row % pack_size)
    before = same & ((along > down) | ((along == down) & (lane < row)))
    rank = jnp.sum(jnp.where(before, 1.0, 0.0), axis=1, keepdims=True)
    place = rank * pack_size + ((row // half) * half + row % pack_size).astype(jnp.float32)
    at = place == lane.astype(jnp.float32)
    order = jnp.sum(jnp.where(at, row.astype(jnp.float32), 0.0), axis=0, keepdims=True)
    chunks = jnp.sum(jnp.where(at, down, 0.0), axis=0, keepdims=True)
    order_ref[0:1, :] = order.astype(jnp.int32)
    order_ref[1:2, :] = chunks.astype(jnp.int32)


def build_table(me, page_request_home, lengths, pack_size):
    per_dev = page_request_home.shape[0]
    requests = lengths.shape[0]
    return pl.pallas_call(
        functools.partial(table_kernel, per_dev, requests, pack_size),
        out_shape=(
            jax.ShapeDtypeStruct((per_dev // 128, 128), jnp.int32),
            jax.ShapeDtypeStruct((2, 128), jnp.int32),
        ),
        in_specs=[SMEM, VMEM, VMEM],
        out_specs=(VMEM, VMEM),
        scratch_shapes=[pltpu.VMEM((1, 128), jnp.float32)],
        compiler_params=params(),
        cost_estimate=SMALL,
        name="page_table",
    )(me, page_request_home.reshape(per_dev // 128, 128), lengths.reshape(1, requests))


def attend_kernel(
    req_count,
    per_dev,
    requests,
    order_ref,
    lengths_ref,
    table_in,
    q_ref,
    new_ref,
    pages,
    inbox,
    out_ref,
    table,
    labels_v,
    labels_w,
    labels_s,
    buf,
    acc,
    sem,
    sems,
):
    columns = pages.shape[-1]
    heads_kv = columns // HEAD_WIDTH
    heads = heads_kv * GROUP
    span = STEP_COUNT * heads
    pack_size = LANES // span
    page_size = PAGE_LENGTH * 2
    chunk_size = CHUNK_PAGES * page_size
    new_rows = STEP_COUNT * 2
    tokens = requests * STEP_COUNT
    scale = math.log2(math.e) / math.sqrt(HEAD_WIDTH)
    page_rows = pages.reshape(per_dev, page_size, columns)
    inbox_rows = inbox.reshape(req_count, BLOCK * 2, columns)

    first = pltpu.make_async_copy(inbox.at[:, pl.ds(BLOCK - 1, 1)], labels_v, sem)
    first.start()
    first.wait()
    row = lax.broadcasted_iota(jnp.int32, (2, 128), 0)
    weight = jnp.where(row == 0, float(DIGIT), 1.0)
    for d in range(req_count):
        digits = labels_v[d, 0, :, 0:128].astype(jnp.float32) * weight
        labels_w[d : d + 1, :] = jnp.sum(digits, axis=0, keepdims=True).astype(jnp.int32)
    back = pltpu.make_async_copy(labels_w, labels_s, sem)
    back.start()

    @pl.loop(0, per_dev // 128)
    def _(i):
        @pl.loop(0, 128, unroll=8)
        def _(j):
            table[i, j] = table_in[i, j]

    back.wait()
    for d in range(req_count):
        for k in range(CAP):
            slot = labels_s[d, LABEL_LANE + k]

            @pl.when(slot >= 0)
            def _():
                table[lax.shift_right_logical(slot, 7), slot & 127] = per_dev + d * CAP + k

    batch = PACKS * pack_size
    steps = requests // batch

    def most_chunks(step):
        counts = [order_ref[1, step * batch + u] for u in range(batch)]
        return functools.reduce(jnp.maximum, counts)

    def fetch(step):
        place = lax.rem(step, SLOTS)
        count = most_chunks(step)
        for u in range(batch):
            slot = order_ref[0, step * batch + u] * MAXP
            line = lax.shift_right_logical(slot, 7)
            at = slot & 127

            @pl.loop(0, count)
            def _(c):
                sources = [table[line, at + c * CHUNK_PAGES + j] for j in range(CHUNK_PAGES)]
                most = functools.reduce(jnp.maximum, sources)

                def target(j):
                    start = pl.multiple_of(c * chunk_size + j * page_size, page_size)
                    return buf.at[place, u, pl.ds(start, page_size)]

                @pl.when(most < per_dev)
                def _():
                    for j in range(CHUNK_PAGES):
                        pltpu.make_async_copy(page_rows.at[sources[j]], target(j), sems.at[place, u]).start()

                @pl.when(most >= per_dev)
                def _():
                    for j in range(CHUNK_PAGES):
                        source = sources[j]

                        @pl.when(source < per_dev)
                        def _():
                            pltpu.make_async_copy(page_rows.at[source], target(j), sems.at[place, u]).start()

                        @pl.when(source >= per_dev)
                        def _():
                            e = source - per_dev
                            d = lax.shift_right_logical(e, 1)
                            start = pl.multiple_of((e - d * CAP) * page_size, page_size)
                            pltpu.make_async_copy(
                                inbox_rows.at[d, pl.ds(start, page_size)], target(j), sems.at[place, u]
                            ).start()

    for s in range(min(SLOTS - 1, steps)):
        fetch(jnp.int32(s))

    def compute(step, n):
        place = lax.rem(step, SLOTS)
        width = n * chunk_size
        for u in range(batch):
            whole = buf.at[place, u, pl.ds(0, width)]
            pltpu.make_async_copy(whole, whole, sems.at[place, u]).wait()
        for v in range(PACKS):
            attend_pack(step, place, width, v)

    def attend_pack(step, place, width, v):
        lane = lax.broadcasted_iota(jnp.int32, (HEAD_WIDTH, LANES), 1)
        part = lane // span
        lane_head = (lane % heads) // GROUP
        one = lax.broadcasted_iota(jnp.int32, (1, LANES), 1)
        limit = jnp.zeros((1, LANES), jnp.int32)
        owner = jnp.zeros((1, LANES), jnp.int32)
        rows, kvs, rights = [], [], []
        for u in range(pack_size):
            r = order_ref[0, step * batch + v * pack_size + u]
            rows.append(r)
            q = q_ref[:, pl.ds(pl.multiple_of((r // pack_size) * LANES, LANES), LANES)].astype(jnp.float32)
            own = part == u
            rights.append(
                jnp.concatenate(
                    [jnp.where(own & (lane_head == g), q, 0.0).astype(jnp.bfloat16) for g in range(heads_kv)], axis=0
                )
            )
            kvs.append(buf[place, v * pack_size + u, 0:width, :])
            limit = jnp.where(one // span == u, 2 * lengths_ref[r], limit)
            owner = jnp.where(one // span == u, r & (NEW_GROUP - 1), owner)
        group = rows[0] // NEW_GROUP
        new = new_ref[pl.ds(pl.multiple_of(group * 128, 128), 128), :]
        s = dot(jnp.concatenate(kvs, axis=1), jnp.concatenate(rights, axis=0))
        sn = dot(new, functools.reduce(jnp.add, rights))
        row = lax.broadcasted_iota(jnp.int32, (width, LANES), 0)
        s = jnp.where(((row & 1) == 0) & (row < limit), s * scale, -jnp.inf)
        row = lax.broadcasted_iota(jnp.int32, sn.shape, 0)
        step_of = (one % span) // heads
        seen = ((row & 1) == 0) & (row // new_rows == owner) & ((row % new_rows) // 2 <= step_of)
        sn = jnp.where(seen, sn * scale, -jnp.inf)
        top = jnp.maximum(jnp.max(s, axis=0, keepdims=True), jnp.max(sn, axis=0, keepdims=True))
        w = jnp.exp2(s - top)
        wn = jnp.exp2(sn - top)
        inverse = 1.0 / (jnp.sum(w, axis=0, keepdims=True) + jnp.sum(wn, axis=0, keepdims=True))
        p = jnp.transpose(pltpu.roll(w * inverse, 1, 0)).astype(jnp.bfloat16)
        pn = jnp.transpose(pltpu.roll(wn * inverse, 1, 0)).astype(jnp.bfloat16)
        head = (lax.broadcasted_iota(jnp.int32, (span, HEAD_WIDTH), 0) % heads) // GROUP
        for u in range(pack_size):
            at = slice(u * span, (u + 1) * span)
            full = dot(p[at], kvs[u]) + dot(pn[at], new)
            o = full[:, :HEAD_WIDTH]
            for g in range(1, heads_kv):
                o = jnp.where(head == g, full[:, g * HEAD_WIDTH : (g + 1) * HEAD_WIDTH], o)
            token = rows[u] * STEP_COUNT
            for t in range(STEP_COUNT):
                acc[pl.ds(token + t, heads, stride=tokens), :] = o[t * heads : (t + 1) * heads]

    @pl.loop(0, steps)
    def _(step):
        @pl.when(step + (SLOTS - 1) < steps)
        def _():
            fetch(step + (SLOTS - 1))

        count = most_chunks(step)
        for n in range(1, CHUNKS + 1):

            @pl.when(count == n)
            def _():
                compute(step, n)

    for h in range(heads):
        out_ref[:, h * HEAD_WIDTH : (h + 1) * HEAD_WIDTH] = acc[h * tokens : (h + 1) * tokens].astype(jnp.bfloat16)


def attend(order, lengths, table, q, new, pages, inbox):
    per_dev, _, _, columns = pages.shape
    req_count = inbox.shape[0]
    requests = lengths.shape[0]
    heads = columns // HEAD_WIDTH * GROUP
    tokens = requests * STEP_COUNT
    pack_size = LANES // (STEP_COUNT * heads)
    extent = MAXP * PAGE_LENGTH * 2
    return pl.pallas_call(
        functools.partial(attend_kernel, req_count, per_dev, requests),
        out_shape=jax.ShapeDtypeStruct((tokens, heads * HEAD_WIDTH), jnp.bfloat16),
        in_specs=[SMEM, SMEM, SMEM, VMEM, VMEM, HBM, ANY],
        out_specs=VMEM,
        scratch_shapes=[
            pltpu.SMEM(table.shape, jnp.int32),
            pltpu.VMEM((req_count, 1, 2, columns), jnp.bfloat16),
            pltpu.VMEM((req_count, 128), jnp.int32),
            pltpu.SMEM((req_count, 128), jnp.int32),
            pltpu.VMEM((SLOTS, PACKS * pack_size, extent, columns), jnp.bfloat16),
            pltpu.VMEM((heads * tokens, HEAD_WIDTH), jnp.float32),
            pltpu.SemaphoreType.DMA,
            pltpu.SemaphoreType.DMA((SLOTS, PACKS * pack_size)),
        ],
        compiler_params=params(ATTEND_VMEM),
        cost_estimate=pl.CostEstimate(
            flops=16 * tokens * heads * HEAD_WIDTH * MAXP * PAGE_LENGTH,
            bytes_accessed=requests * extent * columns * 2,
            transcendentals=2 * tokens * heads * MAXP * PAGE_LENGTH,
        ),
        name="attend",
    )(order, lengths, table, q, new, pages, inbox)


def split_kernel(x_ref, o_ref, sems):
    parts, _, block = o_ref.shape
    copies = [
        pltpu.make_async_copy(x_ref.at[:, pl.ds(i * block, block)], o_ref.at[i], sems.at[i]) for i in range(parts)
    ]
    for copy in copies:
        copy.start()
    for copy in copies:
        copy.wait()


def split_columns(x, parts):
    rows, columns = x.shape
    return pl.pallas_call(
        split_kernel,
        out_shape=jax.ShapeDtypeStruct((parts, rows, columns // parts), x.dtype),
        in_specs=[HBM],
        out_specs=VMEM,
        scratch_shapes=[pltpu.SemaphoreType.DMA((parts,))],
        compiler_params=params(),
        cost_estimate=SMALL,
        name="split_columns",
    )(x)


def collect_kernel(count, roles, where_ref, *refs):
    xs, (down_ref, mask_ref), (x_ref, *lows) = refs[:count], refs[count : count + 2], refs[count + 2 :]
    tokens = xs[0].shape[0]
    rows = count * tokens // roles
    per_role = count // roles
    for b in range(count):
        at = where_ref[b]
        if roles == 4:
            at = (at // per_role ^ where_ref[count]) * per_role + at % per_role
        x_ref[pl.ds(pl.multiple_of(at * tokens, tokens), tokens), :] = xs[b][...]
    for j in range(roles):
        s = where_ref[count + j]
        at = j if roles == 4 else s
        x = x_ref[pl.ds(pl.multiple_of(at * rows, rows), rows), :]
        lows[j][...] = (dot(x, down_ref[...], ((1,), (1,))) * mask_ref[s].astype(jnp.float32)).astype(jnp.bfloat16)


def collect(where, xs, down, mask, roles):
    count = len(xs)
    tokens, width = xs[0].shape
    rows = count * tokens // roles
    x, *lows = pl.pallas_call(
        functools.partial(collect_kernel, count, roles),
        out_shape=[jax.ShapeDtypeStruct((count * tokens, width), jnp.bfloat16)]
        + [jax.ShapeDtypeStruct((rows, down.shape[0]), jnp.bfloat16)] * roles,
        in_specs=[SMEM] + [VMEM] * (count + 2),
        out_specs=[VMEM] * (1 + roles),
        compiler_params=params(),
        cost_estimate=SMALL,
        name="collect",
    )(where, *xs, down, mask)
    return x, lows


def project_kernel(roles, tile, x_ref, w_ref, *outs):
    rows = x_ref.shape[0] // roles
    columns = w_ref.shape[1]
    count = PARTS if roles == 4 else 1
    width = columns // count
    for c in range(count):

        @pl.loop(0, width // tile)
        def _(i):
            inner = pl.ds(pl.multiple_of(i * tile, tile), tile)
            at = pl.ds(pl.multiple_of(c * width + i * tile, tile), tile)
            y = dot(x_ref[...], w_ref[:, at]).astype(jnp.bfloat16)
            parts = [y[j * rows : (j + 1) * rows, :] for j in range(roles)]
            if roles == 4:
                own, three, pair, two = outs[0], outs[1], outs[2 + c], outs[2 + count + c]
                own[:, at] = parts[0]
                three[:, at] = parts[3]
                pair[0, :, inner] = parts[1]
                pair[1, :, inner] = parts[3]
                two[:, inner] = parts[2]
            else:
                for j in range(roles):
                    outs[0][j, :, at] = parts[j]


def project(x, w, roles):
    columns = w.shape[1]
    rows = x.shape[0] // roles
    if roles == 4:
        one = jax.ShapeDtypeStruct((rows, columns), jnp.bfloat16)
        outs = [one, one]
        outs = outs + [jax.ShapeDtypeStruct((2, rows, columns // PARTS), jnp.bfloat16)] * PARTS
        outs = outs + [jax.ShapeDtypeStruct((rows, columns // PARTS), jnp.bfloat16)] * PARTS
    else:
        outs = [jax.ShapeDtypeStruct((roles, rows, columns), jnp.bfloat16)]
    return pl.pallas_call(
        functools.partial(project_kernel, roles, min(256, columns)),
        out_shape=outs,
        in_specs=[VMEM, VMEM],
        out_specs=[VMEM] * len(outs),
        compiler_params=params(),
        cost_estimate=SMALL,
        name="project",
    )(x, w)


def add_kernel(lane_ref, own_ref, passed_ref, o_ref):
    middle = (lane_ref[0] == 1) | (lane_ref[0] == 2)

    @pl.when(middle)
    def _():
        o_ref[...] = (own_ref[...].astype(jnp.float32) + passed_ref[1].astype(jnp.float32)).astype(jnp.bfloat16)

    @pl.when(jnp.logical_not(middle))
    def _():
        o_ref[...] = own_ref[...]


def add(lane, own, passed):
    return pl.pallas_call(
        add_kernel,
        out_shape=jax.ShapeDtypeStruct(own.shape, own.dtype),
        in_specs=[SMEM, VMEM, VMEM],
        out_specs=VMEM,
        compiler_params=params(),
        cost_estimate=SMALL,
        name="add",
    )(lane, own, passed)


def adapt_kernel(low_ref, up_ref, o_ref):
    low = jnp.concatenate([low_ref[a] for a in range(low_ref.shape[0])], axis=1)
    o_ref[...] = dot(low, up_ref[...])


def adapt(low, up):
    return pl.pallas_call(
        adapt_kernel,
        out_shape=jax.ShapeDtypeStruct((low.shape[1], up.shape[1]), jnp.float32),
        in_specs=[VMEM, VMEM],
        out_specs=VMEM,
        compiler_params=params(),
        cost_estimate=SMALL,
        name="adapt",
    )(low, up)


def finish_kernel(whole, extra_ref, *refs):
    terms, parts, o_ref = refs[:whole], refs[whole:-1], refs[-1]
    total = extra_ref[...]
    for term in terms:
        if len(term.shape) == 2:
            total = total + term[...].astype(jnp.float32)
        else:
            for j in range(term.shape[0]):
                total = total + term[j].astype(jnp.float32)
    if not parts:
        o_ref[...] = total.astype(jnp.bfloat16)
    width = total.shape[1] // PARTS
    for c in range(PARTS if parts else 0):
        at = slice(c * width, (c + 1) * width)
        piece = total[:, at]
        for term in parts[c::PARTS]:
            piece = piece + (term[...] if len(term.shape) == 2 else term[0]).astype(jnp.float32)
        o_ref[:, at] = piece.astype(jnp.bfloat16)


def finish(terms, parts, extra):
    return pl.pallas_call(
        functools.partial(finish_kernel, len(terms)),
        out_shape=jax.ShapeDtypeStruct(extra.shape, jnp.bfloat16),
        in_specs=[VMEM] * (1 + len(terms) + len(parts)),
        out_specs=VMEM,
        compiler_params=params(),
        cost_estimate=SMALL,
        name="finish",
    )(extra, *terms, *parts)


def exchange(x, axis, distance):
    count = lax.axis_size(axis)
    return lax.ppermute(x, axis, [(i, i ^ distance) for i in range(count)])


def after(x, *others):
    return lax.optimization_barrier((x, *others))[0]


def gather(x):
    my_req = lax.axis_index("req").astype(jnp.int32)
    count = lax.axis_size("req")
    if count != 8:
        whole = lax.all_gather(x, "req", axis=0)
        return [whole[b] for b in range(count)], [jnp.int32(b) for b in range(count)]
    held = [x] + [exchange(x, "req", d) for d in (2, 4, 6)]
    near = [exchange(block, "req", 1) for block in held]
    return held + near, [my_req ^ d for d in (0, 2, 4, 6, 1, 3, 5, 7)]


def scatter(made, low):
    if len(made) == 1:
        moved = lax.all_to_all(made[0], "tp", split_axis=0, concat_axis=0, tiled=True)
        return [moved], [], lax.all_gather(low, "req", axis=0)
    own, three, pairs, twos = made[0], made[1], made[2 : 2 + PARTS], made[2 + PARTS :]
    lane = lax.axis_index("tp").astype(jnp.int32).reshape(1)
    middle = lax.ppermute(after(three, low), "tp", [(1, 2), (2, 1)])
    moved, passed = [], []
    for c in range(PARTS):
        moved.append(exchange(after(pairs[c], *([middle] if c else [low])), "tp", 1))
        passed.append(exchange(add(lane, after(twos[c], middle), moved[c]), "tp", 2))
    gathered = lax.all_gather(after(low, *moved), "req", axis=0)
    return [own, middle], moved + passed, gathered


def on_device(
    queries,
    incoming_key_value,
    key_value_pages,
    page_request_home,
    lengths,
    request_adapter_index,
    adapter_storage_slot,
    adapter_down_factor,
    adapter_up_factor,
    output_projection_weight,
):
    req_count = lax.axis_size("req")
    tp_count = lax.axis_size("tp")
    my_req = lax.axis_index("req").astype(jnp.int32)
    my_lane = lax.axis_index("tp").astype(jnp.int32)
    me = my_req.reshape(1)
    requests = lengths.shape[0]
    columns = key_value_pages.shape[-1]
    heads = columns // HEAD_WIDTH * GROUP
    own_slots, rank, model = adapter_up_factor.shape

    outbox = pack(me, page_request_home, request_adapter_index, key_value_pages, req_count)
    inbox = lax.all_to_all(outbox, "req", split_axis=0, concat_axis=0, tiled=True)

    table, order = build_table(me, page_request_home, lengths, LANES // (STEP_COUNT * heads))
    q = queries.reshape(requests * STEP_COUNT * heads, HEAD_WIDTH).T
    up_blocks = split_columns(adapter_up_factor.reshape(own_slots * rank, model), req_count)
    new = incoming_key_value.transpose(1, 0, 2).reshape(-1, columns)
    down = adapter_down_factor.transpose(0, 2, 1).reshape(own_slots * rank, -1)

    up = lax.all_to_all(up_blocks, "req", split_axis=0, concat_axis=0, tiled=True)
    up = up.reshape(req_count * own_slots * rank, -1)
    slot_count = adapter_storage_slot.shape[0]
    ids = inbox[:, BLOCK - 1, 0, :requests].astype(jnp.int32)
    match = ids[:, :, None] == jnp.arange(slot_count, dtype=jnp.int32)
    slot = jnp.sum(jnp.where(match, adapter_storage_slot, 0), axis=2)
    mine = my_req * own_slots + jnp.arange(own_slots * rank, dtype=jnp.int32) // rank

    roles = [my_lane ^ j for j in range(tp_count)]
    mixed = attend(order, lengths, table, q, new, key_value_pages, inbox)
    blocks, origins = gather(mixed)
    where = jnp.stack(origins + roles)
    token_slot = jnp.repeat(slot, STEP_COUNT, axis=1)
    mask = (token_slot.reshape(tp_count, -1)[:, :, None] == mine).astype(jnp.bfloat16)
    up = lax.all_to_all(after(up_blocks, table, q, new), "req", split_axis=0, concat_axis=0, tiled=True)
    up = up.reshape(req_count * own_slots * rank, -1)
    mask = after(mask, up)
    x, lows = collect(where, blocks, down, mask, tp_count)
    low = [lows[0]] + [exchange(lows[j], "tp", j) for j in range(1, tp_count)]
    low = functools.reduce(jnp.add, [term.astype(jnp.float32) for term in low]).astype(jnp.bfloat16)
    terms, parts, low = scatter(project(x, output_projection_weight, tp_count), low)
    return finish(terms, parts, adapt(low, up))


def solution(mesh):
    return jax.shard_map(
        on_device,
        mesh=mesh,
        in_specs=(
            P("req", "tp"),
            P(None, "req", "tp"),
            P("req", None, None, "tp"),
            P("req"),
            P("req"),
            P("req"),
            P(),
            P("req", "tp", None),
            P("req", None, None),
            P("tp", "req"),
        ),
        out_specs=P("tp", "req"),
        check_vma=False,
    )
```
